32 devices in a mesh: seq: 16 (over z, y, x), head: 2 (over core).
Axes of the slice: x: 2, y: 2, z: 4, core: 2. Of those that a mesh axis runs over, the one named last changes fastest.
Arguments:
- query_rows: bfloat16 [16384, 2048], P('seq', 'head'), may hold values from -6 to 6
- key_rows: bfloat16 [16384, 2048], P('seq', 'head'), may hold values from -6 to 6
- value_rows: bfloat16 [16384, 2048], P('seq', 'head'), may hold values from -6 to 6
- head_scale: float32 [16], P('head'), may hold values from 0.25 to 4
- out_gain: float32 [2048], P('head'), may hold values from 0.5 to 1.5
Outputs:
- attended: bfloat16 [16384, 2048], P('seq', 'head')
The draws below stay inside these ranges and needn't reach their ends.
All inputs are finite; a program needn't handle non-finite values.
Results may differ from the reference program's by a relative error of at most 0.001.
Values sent between devices are 32-bit elements; how exact they have to be, the bound alone decides.
No kernel may reach another device: no remote copies, remote signals or barrier semaphores. Data moves between devices by JAX's collectives and lax.ppermute only.
A program may use at most 320 MiB of HBM per device.

```python
import math
import jax
import jax.numpy as jnp
from jax import lax

H = 16
DH = 128
BLK = 128
TOKENS = 16384


def steps_of(own_key, dims, split, low, largest):
    factor_of, own = 1.0, jax.random.fold_in(own_key, 6)
    for dim, blocks in split:
        heights = jnp.exp(jax.random.uniform(jax.random.fold_in(own, dim), (blocks,), jnp.float32, low / len(split), largest / len(split)))
        factor_of = factor_of * jnp.repeat(heights, dims[dim] // blocks).reshape([-1 if axis == dim else 1 for axis in range(len(dims))])
    return factor_of


def noise(rng, extent, scale, limit, pieces=(), held_as=jnp.bfloat16):
    array = jax.random.normal(rng, extent, jnp.float32) * scale
    if len(pieces) > 0:
        array = steps_of(rng, extent, pieces, -0.22, 0.18) * array
    return jnp.clip(array, min=-limit, max=limit).astype(held_as)


def setup_inputs(seed: int = 0) -> dict:
    key_list = jax.random.split(jax.random.key(seed), 6)
    query_rows = noise(key_list[0], (TOKENS, H * DH), 1.0, 6.0, ((0, 16), (1, 2)))
    key_rows = noise(key_list[1], (TOKENS, H * DH), 1.0, 6.0, ((0, 16), (1, 2)))
    value_rows = noise(key_list[2], (TOKENS, H * DH), 1.0, 6.0, ((0, 16), (1, 2)))
    head_scale = jnp.clip(jnp.exp(math.log(4.0) - 2.7725887 * jax.random.uniform(key_list[3], (H,), jnp.float32) ** steps_of(key_list[3], (H,), ((0, 2),), -0.2, 0.2)), 0.25, 4.0)
    out_gain = jnp.clip(1.0 + 0.1 * jax.random.normal(key_list[4], (H * DH,), jnp.float32), 0.5, 1.5)
    return dict(query_rows=query_rows, key_rows=key_rows, value_rows=value_rows, head_scale=head_scale, out_gain=out_gain)


epsilon = 1e-06
highest = lax.Precision.HIGHEST

def block_step(carry, blocks):
    sums_k, sums_qv, cross = carry
    query_blk, key_blk, value_blk = blocks
    positions = jnp.arange(BLK)
    lower_mask = (positions[:, None] >= positions[None, :]).astype(jnp.float32)
    upper_mask = (positions[:, None] <= positions[None, :]).astype(jnp.float32)
    strict_lower = (positions[:, None] > positions[None, :]).astype(jnp.float32)
    scores = jnp.einsum('htd,had->hta', query_blk, key_blk, precision=highest)
    back_scores = jnp.einsum('had,hbd->hab', key_blk, query_blk, precision=highest)
    weights = jnp.einsum('hta,hab->htb', scores * lower_mask, back_scores * upper_mask, precision=highest) * lower_mask
    inside = jnp.einsum('htb,hbd->htd', weights, value_blk, precision=highest)
    query_state = jnp.einsum('htd,hde->hte', query_blk, sums_k, precision=highest)
    carried = jnp.einsum('hte,hbe->htb', query_state, query_blk, precision=highest) * lower_mask
    prior = jnp.einsum('hde,hef->hdf', sums_k, sums_qv, precision=highest) - cross
    numer = inside + jnp.einsum('htb,hbd->htd', carried, value_blk, precision=highest)
    numer = numer + jnp.einsum('htd,hde->hte', query_blk, prior, precision=highest)
    blk_k = jnp.einsum('had,hae->hde', key_blk, key_blk, precision=highest)
    blk_qv = jnp.einsum('had,hae->hde', query_blk, value_blk, precision=highest)
    earlier = jnp.einsum('hab,hbd->had', back_scores * strict_lower, value_blk, precision=highest)
    blk_cross = jnp.einsum('had,hae->hde', key_blk, earlier, precision=highest)
    new_cross = cross + blk_cross + jnp.einsum('hde,hef->hdf', blk_k, sums_qv, precision=highest)
    return ((sums_k + blk_k, sums_qv + blk_qv, new_cross), numer)

def reference(query_rows, key_rows, value_rows, head_scale, out_gain):
    count = TOKENS // BLK

    def arrange(rows):
        return rows.astype(jnp.float32).reshape(count, BLK, H, DH).transpose(0, 2, 1, 3)
    zeros = jnp.zeros((H, DH, DH), jnp.float32)
    final, numer = lax.scan(block_step, (zeros, zeros, zeros), (arrange(query_rows), arrange(key_rows), arrange(value_rows)))
    numer = numer.transpose(0, 2, 1, 3).reshape(TOKENS, H, DH)
    scaled = numer * head_scale[None, :, None]
    mean_sq = lax.optimization_barrier(jnp.mean(scaled * scaled, axis=(1, 2)))
    normed = scaled * lax.rsqrt(mean_sq + epsilon)[:, None, None]
    return (normed.reshape(TOKENS, H * DH) * out_gain[None, :]).astype(jnp.bfloat16)
```

```python
import functools

import jax
import jax.numpy as jnp
from jax import lax
from jax.experimental import pallas as pl
from jax.experimental.pallas import tpu as pltpu
from jax.sharding import PartitionSpec as P

BLK = 128
VMEM_LIMIT = 48 * 1024 * 1024

epsilon = 1e-06
f32, bf16 = jnp.float32, jnp.bfloat16

NN = (((1,), (0,)), ((), ()))
NT = (((1,), (1,)), ((), ()))
TN = (((0,), (0,)), ((), ()))


def dot(a, b, dims=NN):
    return lax.dot_general(a, b, dims, preferred_element_type=f32)


def split(a):
    high = a.astype(bf16)
    return high, (a - high.astype(f32)).astype(bf16)


def lanes(*parts):
    return jnp.concatenate(parts, axis=1)


def rows(*parts):
    return jnp.concatenate(parts, axis=0)


def dot_f32(a, b):
    a_high, a_low = split(a)
    b_high, b_low = split(b)
    return dot(lanes(a_high, a_low), rows(b_high, b_high)) + dot(a_high, b_low)


def lower():
    shape = (BLK, BLK)
    return lax.broadcasted_iota(jnp.int32, shape, 0) >= lax.broadcasted_iota(jnp.int32, shape, 1)


def moments_kernel(q_ref, k_ref, v_ref, out_ref):
    k = k_ref[...]
    out_ref[0, :BLK] = dot(k, k, TN)
    out_ref[0, BLK:] = dot(q_ref[...], v_ref[...], TN)


def first_stage_kernel(q_ref, k_ref, v_ref, r_ref, d_ref):
    blocks = q_ref.shape[0] // BLK
    mask = lower()
    state = jnp.zeros((BLK, BLK), f32)
    total = jnp.zeros((BLK, BLK), f32)
    for i in range(blocks):
        at = pl.ds(i * BLK, BLK)
        q, k, v = q_ref[at], k_ref[at], v_ref[at]
        a_high, a_low = split(jnp.where(mask, dot(q, k, NT), 0.0))
        r = dot(lanes(a_high, a_low), rows(k, k))
        if i > 0:
            s_high, s_low = split(state)
            r = r + dot(lanes(q, q), rows(s_high, s_low))
        state = state + dot(k, k, TN)
        r_ref[at] = r
        r_high, r_low = split(r)
        total = total + dot(rows(r_high, r_low), rows(v, v), TN)
    d_ref[0] = total


def second_stage_kernel(q_ref, v_ref, r_ref, s_ref, num_ref):
    blocks = q_ref.shape[0] // BLK
    mask = lower()
    s_high, s_low = split(s_ref[0])
    s_both = rows(s_high, s_low)
    state = jnp.zeros((BLK, BLK), f32)
    for i in range(blocks):
        at = pl.ds(i * BLK, BLK)
        q, v = q_ref[at], v_ref[at]
        qq, vv = lanes(q, q), rows(v, v)
        r_high, r_low = split(r_ref[at] + dot(qq, s_both))
        a_high, a_low = split(jnp.where(mask, dot(qq, lanes(r_high, r_low), NT), 0.0))
        num = dot(lanes(a_high, a_low), vv)
        if i > 0:
            d_high, d_low = split(state)
            num = num + dot(qq, rows(d_high, d_low))
        num_ref[at] = num
        if i + 1 < blocks:
            state = state + dot(rows(r_high, r_low), vv, TN)


def owner_local_kernel(moments_ref, s_ref, c_ref, f_ref):
    members = moments_ref.shape[0]
    s = jnp.zeros((BLK, BLK), f32)
    c = jnp.zeros((BLK, BLK), f32)
    f = jnp.zeros((BLK, BLK), f32)
    for m in range(members):
        s_ref[m], c_ref[m], f_ref[m] = s, c, f
        c_own = moments_ref[m, BLK:]
        if m > 0:
            f = f + dot_f32(s, c_own)
        s = s + moments_ref[m, :BLK]
        c = c + c_own
    s_ref[members], c_ref[members], f_ref[members] = s, c, f


def owner_shift_kernel(s_ref, c_ref, f_ref, before_ref, back_ref, out_ref):
    members = back_ref.shape[0]
    before = before_ref[...]
    for m in range(members):
        back_ref[m] = s_ref[m] + before
    out_ref[0] = f_ref[0]
    for m in range(1, members + 1):
        out_ref[m] = f_ref[m] + dot_f32(before, c_ref[m])


def owner_sum_kernel(d_ref, h_ref, base_ref, total_ref):
    members = d_ref.shape[0]
    d = jnp.zeros((BLK, BLK), f32)
    for m in range(members):
        base_ref[m] = h_ref[m] + d
        d = d + d_ref[m]
    total_ref[...] = h_ref[members] + d


def add_kernel(base_ref, before_ref, out_ref):
    for m in range(out_ref.shape[0]):
        out_ref[m] = base_ref[m] + before_ref[...]


def scale_kernel(q_ref, num_ref, d_ref, scale_ref, y_ref, part_ref):
    heads = d_ref.shape[0]
    part = jnp.zeros(part_ref.shape, f32)
    for h in range(heads):
        at = slice(h * BLK, (h + 1) * BLK)
        q = q_ref[:, at]
        d_high, d_low = split(d_ref[h])
        y = (num_ref[:, at] + dot(lanes(q, q), rows(d_high, d_low))) * scale_ref[:, at]
        y_ref[:, at] = y
        part = part + y * y
    part_ref[...] = part


def norm_kernel(features, y_ref, mine_ref, other_ref, gain_ref, out_ref):
    total = jnp.sum(mine_ref[...] + other_ref[...], axis=1, keepdims=True)
    inv = lax.rsqrt(total * (1.0 / features) + epsilon)
    out_ref[...] = (y_ref[...] * inv * gain_ref[...]).astype(bf16)


def params(*semantics):
    return pltpu.CompilerParams(dimension_semantics=semantics, vmem_limit_bytes=VMEM_LIMIT)


def cost(us, moved):
    return pl.CostEstimate(flops=int(us * 4e8), bytes_accessed=int(moved), transcendentals=0)


def per_device(query_rows, key_rows, value_rows, head_scale, out_gain):
    tokens, width = query_rows.shape
    heads = head_scale.shape[0]
    seq = lax.axis_size("seq")
    members = heads
    groups = seq // members
    index_groups = [[g * members + m for m in range(members)] for g in range(groups)]
    onward = [(i, i + members) for i in range(seq - members)]

    def swap(a):
        return lax.all_to_all(a, "seq", 0, 0, axis_index_groups=index_groups)

    head_col = pl.BlockSpec((tokens, BLK), lambda h: (0, h))
    head_mat = pl.BlockSpec((1, BLK, BLK), lambda h: (h, 0, 0))
    mats = lambda n: jax.ShapeDtypeStruct((n, BLK, BLK), f32)
    mat = jax.ShapeDtypeStruct((BLK, BLK), f32)

    moments = pl.pallas_call(
        moments_kernel,
        grid=(heads,),
        in_specs=[head_col] * 3,
        out_specs=pl.BlockSpec((1, 2 * BLK, BLK), lambda h: (h, 0, 0)),
        out_shape=jax.ShapeDtypeStruct((heads, 2 * BLK, BLK), f32),
        compiler_params=params("arbitrary"),
        name="moments",
    )(query_rows, key_rows, value_rows)
    moments_in = swap(moments)

    r_local, d_local = pl.pallas_call(
        first_stage_kernel,
        grid=(heads,),
        in_specs=[head_col] * 3,
        out_specs=[head_col, head_mat],
        out_shape=[jax.ShapeDtypeStruct((tokens, width), f32), mats(heads)],
        compiler_params=params("arbitrary"),
        cost_estimate=cost(10, 10 * tokens * width),
        name="first_stage",
    )(query_rows, key_rows, value_rows)
    d_in = swap(d_local)

    s_part, c_part, f_part = pl.pallas_call(
        owner_local_kernel,
        out_shape=[mats(members + 1)] * 3,
        compiler_params=params(),
        name="owner_local",
    )(moments_in)
    s_before = jnp.zeros((BLK, BLK), f32)
    for _ in range(groups - 1):
        s_before = lax.ppermute(s_before + s_part[members], "seq", onward)
    s_back, h_part = pl.pallas_call(
        owner_shift_kernel,
        out_shape=[mats(members), mats(members + 1)],
        compiler_params=params(),
        name="owner_shift",
    )(s_part, c_part, f_part, s_before)
    s_pre = swap(s_back)

    d_base, d_total = pl.pallas_call(
        owner_sum_kernel,
        out_shape=[mats(members), mat],
        compiler_params=params(),
        name="owner_sum",
    )(d_in, h_part)
    d_before = jnp.zeros((BLK, BLK), f32)
    for _ in range(groups - 1):
        d_before = lax.ppermute(d_before + d_total, "seq", onward)
    d_back = pl.pallas_call(
        add_kernel, out_shape=mats(members), compiler_params=params(), name="owner_add"
    )(d_base, d_before)
    d_pre = swap(d_back)

    num = pl.pallas_call(
        second_stage_kernel,
        grid=(heads,),
        in_specs=[head_col, head_col, head_col, head_mat],
        out_specs=head_col,
        out_shape=jax.ShapeDtypeStruct((tokens, width), f32),
        compiler_params=params("arbitrary"),
        cost_estimate=cost(10, 12 * tokens * width),
        name="second_stage",
    )(query_rows, value_rows, r_local, s_pre)

    step = 256
    row_blk = pl.BlockSpec((step, width), lambda i: (i, 0))
    row_part = pl.BlockSpec((step, BLK), lambda i: (i, 0))
    one_row = pl.BlockSpec((1, width), lambda i: (0, 0))
    scale_row = jnp.repeat(head_scale, BLK)[None, :]
    y, part = pl.pallas_call(
        scale_kernel,
        grid=(tokens // step,),
        in_specs=[row_blk, row_blk, pl.BlockSpec((heads, BLK, BLK), lambda i: (0, 0, 0)), one_row],
        out_specs=[row_blk, row_part],
        out_shape=[jax.ShapeDtypeStruct((tokens, width), f32), jax.ShapeDtypeStruct((tokens, BLK), f32)],
        compiler_params=params("arbitrary"),
        name="scale_squares",
    )(query_rows, num, d_pre, scale_row)
    shards = lax.axis_size("head")
    other = jnp.zeros_like(part)
    for turn in range(1, shards):
        other = other + lax.ppermute(part, "head", [(i, (i + turn) % shards) for i in range(shards)])
    return pl.pallas_call(
        functools.partial(norm_kernel, width * shards),
        grid=(tokens // step,),
        in_specs=[row_blk, row_part, row_part, one_row],
        out_specs=row_blk,
        out_shape=jax.ShapeDtypeStruct((tokens, width), bf16),
        compiler_params=params("arbitrary"),
        name="norm",
    )(y, part, other, out_gain[None, :])


def solution(mesh):
    return jax.shard_map(
        per_device,
        mesh=mesh,
        in_specs=(P("seq", "head"), P("seq", "head"), P("seq", "head"), P("head"), P("head")),
        out_specs=P("seq", "head"),
        check_vma=False,
    )
```

```python
import functools

import jax
import jax.numpy as jnp
from jax import lax
from jax.experimental import pallas as pl
from jax.experimental.pallas import tpu as pltpu
from jax.sharding import PartitionSpec as P

BLK = 128
CHUNK = 256
PAIR = 2
VMEM_LIMIT = 60 * 1024 * 1024

epsilon = 1e-06
f32, bf16 = jnp.float32, jnp.bfloat16

NN = (((1,), (0,)), ((), ()))
NT = (((1,), (1,)), ((), ()))
TN = (((0,), (0,)), ((), ()))


def dot(a, b, dims=NN):
    return lax.dot_general(a, b, dims, preferred_element_type=f32)


def split(a):
    high = a.astype(bf16)
    return high, (a - high.astype(f32)).astype(bf16)


def lanes(*parts):
    return jnp.concatenate(parts, axis=1)


def rows(*parts):
    return jnp.concatenate(parts, axis=0)


def dot_f32(a, b):
    a_high, a_low = split(a)
    b_high, b_low = split(b)
    return dot(lanes(a_high, a_low), rows(b_high, b_high)) + dot(a_high, b_low)


def ordered(size):
    shape = (size, size)
    return lax.broadcasted_iota(jnp.int32, shape, 0) - lax.broadcasted_iota(jnp.int32, shape, 1)


def span(j, size=BLK):
    return slice(j * size, (j + 1) * size)


def moments_kernel(q_ref, k_ref, v_ref, out_ref, kt_ref, vt_ref):
    for j in range(out_ref.shape[0]):
        at = span(j)
        k = k_ref[:, at]
        kt, vt = k.T, v_ref[:, at].T
        kt_ref[at, :], vt_ref[at, :] = kt, vt
        out_ref[j, :BLK] = dot(kt, k)
        out_ref[j, BLK:] = dot(vt, q_ref[:, at])


def first_stage_kernel(q_ref, k_ref, kt_ref, vt_ref, r_ref, d_ref, qt_ref):
    heads = d_ref.shape[0]
    mask = ordered(CHUNK) >= 0
    steps = q_ref.shape[0] // CHUNK
    states = [jnp.zeros((BLK, BLK), f32)] * heads
    for i in range(steps):
        at = span(i, CHUNK)
        for j in range(heads):
            cols = span(j)
            q, k, kt = q_ref[at, cols], k_ref[at, cols], kt_ref[cols, at]
            qt_ref[cols, at] = q.T
            r = dot(lanes(*split(jnp.where(mask, dot(q, kt), 0.0))), rows(k, k))
            if i > 0:
                r = r + dot(lanes(q, q), rows(*split(states[j])))
            if i + 1 < steps:
                states[j] = states[j] + dot(kt, k)
            r_ref[at, span(j, 2 * BLK)] = lanes(*split(r))
    for j in range(heads):
        d = dot(vt_ref[span(j), :], r_ref[:, span(j, 2 * BLK)])
        d_ref[j] = d[:, :BLK] + d[:, BLK:]


def second_stage_kernel(q_ref, qt_ref, vt_ref, r_ref, s_ref, num_ref):
    heads = s_ref.shape[0]
    mask = ordered(CHUNK) <= 0
    steps = q_ref.shape[0] // CHUNK
    states = [jnp.zeros((BLK, BLK), f32)] * heads
    s_both = [rows(*split(s_ref[j])) for j in range(heads)]
    for i in range(steps):
        at = span(i, CHUNK)
        for j in range(heads):
            cols = span(j)
            q, qt, vt = q_ref[at, cols], qt_ref[cols, at], vt_ref[cols, at]
            qt2 = rows(qt, qt)
            pair = r_ref[at, span(j, 2 * BLK)].astype(f32)
            r = lanes(*split(pair[:, :BLK] + pair[:, BLK:] + dot(lanes(q, q), s_both[j])))
            num = dot(lanes(vt, vt), rows(*split(jnp.where(mask, dot(r, qt2), 0.0))))
            if i > 0:
                num = num + dot(lanes(*split(states[j])), qt2)
            num_ref[cols, at] = num
            if i + 1 < steps:
                d = dot(vt, r)
                states[j] = states[j] + d[:, :BLK] + d[:, BLK:]


def owner_local_kernel(moments_ref, s_ref, c_ref, f_ref):
    members = moments_ref.shape[0]
    s = jnp.zeros((BLK, BLK), f32)
    c = jnp.zeros((BLK, BLK), f32)
    f = jnp.zeros((BLK, BLK), f32)
    for m in range(members):
        s_ref[m], c_ref[m], f_ref[m] = s, c, f
        c_own = moments_ref[m, BLK:]
        if m > 0:
            f = f + dot_f32(c_own, s)
        s = s + moments_ref[m, :BLK]
        c = c + c_own
    s_ref[members], c_ref[members], f_ref[members] = s, c, f


def owner_shift_kernel(s_ref, c_ref, f_ref, before_ref, back_ref, out_ref):
    members = back_ref.shape[0]
    before = before_ref[...]
    for m in range(members):
        back_ref[m] = s_ref[m] + before
    out_ref[0] = f_ref[0]
    for m in range(1, members + 1):
        out_ref[m] = f_ref[m] + dot_f32(c_ref[m], before)


def owner_sum_kernel(d_ref, h_ref, base_ref, total_ref):
    members = d_ref.shape[0]
    d = jnp.zeros((BLK, BLK), f32)
    for m in range(members):
        base_ref[m] = h_ref[m] + d
        d = d + d_ref[m]
    total_ref[...] = h_ref[members] + d


def add_kernel(base_ref, before_ref, out_ref):
    for m in range(out_ref.shape[0]):
        out_ref[m] = base_ref[m] + before_ref[...]


def scale_kernel(qt_ref, num_ref, d_ref, gain_ref, scale_ref, y_ref, part_ref):
    first = pl.program_id(0) * d_ref.shape[0]
    part = jnp.zeros((8, qt_ref.shape[1]), f32)
    for j in range(d_ref.shape[0]):
        qt = qt_ref[span(j), :]
        y = num_ref[span(j), :] + dot(lanes(*split(d_ref[j])), rows(qt, qt))
        y = y * scale_ref[first + j]
        part = part + jnp.sum((y * y).reshape(BLK // 8, 8, y.shape[1]), axis=0)
        gain = jnp.broadcast_to(gain_ref[j], (BLK, BLK)).T
        for i in range(y.shape[1] // BLK):
            y_ref[span(j), span(i)] = y[:, span(i)] * gain
    @pl.when(pl.program_id(0) == 0)
    def _():
        part_ref[...] = part
    @pl.when(pl.program_id(0) > 0)
    def _():
        part_ref[...] += part


def norm_kernel(features, y_ref, mine_ref, other_ref, out_ref):
    total = jnp.sum(mine_ref[...] + other_ref[...], axis=0, keepdims=True)
    inv = lax.rsqrt(total * (1.0 / features) + epsilon)
    out_ref[...] = (y_ref[...] * inv).astype(bf16).T


def params(*semantics):
    return pltpu.CompilerParams(dimension_semantics=semantics, vmem_limit_bytes=VMEM_LIMIT)


def cost(us, moved):
    return pl.CostEstimate(flops=int(us * 4e8), bytes_accessed=int(moved), transcendentals=0)


def per_device(query_rows, key_rows, value_rows, head_scale, out_gain):
    tokens, width = query_rows.shape
    heads = head_scale.shape[0]
    seq = lax.axis_size("seq")
    members = heads
    groups = seq // members
    index_groups = [[g * members + m for m in range(members)] for g in range(groups)]
    onward = [(i, i + members) for i in range(seq - members)]

    def swap(a):
        return lax.all_to_all(a, "seq", 0, 0, axis_index_groups=index_groups)

    head_col = pl.BlockSpec((tokens, PAIR * BLK), lambda h: (0, h))
    head_col2 = pl.BlockSpec((tokens, 2 * PAIR * BLK), lambda h: (0, h))
    head_row = pl.BlockSpec((PAIR * BLK, tokens), lambda h: (h, 0))
    head_mat = pl.BlockSpec((PAIR, BLK, BLK), lambda h: (h, 0, 0))
    mats = lambda n: jax.ShapeDtypeStruct((n, BLK, BLK), f32)
    mat = jax.ShapeDtypeStruct((BLK, BLK), f32)
    turned = jax.ShapeDtypeStruct((width, tokens), bf16)
    turned_f32 = jax.ShapeDtypeStruct((width, tokens), f32)

    moments, k_t, v_t = pl.pallas_call(
        moments_kernel,
        grid=(heads // PAIR,),
        in_specs=[head_col] * 3,
        out_specs=[pl.BlockSpec((PAIR, 2 * BLK, BLK), lambda h: (h, 0, 0)), head_row, head_row],
        out_shape=[jax.ShapeDtypeStruct((heads, 2 * BLK, BLK), f32), turned, turned],
        compiler_params=params("arbitrary"),
        name="moments",
    )(query_rows, key_rows, value_rows)
    moments_in = swap(moments)

    r_local, d_local, q_t = pl.pallas_call(
        first_stage_kernel,
        grid=(heads // PAIR,),
        in_specs=[head_col, head_col, head_row, head_row],
        out_specs=[head_col2, head_mat, head_row],
        out_shape=[jax.ShapeDtypeStruct((tokens, 2 * width), bf16), mats(heads), turned],
        compiler_params=params("arbitrary"),
        cost_estimate=cost(10, 10 * tokens * width),
        name="first_stage",
    )(query_rows, key_rows, k_t, v_t)
    d_in = swap(d_local)

    s_part, c_part, f_part = pl.pallas_call(
        owner_local_kernel,
        out_shape=[mats(members + 1)] * 3,
        compiler_params=params(),
        name="owner_local",
    )(moments_in)
    s_before = jnp.zeros((BLK, BLK), f32)
    for _ in range(groups - 1):
        s_before = lax.ppermute(s_before + s_part[members], "seq", onward)
    s_back, h_part = pl.pallas_call(
        owner_shift_kernel,
        out_shape=[mats(members), mats(members + 1)],
        compiler_params=params(),
        name="owner_shift",
    )(s_part, c_part, f_part, s_before)
    s_pre = swap(s_back)

    d_base, d_total = pl.pallas_call(
        owner_sum_kernel,
        out_shape=[mats(members), mat],
        compiler_params=params(),
        name="owner_sum",
    )(d_in, h_part)
    d_before = jnp.zeros((BLK, BLK), f32)
    for _ in range(groups - 1):
        d_before = lax.ppermute(d_before + d_total, "seq", onward)
    d_back = pl.pallas_call(
        add_kernel, out_shape=mats(members), compiler_params=params(), name="owner_add"
    )(d_base, d_before)
    d_pre = swap(d_back)

    num = pl.pallas_call(
        second_stage_kernel,
        grid=(heads // PAIR,),
        in_specs=[head_col, head_row, head_row, head_col2, head_mat],
        out_specs=head_row,
        out_shape=turned_f32,
        compiler_params=params("arbitrary"),
        cost_estimate=cost(10, 12 * tokens * width),
        name="second_stage",
    )(query_rows, q_t, v_t, r_local, s_pre)

    part_blk = pl.BlockSpec((8, tokens), lambda h: (0, 0))
    y, part = pl.pallas_call(
        scale_kernel,
        grid=(heads // PAIR,),
        in_specs=[
            head_row,
            head_row,
            head_mat,
            pl.BlockSpec((PAIR, 1, BLK), lambda h: (h, 0, 0)),
            pl.BlockSpec(memory_space=pltpu.SMEM),
        ],
        out_specs=[head_row, part_blk],
        out_shape=[turned_f32, jax.ShapeDtypeStruct((8, tokens), f32)],
        compiler_params=params("arbitrary"),
        name="scale_squares",
    )(q_t, num, d_pre, out_gain.reshape(heads, 1, BLK), head_scale)
    shards = lax.axis_size("head")
    other = jnp.zeros_like(part)
    for turn in range(1, shards):
        other = other + lax.ppermute(part, "head", [(i, (i + turn) % shards) for i in range(shards)])
    step = 256
    col_blk = pl.BlockSpec((width, step), lambda i: (0, i))
    col_part = pl.BlockSpec((8, step), lambda i: (0, i))
    return pl.pallas_call(
        functools.partial(norm_kernel, width * shards),
        grid=(tokens // step,),
        in_specs=[col_blk, col_part, col_part],
        out_specs=pl.BlockSpec((step, width), lambda i: (i, 0)),
        out_shape=jax.ShapeDtypeStruct((tokens, width), bf16),
        compiler_params=params("arbitrary"),
        name="norm",
    )(y, part, other)


def solution(mesh):
    return jax.shard_map(
        per_device,
        mesh=mesh,
        in_specs=(P("seq", "head"), P("seq", "head"), P("seq", "head"), P("head"), P("head")),
        out_specs=P("seq", "head"),
        check_vma=False,
    )
```

```python
import functools

import jax
import jax.numpy as jnp
from jax import lax
from jax.experimental import pallas as pl
from jax.experimental.pallas import tpu as pltpu
from jax.sharding import PartitionSpec as P

BLK = 128
CHUNK = 256
PAIR = 2
SMALL = 8 * 1024 * 1024
LARGE = 60 * 1024 * 1024

epsilon = 1e-06
f32, bf16 = jnp.float32, jnp.bfloat16

NN = (((1,), (0,)), ((), ()))
NT = (((1,), (1,)), ((), ()))
TN = (((0,), (0,)), ((), ()))


def dot(a, b, dims=NN):
    return lax.dot_general(a, b, dims, preferred_element_type=f32)


def split(a):
    high = a.astype(bf16)
    return high, (a - high.astype(f32)).astype(bf16)


def lanes(*parts):
    return jnp.concatenate(parts, axis=1)


def rows(*parts):
    return jnp.concatenate(parts, axis=0)


def dot_f32(a, b):
    a_high, a_low = split(a)
    b_high, b_low = split(b)
    return dot(lanes(a_high, a_low), rows(b_high, b_high)) + dot(a_high, b_low)


def ordered(size):
    shape = (size, size)
    return lax.broadcasted_iota(jnp.int32, shape, 0) - lax.broadcasted_iota(jnp.int32, shape, 1)


def span(j, size=BLK):
    return slice(j * size, (j + 1) * size)


def columns(p):
    return pl.ds(pl.multiple_of(p * PAIR * BLK, PAIR * BLK), PAIR * BLK)


def copies(moves, sems, p):
    return [
        pltpu.make_async_copy(source(p), target(p), sems.at[n, p])
        for n, (source, target) in enumerate(moves)
    ]


def streamed(pairs, reads, writes, read_sems, write_sems, body):
    for p in range(pairs):
        for copy in copies(reads, read_sems, p):
            copy.start()

    @pl.loop(0, pairs)
    def _(p):
        for copy in copies(reads, read_sems, p):
            copy.wait()
        body(p)
        for copy in copies(writes, write_sems, p):
            copy.start()

    for p in range(pairs):
        for copy in copies(writes, write_sems, p):
            copy.wait()


def by_columns(hbm):
    return lambda p: hbm.at[:, columns(p)]


def by_pair(ref):
    return lambda p: ref.at[p]


def moments_kernel(q_hbm, k_hbm, v_hbm, m_hbm, kt_hbm, vt_hbm, q_ref, k_ref, v_ref, m_ref, kt_ref, vt_ref, *sems):
    def body(p):
        for j in range(PAIR):
            k = k_ref[p, :, span(j)]
            kt, vt = k.T, v_ref[p, :, span(j)].T
            kt_ref[p, span(j)], vt_ref[p, span(j)] = kt, vt
            m_ref[p, j, :BLK] = dot(kt, k)
            m_ref[p, j, BLK:] = dot(vt, q_ref[p, :, span(j)])

    reads = [(by_columns(a), by_pair(b)) for a, b in ((k_hbm, k_ref), (v_hbm, v_ref), (q_hbm, q_ref))]
    writes = [(by_pair(a), by_pair(b)) for a, b in ((kt_ref, kt_hbm), (vt_ref, vt_hbm), (m_ref, m_hbm))]
    streamed(q_ref.shape[0], reads, writes, *sems, body)


def first_stage_kernel(
    q_hbm, k_hbm, kt_hbm, vt_hbm, r_hbm, d_hbm, qt_hbm, q_ref, k_ref, kt_ref, vt_ref, r_ref, d_ref, qt_ref, *sems
):
    steps = q_ref.shape[1] // CHUNK
    mask = ordered(CHUNK) >= 0

    def body(p):
        states = [jnp.zeros((BLK, BLK), f32)] * PAIR
        for i in range(steps):
            at = span(i, CHUNK)
            for j in range(PAIR):
                q, k, kt = q_ref[p, at, span(j)], k_ref[p, at, span(j)], kt_ref[p, span(j), at]
                qt_ref[p, span(j), at] = q.T
                r = dot(lanes(*split(jnp.where(mask, dot(q, kt), 0.0))), rows(k, k))
                if i > 0:
                    r = r + dot(lanes(q, q), rows(*split(states[j])))
                if i + 1 < steps:
                    states[j] = states[j] + dot(kt, k)
                r_ref[p, j, at] = lanes(*split(r))
        for j in range(PAIR):
            d = dot(vt_ref[p, span(j)], r_ref[p, j])
            d_ref[p, j] = d[:, :BLK] + d[:, BLK:]

    reads = [(by_columns(a), by_pair(b)) for a, b in ((q_hbm, q_ref), (k_hbm, k_ref))]
    reads += [(by_pair(a), by_pair(b)) for a, b in ((kt_hbm, kt_ref), (vt_hbm, vt_ref))]
    writes = [(by_pair(a), by_pair(b)) for a, b in ((r_ref, r_hbm), (d_ref, d_hbm), (qt_ref, qt_hbm))]
    streamed(q_ref.shape[0], reads, writes, *sems, body)


def second_stage_kernel(
    q_hbm, qt_hbm, vt_hbm, r_hbm, s_hbm, num_hbm, q_ref, qt_ref, vt_ref, r_ref, s_ref, num_ref, *sems
):
    steps = q_ref.shape[1] // CHUNK
    mask = ordered(CHUNK) <= 0

    def body(p):
        states = [jnp.zeros((BLK, BLK), f32)] * PAIR
        s_both = [rows(*split(s_ref[p, j])) for j in range(PAIR)]
        for i in range(steps):
            at = span(i, CHUNK)
            for j in range(PAIR):
                q, qt, vt = q_ref[p, at, span(j)], qt_ref[p, span(j), at], vt_ref[p, span(j), at]
                qt2 = rows(qt, qt)
                pair = r_ref[p, j, at].astype(f32)
                r = lanes(*split(pair[:, :BLK] + pair[:, BLK:] + dot(lanes(q, q), s_both[j])))
                num = dot(lanes(vt, vt), rows(*split(jnp.where(mask, dot(r, qt2), 0.0))))
                if i > 0:
                    num = num + dot(lanes(*split(states[j])), qt2)
                num_ref[p, span(j), at] = num
                if i + 1 < steps:
                    d = dot(vt, r)
                    states[j] = states[j] + d[:, :BLK] + d[:, BLK:]

    reads = [(by_columns(q_hbm), by_pair(q_ref))]
    reads += [
        (by_pair(a), by_pair(b))
        for a, b in ((s_hbm, s_ref), (r_hbm, r_ref), (qt_hbm, qt_ref), (vt_hbm, vt_ref))
    ]
    streamed(q_ref.shape[0], reads, [(by_pair(num_ref), by_pair(num_hbm))], *sems, body)


def owner_local_kernel(moments_ref, s_ref, c_ref, f_ref):
    members = moments_ref.shape[0]
    s = jnp.zeros((BLK, BLK), f32)
    c = jnp.zeros((BLK, BLK), f32)
    f = jnp.zeros((BLK, BLK), f32)
    for m in range(members):
        s_ref[m], c_ref[m], f_ref[m] = s, c, f
        c_own = moments_ref[m, BLK:]
        if m > 0:
            f = f + dot_f32(c_own, s)
        s = s + moments_ref[m, :BLK]
        c = c + c_own
    s_ref[members], c_ref[members], f_ref[members] = s, c, f


def owner_shift_kernel(s_ref, c_ref, f_ref, before_ref, back_ref, out_ref):
    members = back_ref.shape[0]
    before = before_ref[...]
    for m in range(members):
        back_ref[m] = s_ref[m] + before
    out_ref[0] = f_ref[0]
    for m in range(1, members + 1):
        out_ref[m] = f_ref[m] + dot_f32(c_ref[m], before)


def owner_sum_kernel(d_ref, h_ref, base_ref, total_ref):
    members = d_ref.shape[0]
    d = jnp.zeros((BLK, BLK), f32)
    for m in range(members):
        base_ref[m] = h_ref[m] + d
        d = d + d_ref[m]
    total_ref[...] = h_ref[members] + d


def add_kernel(base_ref, before_ref, out_ref):
    for m in range(out_ref.shape[0]):
        out_ref[m] = base_ref[m] + before_ref[...]


def scale_kernel(
    qt_hbm, num_hbm, d_hbm, gain_ref, scale_ref, y_hbm, part_ref, qt_ref, num_ref, d_ref, y_ref, *sems
):
    pairs, _, tokens = qt_ref.shape
    part_ref[...] = jnp.zeros_like(part_ref)

    def body(p):
        part = part_ref[...]
        for j in range(PAIR):
            h = p * PAIR + j
            qt = qt_ref[p, span(j)]
            y = (num_ref[p, span(j)] + dot(lanes(*split(d_ref[p, j])), rows(qt, qt))) * scale_ref[h]
            part = part + jnp.sum((y * y).reshape(BLK // 8, 8, tokens), axis=0)
            gain = jnp.broadcast_to(gain_ref[h], (BLK, BLK)).T
            for i in range(tokens // BLK):
                y_ref[p, span(j), span(i)] = y[:, span(i)] * gain
        part_ref[...] = part

    reads = [(by_pair(a), by_pair(b)) for a, b in ((d_hbm, d_ref), (qt_hbm, qt_ref), (num_hbm, num_ref))]
    streamed(pairs, reads, [(by_pair(y_ref), by_pair(y_hbm))], *sems, body)


def norm_kernel(features, y_hbm, mine_hbm, other_hbm, out_hbm, y_ref, parts_ref, out_ref, y_sems, part_sems, sems):
    pairs, wide, tokens = y_ref.shape
    steps = tokens // CHUNK

    def y_copy(i):
        at = span(i, CHUNK)
        return pltpu.make_async_copy(y_hbm.at[:, :, at], y_ref.at[:, :, at], y_sems.at[i])

    def out_copy(i):
        at = span(i, CHUNK)
        return pltpu.make_async_copy(out_ref.at[at], out_hbm.at[at], sems.at[i])

    def part_copy(n):
        return pltpu.make_async_copy((mine_hbm, other_hbm)[n], parts_ref.at[n], part_sems.at[n])

    part_copy(0).start()
    part_copy(1).start()
    for i in range(steps):
        y_copy(i).start()
    part_copy(0).wait()
    part_copy(1).wait()
    total = jnp.sum(parts_ref[0] + parts_ref[1], axis=0, keepdims=True)
    inv = lax.rsqrt(total * (1.0 / features) + epsilon)
    for i in range(steps):
        at = span(i, CHUNK)
        y_copy(i).wait()
        for p in range(pairs):
            out_ref[at, span(p, wide)] = (y_ref[p, :, at] * inv[:, at]).astype(bf16).T
        out_copy(i).start()
    for i in range(steps):
        out_copy(i).wait()


def params(limit=SMALL):
    return pltpu.CompilerParams(vmem_limit_bytes=limit)


def cost(us, moved):
    return pl.CostEstimate(flops=int(us * 4e8), bytes_accessed=int(moved), transcendentals=0)


def per_device(query_rows, key_rows, value_rows, head_scale, out_gain):
    tokens, width = query_rows.shape
    heads = head_scale.shape[0]
    seq = lax.axis_size("seq")
    members = heads
    groups = seq // members
    index_groups = [[g * members + m for m in range(members)] for g in range(groups)]
    onward = [(i, i + members) for i in range(seq - members)]

    def swap(a):
        return lax.all_to_all(a, "seq", 0, 0, axis_index_groups=index_groups)

    mats = lambda n: jax.ShapeDtypeStruct((n, BLK, BLK), f32)
    mat = jax.ShapeDtypeStruct((BLK, BLK), f32)
    pairs = heads // PAIR
    shape = jax.ShapeDtypeStruct
    upright = shape((pairs, tokens, PAIR * BLK), bf16)
    turned = shape((pairs, PAIR * BLK, tokens), bf16)
    turned_f32 = shape((pairs, PAIR * BLK, tokens), f32)
    twofold = shape((pairs, PAIR, tokens, 2 * BLK), bf16)
    pair_mats = shape((pairs, PAIR, BLK, BLK), f32)
    moment_mats = shape((pairs, PAIR, 2 * BLK, BLK), f32)
    in_hbm = pl.BlockSpec(memory_space=pltpu.HBM)

    def buffers(reads, writes):
        sems = [pltpu.SemaphoreType.DMA((len(a), pairs)) for a in (reads, writes)]
        return [pltpu.VMEM(a.shape, a.dtype) for a in reads + writes] + sems

    def stream_call(kernel, reads, writes, us, name):
        return pl.pallas_call(
            kernel,
            in_specs=[in_hbm] * len(reads),
            out_specs=[in_hbm] * len(writes),
            out_shape=writes,
            scratch_shapes=buffers(reads, writes),
            compiler_params=params(LARGE),
            cost_estimate=cost(us, 10 * tokens * width),
            name=name,
        )

    moments, k_t, v_t = pl.pallas_call(
        moments_kernel,
        in_specs=[in_hbm] * 3,
        out_specs=[in_hbm] * 3,
        out_shape=[moment_mats, turned, turned],
        scratch_shapes=buffers([upright] * 3, [moment_mats, turned, turned]),
        compiler_params=params(LARGE),
        name="moments",
    )(query_rows, key_rows, value_rows)
    moments_in = swap(moments.reshape(heads, 2 * BLK, BLK))

    r_local, d_local, q_t = stream_call(
        first_stage_kernel, [upright, upright, turned, turned], [twofold, pair_mats, turned], 10, "first_stage"
    )(query_rows, key_rows, k_t, v_t)
    d_in = swap(d_local.reshape(heads, BLK, BLK))

    s_part, c_part, f_part = pl.pallas_call(
        owner_local_kernel,
        out_shape=[mats(members + 1)] * 3,
        compiler_params=params(),
        name="owner_local",
    )(moments_in)
    s_before = jnp.zeros((BLK, BLK), f32)
    for _ in range(groups - 1):
        s_before = lax.ppermute(s_before + s_part[members], "seq", onward)
    s_back, h_part = pl.pallas_call(
        owner_shift_kernel,
        out_shape=[mats(members), mats(members + 1)],
        compiler_params=params(),
        name="owner_shift",
    )(s_part, c_part, f_part, s_before)
    s_pre = swap(s_back)

    d_base, d_total = pl.pallas_call(
        owner_sum_kernel,
        out_shape=[mats(members), mat],
        compiler_params=params(),
        name="owner_sum",
    )(d_in, h_part)
    d_before = jnp.zeros((BLK, BLK), f32)
    for _ in range(groups - 1):
        d_before = lax.ppermute(d_before + d_total, "seq", onward)
    d_back = pl.pallas_call(
        add_kernel, out_shape=mats(members), compiler_params=params(), name="owner_add"
    )(d_base, d_before)
    d_pre = swap(d_back)

    (num,) = stream_call(
        second_stage_kernel, [upright, turned, turned, twofold, pair_mats], [turned_f32], 10, "second_stage"
    )(query_rows, q_t, v_t, r_local, s_pre.reshape(pair_mats.shape))

    in_vmem = pl.BlockSpec(memory_space=pltpu.VMEM)
    part_shape = shape((8, tokens), f32)
    y, part = pl.pallas_call(
        scale_kernel,
        in_specs=[in_hbm] * 3 + [in_vmem, pl.BlockSpec(memory_space=pltpu.SMEM)],
        out_specs=[in_hbm, in_vmem],
        out_shape=[turned_f32, part_shape],
        scratch_shapes=buffers([turned, turned_f32, pair_mats], [turned_f32]),
        compiler_params=params(LARGE),
        name="scale_squares",
    )(q_t, num, d_pre.reshape(pair_mats.shape), out_gain.reshape(heads, 1, BLK), head_scale)
    shards = lax.axis_size("head")
    other = jnp.zeros_like(part)
    for turn in range(1, shards):
        other = other + lax.ppermute(part, "head", [(i, (i + turn) % shards) for i in range(shards)])
    steps = tokens // CHUNK
    return pl.pallas_call(
        functools.partial(norm_kernel, width * shards),
        in_specs=[in_hbm] * 3,
        out_specs=in_hbm,
        out_shape=shape((tokens, width), bf16),
        scratch_shapes=[
            pltpu.VMEM(turned_f32.shape, f32),
            pltpu.VMEM((2, 8, tokens), f32),
            pltpu.VMEM((tokens, width), bf16),
            pltpu.SemaphoreType.DMA((steps,)),
            pltpu.SemaphoreType.DMA((2,)),
            pltpu.SemaphoreType.DMA((steps,)),
        ],
        compiler_params=params(LARGE),
        name="norm",
    )(y, part, other)


def solution(mesh):
    return jax.shard_map(
        per_device,
        mesh=mesh,
        in_specs=(P("seq", "head"), P("seq", "head"), P("seq", "head"), P("head"), P("head")),
        out_specs=P("seq", "head"),
        check_vma=False,
    )
```

```python
import functools

import jax
import jax.numpy as jnp
from jax import lax
from jax.experimental import pallas as pl
from jax.experimental.pallas import tpu as pltpu
from jax.sharding import PartitionSpec as P

BLK = 128
CHUNK = 256
PAIR = 2
SMALL = 8 * 1024 * 1024
LARGE = 60 * 1024 * 1024

epsilon = 1e-06
f32, bf16 = jnp.float32, jnp.bfloat16

NN = (((1,), (0,)), ((), ()))
NT = (((1,), (1,)), ((), ()))
TN = (((0,), (0,)), ((), ()))


def dot(a, b, dims=NN):
    return lax.dot_general(a, b, dims, preferred_element_type=f32)


def split(a):
    high = a.astype(bf16)
    return high, (a - high.astype(f32)).astype(bf16)


def lanes(*parts):
    return jnp.concatenate(parts, axis=1)


def rows(*parts):
    return jnp.concatenate(parts, axis=0)


def dot_f32(a, b):
    a_high, a_low = split(a)
    b_high, b_low = split(b)
    return dot(lanes(a_high, a_low), rows(b_high, b_high)) + dot(a_high, b_low)


def ordered(size):
    shape = (size, size)
    return lax.broadcasted_iota(jnp.int32, shape, 0) - lax.broadcasted_iota(jnp.int32, shape, 1)


def span(j, size=BLK):
    return slice(j * size, (j + 1) * size)


def columns(p):
    return pl.ds(pl.multiple_of(p * PAIR * BLK, PAIR * BLK), PAIR * BLK)


def copies(moves, sems, p):
    return [
        pltpu.make_async_copy(source(p), target(p), sems.at[n, p])
        for n, (source, target) in enumerate(moves)
    ]


def streamed(pairs, reads, writes, read_sems, write_sems, body):
    for copy in copies(reads, read_sems, 0):
        copy.start()

    @pl.loop(0, pairs)
    def _(p):
        for copy in copies(reads, read_sems, p):
            copy.wait()

        @pl.when(p + 1 < pairs)
        def _():
            for copy in copies(reads, read_sems, p + 1):
                copy.start()

        body(p)
        for copy in copies(writes, write_sems, p):
            copy.start()

    for p in range(pairs):
        for copy in copies(writes, write_sems, p):
            copy.wait()


def by_columns(hbm):
    return lambda p: hbm.at[:, columns(p)]


def by_pair(ref):
    return lambda p: ref.at[p]


def moments_kernel(q_hbm, k_hbm, v_hbm, m_hbm, kt_hbm, vt_hbm, q_ref, k_ref, v_ref, m_ref, kt_ref, vt_ref, *sems):
    def body(p):
        for j in range(PAIR):
            k = k_ref[p, :, span(j)]
            kt, vt = k.T, v_ref[p, :, span(j)].T
            kt_ref[p, span(j)], vt_ref[p, span(j)] = kt, vt
            m_ref[p, j, :BLK] = dot(kt, k)
            m_ref[p, j, BLK:] = dot(vt, q_ref[p, :, span(j)])

    reads = [(by_columns(a), by_pair(b)) for a, b in ((k_hbm, k_ref), (v_hbm, v_ref), (q_hbm, q_ref))]
    writes = [(by_pair(a), by_pair(b)) for a, b in ((kt_ref, kt_hbm), (vt_ref, vt_hbm), (m_ref, m_hbm))]
    streamed(q_ref.shape[0], reads, writes, *sems, body)


def first_stage_kernel(
    q_hbm, k_hbm, kt_hbm, vt_hbm, r_hbm, d_hbm, qt_hbm, q_ref, k_ref, kt_ref, vt_ref, r_ref, d_ref, qt_ref, *sems
):
    steps = q_ref.shape[1] // CHUNK
    mask = ordered(CHUNK) >= 0

    def body(p):
        states = [jnp.zeros((BLK, BLK), f32)] * PAIR
        for i in range(steps):
            at = span(i, CHUNK)
            for j in range(PAIR):
                q, k, kt = q_ref[p, at, span(j)], k_ref[p, at, span(j)], kt_ref[p, span(j), at]
                qt_ref[p, span(j), at] = q.T
                r = dot(lanes(*split(jnp.where(mask, dot(q, kt), 0.0))), rows(k, k))
                if i > 0:
                    r = r + dot(lanes(q, q), rows(*split(states[j])))
                if i + 1 < steps:
                    states[j] = states[j] + dot(kt, k)
                r_ref[p, j, at] = lanes(*split(r))
        for j in range(PAIR):
            d = dot(vt_ref[p, span(j)], r_ref[p, j])
            d_ref[p, j] = d[:, :BLK] + d[:, BLK:]

    reads = [(by_columns(a), by_pair(b)) for a, b in ((q_hbm, q_ref), (k_hbm, k_ref))]
    reads += [(by_pair(a), by_pair(b)) for a, b in ((kt_hbm, kt_ref), (vt_hbm, vt_ref))]
    writes = [(by_pair(a), by_pair(b)) for a, b in ((r_ref, r_hbm), (d_ref, d_hbm), (qt_ref, qt_hbm))]
    streamed(q_ref.shape[0], reads, writes, *sems, body)


def second_stage_kernel(
    q_hbm, qt_hbm, vt_hbm, r_hbm, s_hbm, num_hbm, q_ref, qt_ref, vt_ref, r_ref, s_ref, num_ref, *sems
):
    steps = q_ref.shape[1] // CHUNK
    mask = ordered(CHUNK) <= 0

    def body(p):
        states = [jnp.zeros((BLK, BLK), f32)] * PAIR
        s_both = [rows(*split(s_ref[p, j])) for j in range(PAIR)]
        for i in range(steps):
            at = span(i, CHUNK)
            for j in range(PAIR):
                q, qt, vt = q_ref[p, at, span(j)], qt_ref[p, span(j), at], vt_ref[p, span(j), at]
                qt2 = rows(qt, qt)
                pair = r_ref[p, j, at].astype(f32)
                r = lanes(*split(pair[:, :BLK] + pair[:, BLK:] + dot(lanes(q, q), s_both[j])))
                num = dot(lanes(vt, vt), rows(*split(jnp.where(mask, dot(r, qt2), 0.0))))
                if i > 0:
                    num = num + dot(lanes(*split(states[j])), qt2)
                num_ref[p, span(j), at] = num
                if i + 1 < steps:
                    d = dot(vt, r)
                    states[j] = states[j] + d[:, :BLK] + d[:, BLK:]

    reads = [(by_columns(q_hbm), by_pair(q_ref))]
    reads += [
        (by_pair(a), by_pair(b))
        for a, b in ((s_hbm, s_ref), (r_hbm, r_ref), (qt_hbm, qt_ref), (vt_hbm, vt_ref))
    ]
    streamed(q_ref.shape[0], reads, [(by_pair(num_ref), by_pair(num_hbm))], *sems, body)


def owner_local_kernel(moments_ref, s_ref, c_ref, f_ref):
    members = moments_ref.shape[0]
    s = jnp.zeros((BLK, BLK), f32)
    c = jnp.zeros((BLK, BLK), f32)
    f = jnp.zeros((BLK, BLK), f32)
    for m in range(members):
        s_ref[m], c_ref[m], f_ref[m] = s, c, f
        c_own = moments_ref[m, BLK:]
        if m > 0:
            f = f + dot_f32(c_own, s)
        s = s + moments_ref[m, :BLK]
        c = c + c_own
    s_ref[members], c_ref[members], f_ref[members] = s, c, f


def masked(ref, members):
    return jnp.where(lax.axis_index("seq") < members, 0.0, ref[...])


def owner_shift_kernel(s_ref, c_ref, f_ref, before_ref, back_ref, out_ref):
    members = back_ref.shape[0]
    before = masked(before_ref, members)
    for m in range(members):
        back_ref[m] = s_ref[m] + before
    out_ref[0] = f_ref[0]
    for m in range(1, members + 1):
        out_ref[m] = f_ref[m] + dot_f32(c_ref[m], before)


def owner_sum_kernel(d_ref, h_ref, base_ref, total_ref):
    members = d_ref.shape[0]
    d = jnp.zeros((BLK, BLK), f32)
    for m in range(members):
        base_ref[m] = h_ref[m] + d
        d = d + d_ref[m]
    total_ref[...] = h_ref[members] + d


def add_kernel(base_ref, before_ref, out_ref):
    members = out_ref.shape[0]
    before = masked(before_ref, members)
    for m in range(members):
        out_ref[m] = base_ref[m] + before


def scale_kernel(
    qt_hbm, num_hbm, d_hbm, gain_ref, scale_ref, y_hbm, part_ref, qt_ref, num_ref, d_ref, y_ref, *sems
):
    pairs, _, tokens = qt_ref.shape
    part_ref[...] = jnp.zeros_like(part_ref)

    def body(p):
        part = part_ref[...]
        for j in range(PAIR):
            h = p * PAIR + j
            qt = qt_ref[p, span(j)]
            y = (num_ref[p, span(j)] + dot(lanes(*split(d_ref[p, j])), rows(qt, qt))) * scale_ref[h]
            part = part + jnp.sum((y * y).reshape(BLK // 8, 8, tokens), axis=0)
            gain = jnp.broadcast_to(gain_ref[h], (BLK, BLK)).T
            for i in range(tokens // BLK):
                y_ref[p, span(j), span(i)] = y[:, span(i)] * gain
        part_ref[...] = part

    reads = [(by_pair(a), by_pair(b)) for a, b in ((d_hbm, d_ref), (qt_hbm, qt_ref), (num_hbm, num_ref))]
    streamed(pairs, reads, [(by_pair(y_ref), by_pair(y_hbm))], *sems, body)


def norm_kernel(features, y_hbm, mine_hbm, other_hbm, out_hbm, y_ref, parts_ref, out_ref, y_sems, part_sems, sems):
    pairs, wide, tokens = y_ref.shape
    steps = tokens // CHUNK

    def y_copy(i):
        at = span(i, CHUNK)
        return pltpu.make_async_copy(y_hbm.at[:, :, at], y_ref.at[:, :, at], y_sems.at[i])

    def out_copy(i):
        at = span(i, CHUNK)
        return pltpu.make_async_copy(out_ref.at[at], out_hbm.at[at], sems.at[i])

    def part_copy(n):
        return pltpu.make_async_copy((mine_hbm, other_hbm)[n], parts_ref.at[n], part_sems.at[n])

    part_copy(0).start()
    part_copy(1).start()
    for i in range(steps):
        y_copy(i).start()
    part_copy(0).wait()
    part_copy(1).wait()
    total = jnp.sum(parts_ref[0] + parts_ref[1], axis=0, keepdims=True)
    inv = lax.rsqrt(total * (1.0 / features) + epsilon)
    for i in range(steps):
        at = span(i, CHUNK)
        y_copy(i).wait()
        for p in range(pairs):
            out_ref[at, span(p, wide)] = (y_ref[p, :, at] * inv[:, at]).astype(bf16).T
        out_copy(i).start()
    for i in range(steps):
        out_copy(i).wait()


def params(limit=SMALL):
    return pltpu.CompilerParams(vmem_limit_bytes=limit)


def cost(us, moved):
    return pl.CostEstimate(flops=int(us * 4e8), bytes_accessed=int(moved), transcendentals=0)


def per_device(query_rows, key_rows, value_rows, head_scale, out_gain):
    tokens, width = query_rows.shape
    heads = head_scale.shape[0]
    seq = lax.axis_size("seq")
    members = heads
    groups = seq // members
    index_groups = [[g * members + m for m in range(members)] for g in range(groups)]
    onward = [(i, i + members) for i in range(seq - members)]
    if groups == 2:
        onward += [(i + members, i) for i in range(members)]

    def swap(a):
        return lax.all_to_all(a, "seq", 0, 0, axis_index_groups=index_groups)

    mats = lambda n: jax.ShapeDtypeStruct((n, BLK, BLK), f32)
    mat = jax.ShapeDtypeStruct((BLK, BLK), f32)
    pairs = heads // PAIR
    shape = jax.ShapeDtypeStruct
    upright = shape((pairs, tokens, PAIR * BLK), bf16)
    turned = shape((pairs, PAIR * BLK, tokens), bf16)
    turned_f32 = shape((pairs, PAIR * BLK, tokens), f32)
    twofold = shape((pairs, PAIR, tokens, 2 * BLK), bf16)
    pair_mats = shape((pairs, PAIR, BLK, BLK), f32)
    moment_mats = shape((pairs, PAIR, 2 * BLK, BLK), f32)
    in_hbm = pl.BlockSpec(memory_space=pl.ANY)

    def buffers(reads, writes):
        sems = [pltpu.SemaphoreType.DMA((len(a), pairs)) for a in (reads, writes)]
        return [pltpu.VMEM(a.shape, a.dtype) for a in reads + writes] + sems

    def stream_call(kernel, reads, writes, us, name):
        return pl.pallas_call(
            kernel,
            in_specs=[in_hbm] * len(reads),
            out_specs=[in_hbm] * len(writes),
            out_shape=writes,
            scratch_shapes=buffers(reads, writes),
            compiler_params=params(LARGE),
            cost_estimate=cost(us, 10 * tokens * width),
            name=name,
        )

    moments, k_t, v_t = pl.pallas_call(
        moments_kernel,
        in_specs=[in_hbm] * 3,
        out_specs=[in_hbm] * 3,
        out_shape=[moment_mats, turned, turned],
        scratch_shapes=buffers([upright] * 3, [moment_mats, turned, turned]),
        compiler_params=params(LARGE),
        name="moments",
    )(query_rows, key_rows, value_rows)
    moments_in = swap(moments.reshape(heads, 2 * BLK, BLK))

    r_local, d_local, q_t = stream_call(
        first_stage_kernel, [upright, upright, turned, turned], [twofold, pair_mats, turned], 10, "first_stage"
    )(query_rows, key_rows, k_t, v_t)
    d_in = swap(d_local.reshape(heads, BLK, BLK))

    s_part, c_part, f_part = pl.pallas_call(
        owner_local_kernel,
        out_shape=[mats(members + 1)] * 3,
        compiler_params=params(),
        name="owner_local",
    )(moments_in)
    s_before = jnp.zeros((BLK, BLK), f32)
    for _ in range(groups - 1):
        s_before = lax.ppermute(s_before + s_part[members], "seq", onward)
    s_back, h_part = pl.pallas_call(
        owner_shift_kernel,
        out_shape=[mats(members), mats(members + 1)],
        compiler_params=params(),
        name="owner_shift",
    )(s_part, c_part, f_part, s_before)
    s_pre = swap(s_back)

    d_base, d_total = pl.pallas_call(
        owner_sum_kernel,
        out_shape=[mats(members), mat],
        compiler_params=params(),
        name="owner_sum",
    )(d_in, h_part)
    d_before = jnp.zeros((BLK, BLK), f32)
    for _ in range(groups - 1):
        d_before = lax.ppermute(d_before + d_total, "seq", onward)
    d_back = pl.pallas_call(
        add_kernel, out_shape=mats(members), compiler_params=params(), name="owner_add"
    )(d_base, d_before)
    d_pre = swap(d_back)

    (num,) = stream_call(
        second_stage_kernel, [upright, turned, turned, twofold, pair_mats], [turned_f32], 10, "second_stage"
    )(query_rows, q_t, v_t, r_local, s_pre.reshape(pair_mats.shape))

    in_vmem = pl.BlockSpec(memory_space=pltpu.VMEM)
    part_shape = shape((8, tokens), f32)
    y, part = pl.pallas_call(
        scale_kernel,
        in_specs=[in_hbm] * 3 + [in_vmem, pl.BlockSpec(memory_space=pltpu.SMEM)],
        out_specs=[in_hbm, in_vmem],
        out_shape=[turned_f32, part_shape],
        scratch_shapes=buffers([turned, turned_f32, pair_mats], [turned_f32]),
        compiler_params=params(LARGE),
        name="scale_squares",
    )(q_t, num, d_pre.reshape(pair_mats.shape), out_gain.reshape(heads, 1, BLK), head_scale)
    shards = lax.axis_size("head")
    other = jnp.zeros_like(part)
    for turn in range(1, shards):
        other = other + lax.ppermute(part, "head", [(i, (i + turn) % shards) for i in range(shards)])
    steps = tokens // CHUNK
    return pl.pallas_call(
        functools.partial(norm_kernel, width * shards),
        in_specs=[in_hbm] * 3,
        out_specs=in_hbm,
        out_shape=shape((tokens, width), bf16),
        scratch_shapes=[
            pltpu.VMEM(turned_f32.shape, f32),
            pltpu.VMEM((2, 8, tokens), f32),
            pltpu.VMEM((tokens, width), bf16),
            pltpu.SemaphoreType.DMA((steps,)),
            pltpu.SemaphoreType.DMA((2,)),
            pltpu.SemaphoreType.DMA((steps,)),
        ],
        compiler_params=params(LARGE),
        name="norm",
    )(y, part, other)


def solution(mesh):
    return jax.shard_map(
        per_device,
        mesh=mesh,
        in_specs=(P("seq", "head"), P("seq", "head"), P("seq", "head"), P("head"), P("head")),
        out_specs=P("seq", "head"),
        check_vma=False,
    )
```

```python
import functools

import jax
import jax.numpy as jnp
from jax import lax
from jax.experimental import pallas as pl
from jax.experimental.pallas import tpu as pltpu
from jax.sharding import PartitionSpec as P

BLK = 128
CHUNK = 256
PAIR = 2
SMALL = 8 * 1024 * 1024
LARGE = 60 * 1024 * 1024
LATE = 52 * 1024 * 1024
LAST = 52 * 1024 * 1024

epsilon = 1e-06
f32, bf16 = jnp.float32, jnp.bfloat16

NN = (((1,), (0,)), ((), ()))
NT = (((1,), (1,)), ((), ()))
TN = (((0,), (0,)), ((), ()))


def dot(a, b, dims=NN):
    return lax.dot_general(a, b, dims, preferred_element_type=f32)


def split(a):
    high = a.astype(bf16)
    return high, (a - high.astype(f32)).astype(bf16)


def lanes(*parts):
    return jnp.concatenate(parts, axis=1)


def rows(*parts):
    return jnp.concatenate(parts, axis=0)


def dot_f32(a, b):
    a_high, a_low = split(a)
    b_high, b_low = split(b)
    return dot(lanes(a_high, a_low), rows(b_high, b_high)) + dot(a_high, b_low)


def ordered(size):
    shape = (size, size)
    return lax.broadcasted_iota(jnp.int32, shape, 0) - lax.broadcasted_iota(jnp.int32, shape, 1)


def span(j, size=BLK):
    return slice(j * size, (j + 1) * size)


def columns(p):
    return pl.ds(pl.multiple_of(p * PAIR * BLK, PAIR * BLK), PAIR * BLK)


def copies(moves, sems, p):
    return [
        pltpu.make_async_copy(source(p), target(p), sems.at[n, p])
        for n, (source, target) in enumerate(moves)
    ]


def start(moves, sems, first, last):
    for p in range(first, last):
        for copy in copies(moves, sems, p):
            copy.start()


def wait(moves, sems, p):
    for copy in copies(moves, sems, p):
        copy.wait()


def by_columns(hbm):
    return lambda p: hbm.at[:, columns(p)]


def by_pair(ref):
    return lambda p: ref.at[p]


def by_mats(ref):
    return lambda p: ref.at[pl.ds(p * PAIR, PAIR)]


def moments_kernel(q_hbm, k_hbm, v_hbm, m_hbm, q_ref, k_ref, v_ref, m_ref, read_sems, write_sems):
    pairs = q_ref.shape[0]
    reads = [(by_columns(a), by_pair(b)) for a, b in ((k_hbm, k_ref), (v_hbm, v_ref), (q_hbm, q_ref))]
    writes = [(by_pair(m_ref), by_pair(m_hbm))]
    start(reads, read_sems, 0, pairs)
    for p in range(pairs):
        wait(reads, read_sems, p)
        for j in range(PAIR):
            k = k_ref[p, :, span(j)]
            m_ref[p, j, :BLK] = dot(k.T, k)
            m_ref[p, j, BLK:] = dot(v_ref[p, :, span(j)].T, q_ref[p, :, span(j)])
        start(writes, write_sems, p, p + 1)
    for p in range(pairs):
        wait(writes, write_sems, p)


def first_stage_kernel(
    q_hbm, k_hbm, v_hbm, r_hbm, d_hbm, q_ref, k_ref, v_ref, r_ref, d_ref, read_sems, write_sems
):
    pairs, tokens, _ = q_ref.shape
    steps = tokens // CHUNK
    mask = ordered(CHUNK) >= 0
    reads = [(by_columns(a), by_pair(b)) for a, b in ((q_hbm, q_ref), (k_hbm, k_ref), (v_hbm, v_ref))]
    writes = [(by_pair(r_ref), by_pair(r_hbm)), (by_pair(d_ref), by_pair(d_hbm))]
    start(reads, read_sems, 0, pairs)

    @pl.loop(0, pairs)
    def _(p):
        wait(reads, read_sems, p)
        states = [jnp.zeros((BLK, BLK), f32)] * PAIR
        for i in range(steps):
            at = span(i, CHUNK)
            for j in range(PAIR):
                q, k = q_ref[p, at, span(j)], k_ref[p, at, span(j)]
                kt = k.T
                r = dot(lanes(*split(jnp.where(mask, dot(q, kt), 0.0))), rows(k, k))
                if i > 0:
                    r = r + dot(lanes(q, q), rows(*split(states[j])))
                if i + 1 < steps:
                    states[j] = states[j] + dot(kt, k)
                r_ref[p, j, at] = lanes(*split(r))
        for j in range(PAIR):
            d = dot(v_ref[p, :, span(j)].T, r_ref[p, j])
            d_ref[p, j] = d[:, :BLK] + d[:, BLK:]
        for copy in copies(writes, write_sems, p):
            copy.start()

    for p in range(pairs):
        wait(writes, write_sems, p)


def second_stage(p, q_ref, v_ref, r_ref, s_ref, states, store):
    tokens = q_ref.shape[1]
    steps = tokens // CHUNK
    mask = ordered(CHUNK) <= 0
    s_both = [rows(*split(s_ref[p * PAIR + j])) for j in range(PAIR)]
    for i in range(steps):
        at = span(i, CHUNK)
        for j in range(PAIR):
            q = q_ref[p, at, span(j)]
            qt, vt = q.T, v_ref[p, at, span(j)].T
            qt2 = rows(qt, qt)
            pair = r_ref[p, j, at].astype(f32)
            r = lanes(*split(pair[:, :BLK] + pair[:, BLK:] + dot(lanes(q, q), s_both[j])))
            num = dot(lanes(vt, vt), rows(*split(jnp.where(mask, dot(r, qt2), 0.0))))
            if states[j] is not None:
                num = num + dot(lanes(*split(states[j])), qt2)
            store(i, j, num)
            if i + 1 < steps:
                d = dot(vt, r)
                d = d[:, :BLK] + d[:, BLK:]
                states[j] = d if states[j] is None else states[j] + d


def early_kernel(
    q_hbm, v_hbm, r_hbm, s_ref, num_hbm, q_ref, v_ref, r_ref, num_ref, read_sems, write_sems
):
    pairs = q_ref.shape[0]
    reads = [(by_columns(q_hbm), by_pair(q_ref)), (by_pair(r_hbm), by_pair(r_ref)), (by_columns(v_hbm), by_pair(v_ref))]
    writes = [(by_pair(num_ref), by_pair(num_hbm))]
    start(reads, read_sems, 0, pairs)

    @pl.loop(0, pairs)
    def _(p):
        wait(reads, read_sems, p)

        def store(i, j, num):
            num_ref[p, span(j), span(i, CHUNK)] = num

        second_stage(p, q_ref, v_ref, r_ref, s_ref, [None] * PAIR, store)
        for copy in copies(writes, write_sems, p):
            copy.start()

    for p in range(pairs):
        wait(writes, write_sems, p)


def late_kernel(
    q_hbm, v_hbm, r_hbm, s_hbm, num_hbm, d_ref, gain_ref, scale_ref, y_hbm, part_ref,
    q_ref, v_ref, r_ref, s_ref, num_ref, y_ref, gains_ref, early_sems, late_sems, write_sems
):
    pairs = q_ref.shape[0]
    early = num_ref.shape[0]
    tokens = q_ref.shape[1]
    reads_early = [(by_columns(q_hbm), by_pair(q_ref)), (by_pair(num_hbm), by_pair(num_ref))]
    reads_late = [
        (by_columns(q_hbm), by_pair(q_ref)),
        (by_columns(v_hbm), by_pair(v_ref)),
        (by_pair(r_hbm), by_pair(r_ref)),
        (by_mats(s_hbm), by_mats(s_ref)),
    ]
    writes = [(by_pair(y_ref), by_pair(y_hbm))]
    start(reads_late, late_sems, early, pairs)
    start(reads_early, early_sems, 0, early)
    part_ref[...] = jnp.zeros_like(part_ref)
    for h in range(pairs * PAIR):
        gains_ref[h] = jnp.broadcast_to(gain_ref[h], (BLK, BLK)).T

    def finish(p, i, j, num):
        h = p * PAIR + j
        y = num * scale_ref[h]
        part_ref[:, span(i, CHUNK)] += jnp.sum((y * y).reshape(BLK // 8, 8, CHUNK), axis=0)
        y_ref[p, span(j), span(i, CHUNK)] = y * lanes(*[gains_ref[h]] * (CHUNK // BLK))

    @pl.loop(early, pairs)
    def _(p):
        wait(reads_late, late_sems, p)
        states = [d_ref[p * PAIR + j] for j in range(PAIR)]
        second_stage(p, q_ref, v_ref, r_ref, s_ref, states, functools.partial(finish, p))
        for copy in copies(writes, write_sems, p):
            copy.start()

    @pl.loop(0, early)
    def _(p):
        wait(reads_early, early_sems, p)
        for j in range(PAIR):
            before = lanes(*split(d_ref[p * PAIR + j]))
            for i in range(tokens // CHUNK):
                qt = q_ref[p, span(i, CHUNK), span(j)].T
                finish(p, i, j, num_ref[p, span(j), span(i, CHUNK)] + dot(before, rows(qt, qt)))
        for copy in copies(writes, write_sems, p):
            copy.start()

    for p in range(pairs):
        wait(writes, write_sems, p)


def owner_local_kernel(moments_ref, s_ref, c_ref, f_ref):
    members = moments_ref.shape[0]
    s = jnp.zeros((BLK, BLK), f32)
    c = jnp.zeros((BLK, BLK), f32)
    f = jnp.zeros((BLK, BLK), f32)
    for m in range(members):
        s_ref[m], c_ref[m], f_ref[m] = s, c, f
        c_own = moments_ref[m, BLK:]
        if m > 0:
            f = f + dot_f32(c_own, s)
        s = s + moments_ref[m, :BLK]
        c = c + c_own
    s_ref[members], c_ref[members], f_ref[members] = s, c, f


def owner_shift_kernel(s_ref, c_ref, f_ref, before_ref, back_ref, out_ref):
    members = back_ref.shape[0]
    before = before_ref[...]
    for m in range(members):
        back_ref[m] = s_ref[m] + before
    out_ref[0] = f_ref[0]
    for m in range(1, members + 1):
        out_ref[m] = f_ref[m] + dot_f32(c_ref[m], before)


def owner_sum_kernel(d_ref, h_ref, base_ref, total_ref):
    members = d_ref.shape[0]
    d = jnp.zeros((BLK, BLK), f32)
    for m in range(members):
        base_ref[m] = h_ref[m] + d
        d = d + d_ref[m]
    total_ref[...] = h_ref[members] + d


def add_kernel(base_ref, before_ref, out_ref):
    for m in range(out_ref.shape[0]):
        out_ref[m] = base_ref[m] + before_ref[...]


def norm_kernel(features, y_hbm, mine_ref, other_ref, out_hbm, y_ref, out_ref, read_sems, write_sems):
    pairs, wide, tokens = y_ref.shape
    steps = tokens // CHUNK

    def y_copy(i):
        at = span(i, CHUNK)
        return pltpu.make_async_copy(y_hbm.at[:, :, at], y_ref.at[:, :, at], read_sems.at[i])

    def out_copy(i):
        at = span(i, CHUNK)
        return pltpu.make_async_copy(out_ref.at[at], out_hbm.at[at], write_sems.at[i])

    for i in range(steps):
        y_copy(i).start()
    total = jnp.sum(mine_ref[...] + other_ref[...], axis=0, keepdims=True)
    inv = lax.rsqrt(total * (1.0 / features) + epsilon)
    for i in range(steps):
        at = span(i, CHUNK)
        y_copy(i).wait()
        for p in range(pairs):
            out_ref[at, span(p, wide)] = (y_ref[p, :, at] * inv[:, at]).astype(bf16).T
        out_copy(i).start()
    for i in range(steps):
        out_copy(i).wait()


def params(limit=SMALL):
    return pltpu.CompilerParams(vmem_limit_bytes=limit)


def cost(us, moved):
    return pl.CostEstimate(flops=int(us * 4e8), bytes_accessed=int(moved), transcendentals=0)


def per_device(query_rows, key_rows, value_rows, head_scale, out_gain):
    tokens, width = query_rows.shape
    heads = head_scale.shape[0]
    seq = lax.axis_size("seq")
    members = heads
    groups = seq // members
    index_groups = [[g * members + m for m in range(members)] for g in range(groups)]
    onward = [(i, i + members) for i in range(seq - members)]

    def swap(a):
        return lax.all_to_all(a, "seq", 0, 0, axis_index_groups=index_groups)

    mats = lambda n: jax.ShapeDtypeStruct((n, BLK, BLK), f32)
    mat = jax.ShapeDtypeStruct((BLK, BLK), f32)
    pairs = heads // PAIR
    early = pairs // 2
    shape = jax.ShapeDtypeStruct
    upright = shape((pairs, tokens, PAIR * BLK), bf16)
    turned_f32 = shape((pairs, PAIR * BLK, tokens), f32)
    twofold = shape((pairs, PAIR, tokens, 2 * BLK), bf16)
    pair_mats = shape((pairs, PAIR, BLK, BLK), f32)
    moment_mats = shape((pairs, PAIR, 2 * BLK, BLK), f32)
    anywhere = pl.BlockSpec(memory_space=pl.ANY)
    in_vmem = pl.BlockSpec(memory_space=pltpu.VMEM)
    in_smem = pl.BlockSpec(memory_space=pltpu.SMEM)

    def cut(a, n):
        return shape((n,) + a.shape[1:], a.dtype)

    def vmem(*arrays):
        return [pltpu.VMEM(a.shape, a.dtype) for a in arrays]

    def sems(*counts):
        return [pltpu.SemaphoreType.DMA((n, pairs)) for n in counts]

    moments = pl.pallas_call(
        moments_kernel,
        in_specs=[anywhere] * 3,
        out_specs=anywhere,
        out_shape=moment_mats,
        scratch_shapes=vmem(upright, upright, upright, moment_mats) + sems(3, 1),
        compiler_params=params(LARGE),
        name="moments",
    )(query_rows, key_rows, value_rows)
    moments_in = swap(moments.reshape(heads, 2 * BLK, BLK))

    r_local, d_local = pl.pallas_call(
        first_stage_kernel,
        in_specs=[anywhere] * 3,
        out_specs=[anywhere] * 2,
        out_shape=[twofold, pair_mats],
        scratch_shapes=vmem(upright, upright, upright, twofold, pair_mats) + sems(3, 2),
        compiler_params=params(LARGE),
        cost_estimate=cost(10, 10 * tokens * width),
        name="first_stage",
    )(query_rows, key_rows, value_rows)
    d_in = swap(d_local.reshape(heads, BLK, BLK))

    s_part, c_part, f_part = pl.pallas_call(
        owner_local_kernel,
        out_shape=[mats(members + 1)] * 3,
        compiler_params=params(),
        name="owner_local",
    )(moments_in)
    s_before = jnp.zeros((BLK, BLK), f32)
    for _ in range(groups - 1):
        s_before = lax.ppermute(s_before + s_part[members], "seq", onward)
    s_back, h_part = pl.pallas_call(
        owner_shift_kernel,
        out_shape=[mats(members), mats(members + 1)],
        compiler_params=params(),
        name="owner_shift",
    )(s_part, c_part, f_part, s_before)
    s_pre = swap(s_back)

    d_base, d_total = pl.pallas_call(
        owner_sum_kernel,
        out_shape=[mats(members), mat],
        compiler_params=params(),
        name="owner_sum",
    )(d_in, h_part)
    d_before = jnp.zeros((BLK, BLK), f32)
    for _ in range(groups - 1):
        d_before = lax.ppermute(d_before + d_total, "seq", onward)
    d_back = pl.pallas_call(
        add_kernel, out_shape=mats(members), compiler_params=params(), name="owner_add"
    )(d_base, d_before)
    d_pre = swap(d_back)

    num = pl.pallas_call(
        early_kernel,
        in_specs=[anywhere] * 3 + [in_vmem],
        out_specs=anywhere,
        out_shape=cut(turned_f32, early),
        scratch_shapes=vmem(*[cut(a, early) for a in (upright, upright, twofold, turned_f32)]) + sems(3, 1),
        compiler_params=params(LARGE),
        cost_estimate=cost(6, 6 * tokens * width),
        name="second_early",
    )(query_rows, value_rows, r_local, s_pre)

    part_shape = shape((8, tokens), f32)
    y, part = pl.pallas_call(
        late_kernel,
        in_specs=[anywhere] * 5 + [in_vmem, in_vmem, in_smem],
        out_specs=[anywhere, in_vmem],
        out_shape=[turned_f32, part_shape],
        scratch_shapes=vmem(
            upright, upright, twofold, mats(heads), cut(turned_f32, early), turned_f32, mats(heads)
        )
        + sems(2, 4, 1),
        compiler_params=params(LATE),
        name="second_late",
    )(query_rows, value_rows, r_local, s_pre, num, d_pre, out_gain.reshape(heads, 1, BLK), head_scale)
    shards = lax.axis_size("head")
    other = jnp.zeros_like(part)
    for turn in range(1, shards):
        other = other + lax.ppermute(part, "head", [(i, (i + turn) % shards) for i in range(shards)])
    return pl.pallas_call(
        functools.partial(norm_kernel, width * shards),
        in_specs=[anywhere, in_vmem, in_vmem],
        out_specs=anywhere,
        out_shape=shape((tokens, width), bf16),
        scratch_shapes=vmem(turned_f32, shape((tokens, width), bf16))
        + [pltpu.SemaphoreType.DMA((tokens // CHUNK,))] * 2,
        compiler_params=params(LAST),
        name="norm",
    )(y, part, other)


def solution(mesh):
    return jax.shard_map(
        per_device,
        mesh=mesh,
        in_specs=(P("seq", "head"), P("seq", "head"), P("seq", "head"), P("head"), P("head")),
        out_specs=P("seq", "head"),
        check_vma=False,
    )
```

```python
import functools

import jax
import jax.numpy as jnp
from jax import lax
from jax.experimental import pallas as pl
from jax.experimental.pallas import tpu as pltpu
from jax.sharding import PartitionSpec as P

BLK = 128
CHUNK = 256
PAIR = 2
SMALL = 8 * 1024 * 1024
LARGE = 60 * 1024 * 1024
LATE = 52 * 1024 * 1024
LAST = 52 * 1024 * 1024

epsilon = 1e-06
f32, bf16 = jnp.float32, jnp.bfloat16

NN = (((1,), (0,)), ((), ()))
NT = (((1,), (1,)), ((), ()))
TN = (((0,), (0,)), ((), ()))


def dot(a, b, dims=NN):
    return lax.dot_general(a, b, dims, preferred_element_type=f32)


def split(a):
    high = a.astype(bf16)
    return high, (a - high.astype(f32)).astype(bf16)


def lanes(*parts):
    return jnp.concatenate(parts, axis=1)


def rows(*parts):
    return jnp.concatenate(parts, axis=0)


def dot_f32(a, b):
    a_high, a_low = split(a)
    b_high, b_low = split(b)
    return dot(lanes(a_high, a_low), rows(b_high, b_high)) + dot(a_high, b_low)


def ordered(size):
    shape = (size, size)
    return lax.broadcasted_iota(jnp.int32, shape, 0) - lax.broadcasted_iota(jnp.int32, shape, 1)


def span(j, size=BLK):
    return slice(j * size, (j + 1) * size)


def columns(p):
    return pl.ds(pl.multiple_of(p * PAIR * BLK, PAIR * BLK), PAIR * BLK)


def copies(moves, sems, p):
    return [
        pltpu.make_async_copy(source(p), target(p), sems.at[n, p])
        for n, (source, target) in enumerate(moves)
    ]


def start(moves, sems, first, last):
    for p in range(first, last):
        for copy in copies(moves, sems, p):
            copy.start()


def wait(moves, sems, p):
    for copy in copies(moves, sems, p):
        copy.wait()


def by_columns(hbm):
    return lambda p: hbm.at[:, columns(p)]


def by_pair(ref):
    return lambda p: ref.at[p]


def by_mats(ref):
    return lambda p: ref.at[pl.ds(p * PAIR, PAIR)]


def moments_kernel(q_hbm, k_hbm, v_hbm, m_hbm, q_ref, k_ref, v_ref, m_ref, read_sems, write_sems):
    pairs = q_ref.shape[0]
    reads = [(by_columns(a), by_pair(b)) for a, b in ((k_hbm, k_ref), (v_hbm, v_ref), (q_hbm, q_ref))]
    writes = [(by_pair(m_ref), by_pair(m_hbm))]
    start(reads, read_sems, 0, pairs)
    for p in range(pairs):
        wait(reads, read_sems, p)
        for j in range(PAIR):
            k = k_ref[p, :, span(j)]
            m_ref[p, j, :BLK] = dot(k.T, k)
            m_ref[p, j, BLK:] = dot(v_ref[p, :, span(j)].T, q_ref[p, :, span(j)])
        start(writes, write_sems, p, p + 1)
    for p in range(pairs):
        wait(writes, write_sems, p)


def running(parts, first=None):
    totals = [first]
    for part in parts:
        totals.append(part if totals[-1] is None else totals[-1] + part)
    return totals


def halves_sum(a):
    return a[:, :BLK] + a[:, BLK:]


def chunk_units(tokens):
    return [(i, j, span(i, CHUNK), span(j)) for i in range(tokens // CHUNK) for j in range(PAIR)]


def first_stage_kernel(
    q_hbm, k_hbm, v_hbm, r_hbm, d_hbm, q_ref, k_ref, v_ref, r_ref, d_ref, a_ref, read_sems, write_sems
):
    pairs, tokens, _ = q_ref.shape
    steps = tokens // CHUNK
    units = chunk_units(tokens)
    mask = ordered(CHUNK) <= 0
    reads = [(by_columns(a), by_pair(b)) for a, b in ((q_hbm, q_ref), (k_hbm, k_ref), (v_hbm, v_ref))]
    writes = [(by_pair(r_ref), by_pair(r_hbm)), (by_pair(d_ref), by_pair(d_hbm))]
    start(reads, read_sems, 0, pairs)

    @pl.loop(0, pairs)
    def _(p):
        wait(reads, read_sems, p)
        for i, j, at, cols in units:
            a = dot(k_ref[p, at, cols], q_ref[p, at, cols].T)
            a_ref[j, i] = rows(*split(jnp.where(mask, a, 0.0)))
        states = []
        for j in range(PAIR):
            blocks = [k_ref[p, span(i, CHUNK), span(j)] for i in range(steps - 1)]
            states.append(running([dot(k.T, k) for k in blocks]))
        for i, j, at, cols in units:
            kt = k_ref[p, at, cols].T
            r = dot(lanes(kt, kt), a_ref[j, i])
            if i > 0:
                qt = q_ref[p, at, cols].T
                r = r + dot(lanes(*split(states[j][i])), rows(qt, qt))
            r_high, r_low = split(r)
            r_ref[p, j, at] = lanes(r_high.T, r_low.T)
        for j in range(PAIR):
            d_ref[p, j] = halves_sum(dot(v_ref[p, :, span(j)].T, r_ref[p, j]))
        for copy in copies(writes, write_sems, p):
            copy.start()

    for p in range(pairs):
        wait(writes, write_sems, p)


def second_stage(p, q_ref, v_ref, r_ref, s_ref, a_ref, first, store):
    tokens = q_ref.shape[1]
    steps = tokens // CHUNK
    units = chunk_units(tokens)
    mask = ordered(CHUNK) <= 0
    s_both = [rows(*split(s_ref[p * PAIR + j])) for j in range(PAIR)]
    for j in range(PAIR):
        for i in range(steps):
            at = span(i, CHUNK)
            q = q_ref[p, at, span(j)]
            r = halves_sum(r_ref[p, j, at].astype(f32)) + dot(lanes(q, q), s_both[j])
            r_ref[p, j, at] = lanes(*split(r))
    for i, j, at, cols in units:
        qt = q_ref[p, at, cols].T
        a = dot(r_ref[p, j, at], rows(qt, qt))
        a_ref[j, i] = rows(*split(jnp.where(mask, a, 0.0)))
    sums = [[] for _ in range(PAIR)]
    for i, j, at, cols in units:
        if i + 1 < steps:
            sums[j].append(halves_sum(dot(v_ref[p, at, cols].T, r_ref[p, j, at])))
    states = [running(sums[j], first[j]) for j in range(PAIR)]
    for i, j, at, cols in units:
        vt = v_ref[p, at, cols].T
        num = dot(lanes(vt, vt), a_ref[j, i])
        if states[j][i] is not None:
            qt = q_ref[p, at, cols].T
            num = num + dot(lanes(*split(states[j][i])), rows(qt, qt))
        store(i, j, num)


def early_kernel(
    q_hbm, v_hbm, r_hbm, s_ref, num_hbm, q_ref, v_ref, r_ref, num_ref, a_ref, read_sems, write_sems
):
    pairs = q_ref.shape[0]
    reads = [(by_columns(q_hbm), by_pair(q_ref)), (by_pair(r_hbm), by_pair(r_ref)), (by_columns(v_hbm), by_pair(v_ref))]
    writes = [(by_pair(num_ref), by_pair(num_hbm))]
    start(reads, read_sems, 0, pairs)

    @pl.loop(0, pairs)
    def _(p):
        wait(reads, read_sems, p)

        def store(i, j, num):
            num_ref[p, span(j), span(i, CHUNK)] = num

        second_stage(p, q_ref, v_ref, r_ref, s_ref, a_ref, [None] * PAIR, store)
        for copy in copies(writes, write_sems, p):
            copy.start()

    for p in range(pairs):
        wait(writes, write_sems, p)


def late_kernel(
    q_hbm, v_hbm, r_hbm, s_hbm, num_hbm, d_ref, gain_ref, scale_ref, y_hbm, part_ref,
    q_ref, v_ref, r_ref, s_ref, num_ref, y_ref, gains_ref, a_ref, early_sems, late_sems, write_sems
):
    pairs = q_ref.shape[0]
    early = num_ref.shape[0]
    tokens = q_ref.shape[1]
    reads_early = [(by_columns(q_hbm), by_pair(q_ref)), (by_pair(num_hbm), by_pair(num_ref))]
    reads_late = [
        (by_columns(q_hbm), by_pair(q_ref)),
        (by_columns(v_hbm), by_pair(v_ref)),
        (by_pair(r_hbm), by_pair(r_ref)),
        (by_mats(s_hbm), by_mats(s_ref)),
    ]
    writes = [(by_pair(y_ref), by_pair(y_hbm))]
    start(reads_late, late_sems, early, pairs)
    start(reads_early, early_sems, 0, early)
    part_ref[...] = jnp.zeros_like(part_ref)
    for h in range(pairs * PAIR):
        gains_ref[h] = jnp.broadcast_to(gain_ref[h], (BLK, BLK)).T

    def finish(p, i, j, num):
        h = p * PAIR + j
        y = num * scale_ref[h]
        part_ref[:, span(i, CHUNK)] += jnp.sum((y * y).reshape(BLK // 8, 8, CHUNK), axis=0)
        y_ref[p, span(j), span(i, CHUNK)] = y * lanes(*[gains_ref[h]] * (CHUNK // BLK))

    @pl.loop(early, pairs)
    def _(p):
        wait(reads_late, late_sems, p)
        states = [d_ref[p * PAIR + j] for j in range(PAIR)]
        second_stage(p, q_ref, v_ref, r_ref, s_ref, a_ref, states, functools.partial(finish, p))
        for copy in copies(writes, write_sems, p):
            copy.start()

    @pl.loop(0, early)
    def _(p):
        wait(reads_early, early_sems, p)
        for j in range(PAIR):
            before = lanes(*split(d_ref[p * PAIR + j]))
            for i in range(tokens // CHUNK):
                qt = q_ref[p, span(i, CHUNK), span(j)].T
                finish(p, i, j, num_ref[p, span(j), span(i, CHUNK)] + dot(before, rows(qt, qt)))
        for copy in copies(writes, write_sems, p):
            copy.start()

    for p in range(pairs):
        wait(writes, write_sems, p)


def owner_local_kernel(moments_ref, s_ref, c_ref, f_ref):
    members = moments_ref.shape[0]
    s = jnp.zeros((BLK, BLK), f32)
    c = jnp.zeros((BLK, BLK), f32)
    f = jnp.zeros((BLK, BLK), f32)
    for m in range(members):
        s_ref[m], c_ref[m], f_ref[m] = s, c, f
        c_own = moments_ref[m, BLK:]
        if m > 0:
            f = f + dot_f32(c_own, s)
        s = s + moments_ref[m, :BLK]
        c = c + c_own
    s_ref[members], c_ref[members], f_ref[members] = s, c, f


def owner_shift_kernel(s_ref, c_ref, f_ref, before_ref, back_ref, out_ref):
    members = back_ref.shape[0]
    before = before_ref[...]
    for m in range(members):
        back_ref[m] = s_ref[m] + before
    out_ref[0] = f_ref[0]
    for m in range(1, members + 1):
        out_ref[m] = f_ref[m] + dot_f32(c_ref[m], before)


def owner_sum_kernel(d_ref, h_ref, base_ref, total_ref):
    members = d_ref.shape[0]
    d = jnp.zeros((BLK, BLK), f32)
    for m in range(members):
        base_ref[m] = h_ref[m] + d
        d = d + d_ref[m]
    total_ref[...] = h_ref[members] + d


def add_kernel(base_ref, before_ref, out_ref):
    for m in range(out_ref.shape[0]):
        out_ref[m] = base_ref[m] + before_ref[...]


def norm_kernel(features, y_hbm, mine_ref, other_ref, out_hbm, y_ref, out_ref, read_sems, write_sems):
    pairs, wide, tokens = y_ref.shape
    steps = tokens // CHUNK

    def y_copy(i):
        at = span(i, CHUNK)
        return pltpu.make_async_copy(y_hbm.at[:, :, at], y_ref.at[:, :, at], read_sems.at[i])

    def out_copy(i):
        at = span(i, CHUNK)
        return pltpu.make_async_copy(out_ref.at[at], out_hbm.at[at], write_sems.at[i])

    for i in range(steps):
        y_copy(i).start()
    total = jnp.sum(mine_ref[...] + other_ref[...], axis=0, keepdims=True)
    inv = lax.rsqrt(total * (1.0 / features) + epsilon)
    for i in range(steps):
        at = span(i, CHUNK)
        y_copy(i).wait()
        for p in range(pairs):
            out_ref[at, span(p, wide)] = (y_ref[p, :, at] * inv[:, at]).astype(bf16).T
        out_copy(i).start()
    for i in range(steps):
        out_copy(i).wait()


def params(limit=SMALL):
    return pltpu.CompilerParams(vmem_limit_bytes=limit)


def cost(us, moved):
    return pl.CostEstimate(flops=int(us * 4e8), bytes_accessed=int(moved), transcendentals=0)


def per_device(query_rows, key_rows, value_rows, head_scale, out_gain):
    tokens, width = query_rows.shape
    heads = head_scale.shape[0]
    seq = lax.axis_size("seq")
    members = heads
    groups = seq // members
    index_groups = [[g * members + m for m in range(members)] for g in range(groups)]
    onward = [(i, i + members) for i in range(seq - members)]

    def swap(a):
        return lax.all_to_all(a, "seq", 0, 0, axis_index_groups=index_groups)

    mats = lambda n: jax.ShapeDtypeStruct((n, BLK, BLK), f32)
    mat = jax.ShapeDtypeStruct((BLK, BLK), f32)
    pairs = heads // PAIR
    early = pairs // 2
    shape = jax.ShapeDtypeStruct
    upright = shape((pairs, tokens, PAIR * BLK), bf16)
    turned_f32 = shape((pairs, PAIR * BLK, tokens), f32)
    twofold = shape((pairs, PAIR, tokens, 2 * BLK), bf16)
    pair_mats = shape((pairs, PAIR, BLK, BLK), f32)
    scores = shape((PAIR, tokens // CHUNK, 2 * CHUNK, CHUNK), bf16)
    moment_mats = shape((pairs, PAIR, 2 * BLK, BLK), f32)
    anywhere = pl.BlockSpec(memory_space=pl.ANY)
    in_vmem = pl.BlockSpec(memory_space=pltpu.VMEM)
    in_smem = pl.BlockSpec(memory_space=pltpu.SMEM)

    def cut(a, n):
        return shape((n,) + a.shape[1:], a.dtype)

    def vmem(*arrays):
        return [pltpu.VMEM(a.shape, a.dtype) for a in arrays]

    def sems(*counts):
        return [pltpu.SemaphoreType.DMA((n, pairs)) for n in counts]

    moments = pl.pallas_call(
        moments_kernel,
        in_specs=[anywhere] * 3,
        out_specs=anywhere,
        out_shape=moment_mats,
        scratch_shapes=vmem(upright, upright, upright, moment_mats) + sems(3, 1),
        compiler_params=params(LARGE),
        name="moments",
    )(query_rows, key_rows, value_rows)
    moments_in = swap(moments.reshape(heads, 2 * BLK, BLK))

    r_local, d_local = pl.pallas_call(
        first_stage_kernel,
        in_specs=[anywhere] * 3,
        out_specs=[anywhere] * 2,
        out_shape=[twofold, pair_mats],
        scratch_shapes=vmem(upright, upright, upright, twofold, pair_mats, scores) + sems(3, 2),
        compiler_params=params(LARGE),
        cost_estimate=cost(10, 10 * tokens * width),
        name="first_stage",
    )(query_rows, key_rows, value_rows)
    d_in = swap(d_local.reshape(heads, BLK, BLK))

    s_part, c_part, f_part = pl.pallas_call(
        owner_local_kernel,
        out_shape=[mats(members + 1)] * 3,
        compiler_params=params(),
        name="owner_local",
    )(moments_in)
    s_before = jnp.zeros((BLK, BLK), f32)
    for _ in range(groups - 1):
        s_before = lax.ppermute(s_before + s_part[members], "seq", onward)
    s_back, h_part = pl.pallas_call(
        owner_shift_kernel,
        out_shape=[mats(members), mats(members + 1)],
        compiler_params=params(),
        name="owner_shift",
    )(s_part, c_part, f_part, s_before)
    s_pre = swap(s_back)

    d_base, d_total = pl.pallas_call(
        owner_sum_kernel,
        out_shape=[mats(members), mat],
        compiler_params=params(),
        name="owner_sum",
    )(d_in, h_part)
    d_before = jnp.zeros((BLK, BLK), f32)
    for _ in range(groups - 1):
        d_before = lax.ppermute(d_before + d_total, "seq", onward)
    d_back = pl.pallas_call(
        add_kernel, out_shape=mats(members), compiler_params=params(), name="owner_add"
    )(d_base, d_before)
    d_pre = swap(d_back)

    num = pl.pallas_call(
        early_kernel,
        in_specs=[anywhere] * 3 + [in_vmem],
        out_specs=anywhere,
        out_shape=cut(turned_f32, early),
        scratch_shapes=vmem(*[cut(a, early) for a in (upright, upright, twofold, turned_f32)], scores) + sems(3, 1),
        compiler_params=params(LARGE),
        cost_estimate=cost(6, 6 * tokens * width),
        name="second_early",
    )(query_rows, value_rows, r_local, s_pre)

    part_shape = shape((8, tokens), f32)
    y, part = pl.pallas_call(
        late_kernel,
        in_specs=[anywhere] * 5 + [in_vmem, in_vmem, in_smem],
        out_specs=[anywhere, in_vmem],
        out_shape=[turned_f32, part_shape],
        scratch_shapes=vmem(
            upright, upright, twofold, mats(heads), cut(turned_f32, early), turned_f32, mats(heads), scores
        )
        + sems(2, 4, 1),
        compiler_params=params(LATE),
        name="second_late",
    )(query_rows, value_rows, r_local, s_pre, num, d_pre, out_gain.reshape(heads, 1, BLK), head_scale)
    shards = lax.axis_size("head")
    other = jnp.zeros_like(part)
    for turn in range(1, shards):
        other = other + lax.ppermute(part, "head", [(i, (i + turn) % shards) for i in range(shards)])
    return pl.pallas_call(
        functools.partial(norm_kernel, width * shards),
        in_specs=[anywhere, in_vmem, in_vmem],
        out_specs=anywhere,
        out_shape=shape((tokens, width), bf16),
        scratch_shapes=vmem(turned_f32, shape((tokens, width), bf16))
        + [pltpu.SemaphoreType.DMA((tokens // CHUNK,))] * 2,
        compiler_params=params(LAST),
        name="norm",
    )(y, part, other)


def solution(mesh):
    return jax.shard_map(
        per_device,
        mesh=mesh,
        in_specs=(P("seq", "head"), P("seq", "head"), P("seq", "head"), P("head"), P("head")),
        out_specs=P("seq", "head"),
        check_vma=False,
    )
```

```python
import functools

import jax
import jax.numpy as jnp
from jax import lax
from jax.experimental import pallas as pl
from jax.experimental.pallas import tpu as pltpu
from jax.sharding import PartitionSpec as P

BLK = 128
CHUNK = 256
PAIR = 2
HALF = BLK // 2
PACKED = HALF + 8
SMALL = 8 * 1024 * 1024
LARGE = 60 * 1024 * 1024
LATE = 52 * 1024 * 1024
LAST = 52 * 1024 * 1024

epsilon = 1e-06
f32, bf16 = jnp.float32, jnp.bfloat16

NN = (((1,), (0,)), ((), ()))
NT = (((1,), (1,)), ((), ()))
TN = (((0,), (0,)), ((), ()))


def dot(a, b, dims=NN):
    return lax.dot_general(a, b, dims, preferred_element_type=f32)


def split(a):
    high = a.astype(bf16)
    return high, (a - high.astype(f32)).astype(bf16)


def lanes(*parts):
    return jnp.concatenate(parts, axis=1)


def rows(*parts):
    return jnp.concatenate(parts, axis=0)


def dot_f32(a, b):
    a_high, a_low = split(a)
    b_high, b_low = split(b)
    return dot(lanes(a_high, a_low), rows(b_high, b_high)) + dot(a_high, b_low)


def ordered(size):
    shape = (size, size)
    return lax.broadcasted_iota(jnp.int32, shape, 0) - lax.broadcasted_iota(jnp.int32, shape, 1)


def span(j, size=BLK):
    return slice(j * size, (j + 1) * size)


def half_indices():
    shape = (HALF, BLK)
    return lax.broadcasted_iota(jnp.int32, shape, 0), lax.broadcasted_iota(jnp.int32, shape, 1)


def pack(s):
    row, lane = half_indices()
    corner = pltpu.roll(s[HALF:], HALF, 1)
    diagonal = jnp.sum(jnp.where(lane == row, corner, 0.0), axis=0, keepdims=True)
    return rows(jnp.where(lane >= row, s[:HALF], corner), jnp.broadcast_to(diagonal, (8, BLK)))


def unpack(packed):
    row, lane = half_indices()
    top, diagonal = packed[:HALF], packed[HALF : HALF + 1]
    flipped = rows(top, jnp.zeros_like(top)).T
    corner = jnp.where(lane < row, top, jnp.where(lane == row, diagonal, flipped[:HALF]))
    return rows(
        jnp.where(lane >= row, top, flipped[:HALF]),
        jnp.where(lane < HALF, flipped[HALF:], pltpu.roll(corner, HALF, 1)),
    )


def columns(p):
    return pl.ds(pl.multiple_of(p * PAIR * BLK, PAIR * BLK), PAIR * BLK)


def copies(moves, sems, p):
    return [
        pltpu.make_async_copy(source(p), target(p), sems.at[n, p])
        for n, (source, target) in enumerate(moves)
    ]


def start(moves, sems, first, last):
    for p in range(first, last):
        for copy in copies(moves, sems, p):
            copy.start()


def wait(moves, sems, p):
    for copy in copies(moves, sems, p):
        copy.wait()


def by_columns(hbm):
    return lambda p: hbm.at[:, columns(p)]


def by_pair(ref):
    return lambda p: ref.at[p]


def moments_kernel(q_hbm, k_hbm, v_hbm, m_hbm, q_ref, k_ref, v_ref, m_ref, read_sems, write_sems):
    pairs = q_ref.shape[0]
    reads = [(by_columns(a), by_pair(b)) for a, b in ((k_hbm, k_ref), (v_hbm, v_ref), (q_hbm, q_ref))]
    writes = [(by_pair(m_ref), by_pair(m_hbm))]
    start(reads, read_sems, 0, pairs)
    for p in range(pairs):
        wait(reads, read_sems, p)
        for j in range(PAIR):
            k = k_ref[p, :, span(j)]
            m_ref[p, j, :PACKED] = pack(dot(k.T, k))
            m_ref[p, j, PACKED:] = dot(v_ref[p, :, span(j)].T, q_ref[p, :, span(j)])
        start(writes, write_sems, p, p + 1)
    for p in range(pairs):
        wait(writes, write_sems, p)


def running(parts, first=None):
    totals = [first]
    for part in parts:
        totals.append(part if totals[-1] is None else totals[-1] + part)
    return totals


def halves_sum(a):
    return a[:, :BLK] + a[:, BLK:]


def chunk_units(tokens):
    return [(i, j, span(i, CHUNK), span(j)) for i in range(tokens // CHUNK) for j in range(PAIR)]


def first_stage_kernel(
    q_hbm, k_hbm, v_hbm, r_hbm, d_hbm, q_ref, k_ref, v_ref, r_ref, d_ref, a_ref, read_sems, write_sems
):
    pairs, tokens, _ = q_ref.shape
    steps = tokens // CHUNK
    units = chunk_units(tokens)
    mask = ordered(CHUNK) <= 0
    reads = [(by_columns(a), by_pair(b)) for a, b in ((q_hbm, q_ref), (k_hbm, k_ref), (v_hbm, v_ref))]
    writes = [(by_pair(r_ref), by_pair(r_hbm)), (by_pair(d_ref), by_pair(d_hbm))]
    start(reads, read_sems, 0, pairs)

    @pl.loop(0, pairs)
    def _(p):
        wait(reads, read_sems, p)
        for i, j, at, cols in units:
            a = dot(k_ref[p, at, cols], q_ref[p, at, cols].T)
            a_ref[j, i] = rows(*split(jnp.where(mask, a, 0.0)))
        states = []
        for j in range(PAIR):
            blocks = [k_ref[p, span(i, CHUNK), span(j)] for i in range(steps - 1)]
            states.append(running([dot(k.T, k) for k in blocks]))
        for i, j, at, cols in units:
            kt = k_ref[p, at, cols].T
            r = dot(lanes(kt, kt), a_ref[j, i])
            if i > 0:
                qt = q_ref[p, at, cols].T
                r = r + dot(lanes(*split(states[j][i])), rows(qt, qt))
            r_high, r_low = split(r)
            r_ref[p, j, at] = lanes(r_high.T, r_low.T)
        for j in range(PAIR):
            d_ref[p, j] = halves_sum(dot(v_ref[p, :, span(j)].T, r_ref[p, j]))
        for copy in copies(writes, write_sems, p):
            copy.start()

    for p in range(pairs):
        wait(writes, write_sems, p)


def second_stage(p, q_ref, v_ref, r_ref, s_both, a_ref, first, store):
    tokens = q_ref.shape[1]
    steps = tokens // CHUNK
    units = chunk_units(tokens)
    mask = ordered(CHUNK) <= 0
    for j in range(PAIR):
        for i in range(steps):
            at = span(i, CHUNK)
            q = q_ref[p, at, span(j)]
            r = halves_sum(r_ref[p, j, at].astype(f32)) + dot(lanes(q, q), s_both[j])
            r_ref[p, j, at] = lanes(*split(r))
    for i, j, at, cols in units:
        qt = q_ref[p, at, cols].T
        a = dot(r_ref[p, j, at], rows(qt, qt))
        a_ref[j, i] = rows(*split(jnp.where(mask, a, 0.0)))
    sums = [[] for _ in range(PAIR)]
    for i, j, at, cols in units:
        if i + 1 < steps:
            sums[j].append(halves_sum(dot(v_ref[p, at, cols].T, r_ref[p, j, at])))
    states = [running(sums[j], first[j]) for j in range(PAIR)]
    for i, j, at, cols in units:
        vt = v_ref[p, at, cols].T
        qt = q_ref[p, at, cols].T
        num = dot(lanes(vt, vt), a_ref[j, i]) + dot(lanes(*split(states[j][i])), rows(qt, qt))
        store(i, j, num)


def second_stage_kernel(
    q_hbm, v_hbm, r_hbm, back_ref, gain_ref, scale_ref, y_hbm, part_ref,
    q_ref, v_ref, r_ref, y_ref, gains_ref, a_ref, read_sems, write_sems
):
    pairs = q_ref.shape[0]
    reads = [(by_columns(q_hbm), by_pair(q_ref)), (by_pair(r_hbm), by_pair(r_ref)), (by_columns(v_hbm), by_pair(v_ref))]
    writes = [(by_pair(y_ref), by_pair(y_hbm))]
    start(reads, read_sems, 0, pairs)
    part_ref[...] = jnp.zeros_like(part_ref)
    for h in range(pairs * PAIR):
        gains_ref[h] = jnp.broadcast_to(gain_ref[h], (BLK, BLK)).T

    @pl.loop(0, pairs)
    def _(p):
        def finish(i, j, num):
            h = p * PAIR + j
            y = num * scale_ref[h]
            part_ref[:, span(i, CHUNK)] += jnp.sum((y * y).reshape(BLK // 8, 8, CHUNK), axis=0)
            y_ref[p, span(j), span(i, CHUNK)] = y * lanes(*[gains_ref[h]] * (CHUNK // BLK))

        backs = [back_ref[p * PAIR + j] for j in range(PAIR)]
        s_both = [rows(*split(unpack(back[:PACKED]))) for back in backs]
        wait(reads, read_sems, p)
        second_stage(p, q_ref, v_ref, r_ref, s_both, a_ref, [back[PACKED:] for back in backs], finish)
        for copy in copies(writes, write_sems, p):
            copy.start()

    for p in range(pairs):
        wait(writes, write_sems, p)


def owner_local_kernel(moments_ref, s_ref, c_ref, f_ref):
    members = moments_ref.shape[0]
    s = jnp.zeros((BLK, BLK), f32)
    c = jnp.zeros((BLK, BLK), f32)
    f = jnp.zeros((BLK, BLK), f32)
    for m in range(members):
        s_ref[m], c_ref[m], f_ref[m] = s, c, f
        c_own = moments_ref[m, PACKED:]
        if m > 0:
            f = f + dot_f32(c_own, s)
        s = s + unpack(moments_ref[m, :PACKED])
        c = c + c_own
    s_ref[members], c_ref[members], f_ref[members] = s, c, f


def owner_sum_kernel(d_ref, s_ref, f_ref, base_ref, total_ref):
    members = d_ref.shape[0]
    d = jnp.zeros((BLK, BLK), f32)
    for m in range(members):
        base_ref[m] = f_ref[m] + d
        d = d + d_ref[m]
    total_ref[:BLK] = s_ref[members]
    total_ref[BLK:] = f_ref[members] + d


def owner_back_kernel(s_ref, c_ref, base_ref, before_ref, back_ref):
    s_before, d_before = before_ref[:BLK], before_ref[BLK:]
    for m in range(back_ref.shape[0]):
        back_ref[m, :PACKED] = pack(s_ref[m] + s_before)
        d = base_ref[m] + d_before
        back_ref[m, PACKED:] = d if m == 0 else d + dot_f32(c_ref[m], s_before)


def norm_kernel(features, y_hbm, mine_ref, other_ref, out_hbm, y_ref, out_ref, read_sems, write_sems):
    pairs, wide, tokens = y_ref.shape
    steps = tokens // CHUNK

    def y_copy(i):
        at = span(i, CHUNK)
        return pltpu.make_async_copy(y_hbm.at[:, :, at], y_ref.at[:, :, at], read_sems.at[i])

    def out_copy(i):
        at = span(i, CHUNK)
        return pltpu.make_async_copy(out_ref.at[at], out_hbm.at[at], write_sems.at[i])

    for i in range(steps):
        y_copy(i).start()
    total = jnp.sum(mine_ref[...] + other_ref[...], axis=0, keepdims=True)
    inv = lax.rsqrt(total * (1.0 / features) + epsilon)
    for i in range(steps):
        at = span(i, CHUNK)
        y_copy(i).wait()
        for p in range(pairs):
            out_ref[at, span(p, wide)] = (y_ref[p, :, at] * inv[:, at]).astype(bf16).T
        out_copy(i).start()
    for i in range(steps):
        out_copy(i).wait()


def params(limit=SMALL):
    return pltpu.CompilerParams(vmem_limit_bytes=limit)


def cost(us, moved):
    return pl.CostEstimate(flops=int(us * 4e8), bytes_accessed=int(moved), transcendentals=0)


def per_device(query_rows, key_rows, value_rows, head_scale, out_gain):
    tokens, width = query_rows.shape
    heads = head_scale.shape[0]
    seq = lax.axis_size("seq")
    members = heads
    groups = seq // members
    index_groups = [[g * members + m for m in range(members)] for g in range(groups)]
    onward = [(i, i + members) for i in range(seq - members)]

    def swap(a):
        return lax.all_to_all(a, "seq", 0, 0, axis_index_groups=index_groups)

    mats = lambda n: jax.ShapeDtypeStruct((n, BLK, BLK), f32)
    pairs = heads // PAIR
    shape = jax.ShapeDtypeStruct
    upright = shape((pairs, tokens, PAIR * BLK), bf16)
    turned_f32 = shape((pairs, PAIR * BLK, tokens), f32)
    twofold = shape((pairs, PAIR, tokens, 2 * BLK), bf16)
    pair_mats = shape((pairs, PAIR, BLK, BLK), f32)
    scores = shape((PAIR, tokens // CHUNK, 2 * CHUNK, CHUNK), bf16)
    moment_mats = shape((pairs, PAIR, PACKED + BLK, BLK), f32)
    anywhere = pl.BlockSpec(memory_space=pl.ANY)
    in_vmem = pl.BlockSpec(memory_space=pltpu.VMEM)
    in_smem = pl.BlockSpec(memory_space=pltpu.SMEM)

    def vmem(*arrays):
        return [pltpu.VMEM(a.shape, a.dtype) for a in arrays]

    def sems(*counts):
        return [pltpu.SemaphoreType.DMA((n, pairs)) for n in counts]

    moments = pl.pallas_call(
        moments_kernel,
        in_specs=[anywhere] * 3,
        out_specs=anywhere,
        out_shape=moment_mats,
        scratch_shapes=vmem(upright, upright, upright, moment_mats) + sems(3, 1),
        compiler_params=params(LARGE),
        name="moments",
    )(query_rows, key_rows, value_rows)
    moments_in = swap(moments.reshape(heads, PACKED + BLK, BLK))

    r_local, d_local = pl.pallas_call(
        first_stage_kernel,
        in_specs=[anywhere] * 3,
        out_specs=[anywhere] * 2,
        out_shape=[twofold, pair_mats],
        scratch_shapes=vmem(upright, upright, upright, twofold, pair_mats, scores) + sems(3, 2),
        compiler_params=params(LARGE),
        cost_estimate=cost(10, 10 * tokens * width),
        name="first_stage",
    )(query_rows, key_rows, value_rows)
    d_in = swap(d_local.reshape(heads, BLK, BLK))

    s_part, c_part, f_part = pl.pallas_call(
        owner_local_kernel,
        out_shape=[mats(members + 1)] * 3,
        compiler_params=params(),
        name="owner_local",
    )(moments_in)
    d_base, total = pl.pallas_call(
        owner_sum_kernel,
        out_shape=[mats(members), shape((2 * BLK, BLK), f32)],
        compiler_params=params(),
        name="owner_sum",
    )(d_in, s_part, f_part)
    before = jnp.zeros_like(total)
    for turn in range(groups - 1):
        if turn > 0:
            crossed = jnp.dot(c_part[members], before[:BLK], precision=lax.Precision.HIGHEST)
            before = before + jnp.concatenate([jnp.zeros_like(crossed), crossed])
        before = lax.ppermute(before + total, "seq", onward)
    back = pl.pallas_call(
        owner_back_kernel,
        out_shape=shape((members, PACKED + BLK, BLK), f32),
        compiler_params=params(),
        name="owner_back",
    )(s_part, c_part, d_base, before)
    back_in = swap(back)

    part_shape = shape((8, tokens), f32)
    y, part = pl.pallas_call(
        second_stage_kernel,
        in_specs=[anywhere] * 3 + [in_vmem, in_vmem, in_smem],
        out_specs=[anywhere, in_vmem],
        out_shape=[turned_f32, part_shape],
        scratch_shapes=vmem(upright, upright, twofold, turned_f32, mats(heads), scores) + sems(3, 1),
        compiler_params=params(LATE),
        name="second_stage",
    )(query_rows, value_rows, r_local, back_in, out_gain.reshape(heads, 1, BLK), head_scale)
    shards = lax.axis_size("head")
    other = jnp.zeros_like(part)
    for turn in range(1, shards):
        other = other + lax.ppermute(part, "head", [(i, (i + turn) % shards) for i in range(shards)])
    return pl.pallas_call(
        functools.partial(norm_kernel, width * shards),
        in_specs=[anywhere, in_vmem, in_vmem],
        out_specs=anywhere,
        out_shape=shape((tokens, width), bf16),
        scratch_shapes=vmem(turned_f32, shape((tokens, width), bf16))
        + [pltpu.SemaphoreType.DMA((tokens // CHUNK,))] * 2,
        compiler_params=params(LAST),
        name="norm",
    )(y, part, other)


def solution(mesh):
    return jax.shard_map(
        per_device,
        mesh=mesh,
        in_specs=(P("seq", "head"), P("seq", "head"), P("seq", "head"), P("head"), P("head")),
        out_specs=P("seq", "head"),
        check_vma=False,
    )
```

```python
import functools

import jax
import jax.numpy as jnp
from jax import lax
from jax.experimental import pallas as pl
from jax.experimental.pallas import tpu as pltpu
from jax.sharding import PartitionSpec as P

BLK = 128
CHUNK = 256
PAIR = 2
HALF = BLK // 2
PACKED = HALF + 8
TWO = PACKED + BLK
THREE = TWO + BLK
SMALL = 8 * 1024 * 1024
LARGE = 60 * 1024 * 1024
LATE = 52 * 1024 * 1024
LAST = 52 * 1024 * 1024

epsilon = 1e-06
f32, bf16 = jnp.float32, jnp.bfloat16

NN = (((1,), (0,)), ((), ()))
NT = (((1,), (1,)), ((), ()))
TN = (((0,), (0,)), ((), ()))


def dot(a, b, dims=NN):
    return lax.dot_general(a, b, dims, preferred_element_type=f32)


def split(a):
    high = a.astype(bf16)
    return high, (a - high.astype(f32)).astype(bf16)


def lanes(*parts):
    return jnp.concatenate(parts, axis=1)


def rows(*parts):
    return jnp.concatenate(parts, axis=0)


def dot_f32(a, b):
    a_high, a_low = split(a)
    b_high, b_low = split(b)
    return dot(lanes(a_high, a_low), rows(b_high, b_high)) + dot(a_high, b_low)


def ordered(size):
    shape = (size, size)
    return lax.broadcasted_iota(jnp.int32, shape, 0) - lax.broadcasted_iota(jnp.int32, shape, 1)


def span(j, size=BLK):
    return slice(j * size, (j + 1) * size)


def half_indices():
    shape = (HALF, BLK)
    return lax.broadcasted_iota(jnp.int32, shape, 0), lax.broadcasted_iota(jnp.int32, shape, 1)


def pack(s):
    row, lane = half_indices()
    corner = pltpu.roll(s[HALF:], HALF, 1)
    diagonal = jnp.sum(jnp.where(lane == row, corner, 0.0), axis=0, keepdims=True)
    return rows(jnp.where(lane >= row, s[:HALF], corner), jnp.broadcast_to(diagonal, (8, BLK)))


def unpack(packed):
    row, lane = half_indices()
    top, diagonal = packed[:HALF], packed[HALF : HALF + 1]
    flipped = rows(top, jnp.zeros_like(top)).T
    corner = jnp.where(lane < row, top, jnp.where(lane == row, diagonal, flipped[:HALF]))
    return rows(
        jnp.where(lane >= row, top, flipped[:HALF]),
        jnp.where(lane < HALF, flipped[HALF:], pltpu.roll(corner, HALF, 1)),
    )


def columns(p):
    return pl.ds(pl.multiple_of(p * PAIR * BLK, PAIR * BLK), PAIR * BLK)


def copies(moves, sems, p):
    return [
        pltpu.make_async_copy(source(p), target(p), sems.at[n, p])
        for n, (source, target) in enumerate(moves)
    ]


def start(moves, sems, first, last):
    for p in range(first, last):
        for copy in copies(moves, sems, p):
            copy.start()


def wait(moves, sems, p):
    for copy in copies(moves, sems, p):
        copy.wait()


def by_columns(hbm):
    return lambda p: hbm.at[:, columns(p)]


def by_pair(ref):
    return lambda p: ref.at[p]


def running(parts, first=None):
    totals = [first]
    for part in parts:
        totals.append(part if totals[-1] is None else totals[-1] + part)
    return totals


def halves_sum(a):
    return a[:, :BLK] + a[:, BLK:]


def chunk_units(tokens):
    return [(i, j, span(i, CHUNK), span(j)) for i in range(tokens // CHUNK) for j in range(PAIR)]


def first_stage_kernel(
    q_hbm, k_hbm, v_hbm, r_hbm, m_hbm, q_ref, k_ref, v_ref, r_ref, m_ref, a_ref, read_sems, write_sems
):
    pairs, tokens, _ = q_ref.shape
    steps = tokens // CHUNK
    units = chunk_units(tokens)
    mask = ordered(CHUNK) <= 0
    reads = [(by_columns(a), by_pair(b)) for a, b in ((q_hbm, q_ref), (k_hbm, k_ref), (v_hbm, v_ref))]
    writes = [(by_pair(m_ref), by_pair(m_hbm)), (by_pair(r_ref), by_pair(r_hbm))]
    start(reads, read_sems, 0, pairs)

    @pl.loop(0, pairs)
    def _(p):
        wait(reads, read_sems, p)
        for i, j, at, cols in units:
            a = dot(k_ref[p, at, cols], q_ref[p, at, cols].T)
            a_ref[j, i] = rows(*split(jnp.where(mask, a, 0.0)))
        states = []
        for j in range(PAIR):
            blocks = [k_ref[p, span(i, CHUNK), span(j)] for i in range(steps)]
            states.append(running([dot(k.T, k) for k in blocks]))
            m_ref[p, j, :PACKED] = pack(states[j][steps])
        for i, j, at, cols in units:
            kt = k_ref[p, at, cols].T
            r = dot(lanes(kt, kt), a_ref[j, i])
            if i > 0:
                qt = q_ref[p, at, cols].T
                r = r + dot(lanes(*split(states[j][i])), rows(qt, qt))
            r_high, r_low = split(r)
            r_ref[p, j, at] = lanes(r_high.T, r_low.T)
        for j in range(PAIR):
            vt = v_ref[p, :, span(j)].T
            m_ref[p, j, PACKED:TWO] = dot(vt, q_ref[p, :, span(j)])
            m_ref[p, j, TWO:] = halves_sum(dot(vt, r_ref[p, j]))
        for copy in copies(writes, write_sems, p):
            copy.start()

    for p in range(pairs):
        wait(writes, write_sems, p)


def second_stage(p, q_ref, v_ref, r_ref, s_both, a_ref, first, store):
    tokens = q_ref.shape[1]
    steps = tokens // CHUNK
    units = chunk_units(tokens)
    mask = ordered(CHUNK) <= 0
    for j in range(PAIR):
        for i in range(steps):
            at = span(i, CHUNK)
            q = q_ref[p, at, span(j)]
            r = halves_sum(r_ref[p, j, at].astype(f32)) + dot(lanes(q, q), s_both[j])
            r_ref[p, j, at] = lanes(*split(r))
    for i, j, at, cols in units:
        qt = q_ref[p, at, cols].T
        a = dot(r_ref[p, j, at], rows(qt, qt))
        a_ref[j, i] = rows(*split(jnp.where(mask, a, 0.0)))
    sums = [[] for _ in range(PAIR)]
    for i, j, at, cols in units:
        if i + 1 < steps:
            sums[j].append(halves_sum(dot(v_ref[p, at, cols].T, r_ref[p, j, at])))
    states = [running(sums[j], first[j]) for j in range(PAIR)]
    for i, j, at, cols in units:
        vt = v_ref[p, at, cols].T
        qt = q_ref[p, at, cols].T
        num = dot(lanes(vt, vt), a_ref[j, i]) + dot(lanes(*split(states[j][i])), rows(qt, qt))
        store(i, j, num)


def second_stage_kernel(
    q_hbm, v_hbm, r_hbm, back_ref, gain_ref, scale_ref, y_hbm, part_ref,
    q_ref, v_ref, r_ref, y_ref, gains_ref, a_ref, read_sems, write_sems
):
    pairs = q_ref.shape[0]
    reads = [(by_columns(q_hbm), by_pair(q_ref)), (by_pair(r_hbm), by_pair(r_ref)), (by_columns(v_hbm), by_pair(v_ref))]
    writes = [(by_pair(y_ref), by_pair(y_hbm))]
    start(reads, read_sems, 0, pairs)
    part_ref[...] = jnp.zeros_like(part_ref)
    for h in range(pairs * PAIR):
        gains_ref[h] = jnp.broadcast_to(gain_ref[h], (BLK, BLK)).T

    @pl.loop(0, pairs)
    def _(p):
        def finish(i, j, num):
            h = p * PAIR + j
            y = num * scale_ref[h]
            part_ref[:, span(i, CHUNK)] += jnp.sum((y * y).reshape(BLK // 8, 8, CHUNK), axis=0)
            y_ref[p, span(j), span(i, CHUNK)] = y * lanes(*[gains_ref[h]] * (CHUNK // BLK))

        backs = [back_ref[p * PAIR + j] for j in range(PAIR)]
        s_both = [rows(*split(unpack(back[:PACKED]))) for back in backs]
        wait(reads, read_sems, p)
        second_stage(p, q_ref, v_ref, r_ref, s_both, a_ref, [back[PACKED:] for back in backs], finish)
        for copy in copies(writes, write_sems, p):
            copy.start()

    for p in range(pairs):
        wait(writes, write_sems, p)


def owner_kernel(moments_ref, s_ref, c_ref, base_ref, total_ref):
    members = moments_ref.shape[0]
    packed = jnp.zeros((PACKED, BLK), f32)
    c = jnp.zeros((BLK, BLK), f32)
    d = jnp.zeros((BLK, BLK), f32)
    for m in range(members):
        s_ref[m], c_ref[m], base_ref[m] = packed, c, d
        c_own = moments_ref[m, PACKED:TWO]
        d = d + moments_ref[m, TWO:]
        if m > 0:
            d = d + dot_f32(c_own, unpack(packed))
        packed = packed + moments_ref[m, :PACKED]
        c = c + c_own
    c_ref[members] = c
    total_ref[:PACKED] = packed
    total_ref[PACKED:] = d


def owner_onward_kernel(c_ref, total_ref, before_ref, out_ref):
    s_before = before_ref[:PACKED]
    out_ref[:PACKED] = total_ref[:PACKED] + s_before
    crossed = dot_f32(c_ref[c_ref.shape[0] - 1], unpack(s_before))
    out_ref[PACKED:] = total_ref[PACKED:] + before_ref[PACKED:] + crossed


def owner_back_kernel(s_ref, c_ref, base_ref, before_ref, back_ref):
    packed, d_before = before_ref[:PACKED], before_ref[PACKED:]
    s_before = unpack(packed)
    for m in range(back_ref.shape[0]):
        back_ref[m, :PACKED] = s_ref[m] + packed
        d = base_ref[m] + d_before
        back_ref[m, PACKED:] = d if m == 0 else d + dot_f32(c_ref[m], s_before)


def norm_kernel(features, y_hbm, mine_ref, other_ref, out_hbm, y_ref, out_ref, read_sems, write_sems):
    pairs, wide, tokens = y_ref.shape
    steps = tokens // CHUNK

    def y_copy(i):
        at = span(i, CHUNK)
        return pltpu.make_async_copy(y_hbm.at[:, :, at], y_ref.at[:, :, at], read_sems.at[i])

    def out_copy(i):
        at = span(i, CHUNK)
        return pltpu.make_async_copy(out_ref.at[at], out_hbm.at[at], write_sems.at[i])

    for i in range(steps):
        y_copy(i).start()
    total = jnp.sum(mine_ref[...] + other_ref[...], axis=0, keepdims=True)
    inv = lax.rsqrt(total * (1.0 / features) + epsilon)
    for i in range(steps):
        at = span(i, CHUNK)
        y_copy(i).wait()
        for p in range(pairs):
            out_ref[at, span(p, wide)] = (y_ref[p, :, at] * inv[:, at]).astype(bf16).T
        out_copy(i).start()
    for i in range(steps):
        out_copy(i).wait()


def params(limit=SMALL):
    return pltpu.CompilerParams(vmem_limit_bytes=limit)


def per_device(query_rows, key_rows, value_rows, head_scale, out_gain):
    tokens, width = query_rows.shape
    heads = head_scale.shape[0]
    seq = lax.axis_size("seq")
    members = heads
    groups = seq // members
    index_groups = [[g * members + m for m in range(members)] for g in range(groups)]
    onward = [(i, i + members) for i in range(seq - members)]

    def swap(a):
        return lax.all_to_all(a, "seq", 0, 0, axis_index_groups=index_groups)

    mats = lambda n: jax.ShapeDtypeStruct((n, BLK, BLK), f32)
    pairs = heads // PAIR
    shape = jax.ShapeDtypeStruct
    upright = shape((pairs, tokens, PAIR * BLK), bf16)
    turned_f32 = shape((pairs, PAIR * BLK, tokens), f32)
    twofold = shape((pairs, PAIR, tokens, 2 * BLK), bf16)
    scores = shape((PAIR, tokens // CHUNK, 2 * CHUNK, CHUNK), bf16)
    moment_mats = shape((pairs, PAIR, THREE, BLK), f32)
    anywhere = pl.BlockSpec(memory_space=pl.ANY)
    in_vmem = pl.BlockSpec(memory_space=pltpu.VMEM)
    in_smem = pl.BlockSpec(memory_space=pltpu.SMEM)

    def vmem(*arrays):
        return [pltpu.VMEM(a.shape, a.dtype) for a in arrays]

    def sems(*counts):
        return [pltpu.SemaphoreType.DMA((n, pairs)) for n in counts]

    r_local, moments = pl.pallas_call(
        first_stage_kernel,
        in_specs=[anywhere] * 3,
        out_specs=[anywhere] * 2,
        out_shape=[twofold, moment_mats],
        scratch_shapes=vmem(upright, upright, upright, twofold, moment_mats, scores) + sems(3, 2),
        compiler_params=params(LARGE),
        name="first_stage",
    )(query_rows, key_rows, value_rows)
    moments_in = swap(moments.reshape(heads, THREE, BLK))

    one = shape((TWO, BLK), f32)
    s_part, c_part, d_base, total = pl.pallas_call(
        owner_kernel,
        out_shape=[shape((members, PACKED, BLK), f32), mats(members + 1), mats(members), one],
        compiler_params=params(),
        name="owner",
    )(moments_in)
    before, passed = jnp.zeros_like(total), total
    for turn in range(groups - 1):
        if turn > 0:
            passed = pl.pallas_call(
                owner_onward_kernel, out_shape=one, compiler_params=params(), name="owner_onward"
            )(c_part, total, before)
        before = lax.ppermute(passed, "seq", onward)
    back = pl.pallas_call(
        owner_back_kernel,
        out_shape=shape((members, TWO, BLK), f32),
        compiler_params=params(),
        name="owner_back",
    )(s_part, c_part, d_base, before)
    back_in = swap(back)

    part_shape = shape((8, tokens), f32)
    y, part = pl.pallas_call(
        second_stage_kernel,
        in_specs=[anywhere] * 3 + [in_vmem, in_vmem, in_smem],
        out_specs=[anywhere, in_vmem],
        out_shape=[turned_f32, part_shape],
        scratch_shapes=vmem(upright, upright, twofold, turned_f32, mats(heads), scores) + sems(3, 1),
        compiler_params=params(LATE),
        name="second_stage",
    )(query_rows, value_rows, r_local, back_in, out_gain.reshape(heads, 1, BLK), head_scale)
    shards = lax.axis_size("head")
    other = jnp.zeros_like(part)
    for turn in range(1, shards):
        other = other + lax.ppermute(part, "head", [(i, (i + turn) % shards) for i in range(shards)])
    return pl.pallas_call(
        functools.partial(norm_kernel, width * shards),
        in_specs=[anywhere, in_vmem, in_vmem],
        out_specs=anywhere,
        out_shape=shape((tokens, width), bf16),
        scratch_shapes=vmem(turned_f32, shape((tokens, width), bf16))
        + [pltpu.SemaphoreType.DMA((tokens // CHUNK,))] * 2,
        compiler_params=params(LAST),
        name="norm",
    )(y, part, other)


def solution(mesh):
    return jax.shard_map(
        per_device,
        mesh=mesh,
        in_specs=(P("seq", "head"), P("seq", "head"), P("seq", "head"), P("head"), P("head")),
        out_specs=P("seq", "head"),
        check_vma=False,
    )
```

```python
import functools

import jax
import jax.numpy as jnp
from jax import lax
from jax.experimental import pallas as pl
from jax.experimental.pallas import tpu as pltpu
from jax.sharding import PartitionSpec as P

BLK = 128
CHUNK = 256
PAIR = 2
HALF = BLK // 2
PACKED = HALF + 8
TWO = PACKED + BLK
THREE = TWO + BLK
SMALL = 8 * 1024 * 1024
LARGE = 60 * 1024 * 1024
LATE = 24 * 1024 * 1024
LAST = 12 * 1024 * 1024

epsilon = 1e-06
f32, bf16 = jnp.float32, jnp.bfloat16

NN = (((1,), (0,)), ((), ()))
NT = (((1,), (1,)), ((), ()))
TN = (((0,), (0,)), ((), ()))


def dot(a, b, dims=NN):
    return lax.dot_general(a, b, dims, preferred_element_type=f32)


def split(a):
    high = a.astype(bf16)
    return high, (a - high.astype(f32)).astype(bf16)


def lanes(*parts):
    return jnp.concatenate(parts, axis=1)


def rows(*parts):
    return jnp.concatenate(parts, axis=0)


def dot_f32(a, b):
    a_high, a_low = split(a)
    b_high, b_low = split(b)
    return dot(lanes(a_high, a_low), rows(b_high, b_high)) + dot(a_high, b_low)


def ordered(size):
    shape = (size, size)
    return lax.broadcasted_iota(jnp.int32, shape, 0) - lax.broadcasted_iota(jnp.int32, shape, 1)


def span(j, size=BLK):
    return slice(j * size, (j + 1) * size)


def half_indices():
    shape = (HALF, BLK)
    return lax.broadcasted_iota(jnp.int32, shape, 0), lax.broadcasted_iota(jnp.int32, shape, 1)


def pack(s):
    row, lane = half_indices()
    corner = pltpu.roll(s[HALF:], HALF, 1)
    diagonal = jnp.sum(jnp.where(lane == row, corner, 0.0), axis=0, keepdims=True)
    return rows(jnp.where(lane >= row, s[:HALF], corner), jnp.broadcast_to(diagonal, (8, BLK)))


def unpack(packed):
    row, lane = half_indices()
    top, diagonal = packed[:HALF], packed[HALF : HALF + 1]
    flipped = rows(top, jnp.zeros_like(top)).T
    corner = jnp.where(lane < row, top, jnp.where(lane == row, diagonal, flipped[:HALF]))
    return rows(
        jnp.where(lane >= row, top, flipped[:HALF]),
        jnp.where(lane < HALF, flipped[HALF:], pltpu.roll(corner, HALF, 1)),
    )


def columns(p):
    return pl.ds(pl.multiple_of(p * PAIR * BLK, PAIR * BLK), PAIR * BLK)


def copies(moves, sems, p):
    return [
        pltpu.make_async_copy(source(p), target(p), sems.at[n, p])
        for n, (source, target) in enumerate(moves)
    ]


def start(moves, sems, first, last):
    for p in range(first, last):
        for copy in copies(moves, sems, p):
            copy.start()


def wait(moves, sems, p):
    for copy in copies(moves, sems, p):
        copy.wait()


def by_columns(hbm):
    return lambda p: hbm.at[:, columns(p)]


def by_pair(ref):
    return lambda p: ref.at[p]


def running(parts, first=None):
    totals = [first]
    for part in parts:
        totals.append(part if totals[-1] is None else totals[-1] + part)
    return totals


def halves_sum(a):
    return a[:, :BLK] + a[:, BLK:]


def chunk_units(tokens):
    return [(i, j, span(i, CHUNK), span(j)) for i in range(tokens // CHUNK) for j in range(PAIR)]


def first_stage_kernel(
    q_hbm, k_hbm, v_hbm, r_hbm, m_hbm, q_ref, k_ref, v_ref, r_ref, m_ref, a_ref, read_sems, write_sems
):
    pairs, tokens, _ = q_ref.shape
    steps = tokens // CHUNK
    units = chunk_units(tokens)
    mask = ordered(CHUNK) <= 0
    reads = [(by_columns(a), by_pair(b)) for a, b in ((q_hbm, q_ref), (k_hbm, k_ref), (v_hbm, v_ref))]
    writes = [(by_pair(m_ref), by_pair(m_hbm)), (by_pair(r_ref), by_pair(r_hbm))]
    start(reads, read_sems, 0, pairs)

    @pl.loop(0, pairs)
    def _(p):
        wait(reads, read_sems, p)
        for i, j, at, cols in units:
            a = dot(k_ref[p, at, cols], q_ref[p, at, cols].T)
            a_ref[j, i] = rows(*split(jnp.where(mask, a, 0.0)))
        states = []
        for j in range(PAIR):
            blocks = [k_ref[p, span(i, CHUNK), span(j)] for i in range(steps)]
            states.append(running([dot(k.T, k) for k in blocks]))
            m_ref[p, j, :PACKED] = pack(states[j][steps])
        for i, j, at, cols in units:
            kt = k_ref[p, at, cols].T
            r = dot(lanes(kt, kt), a_ref[j, i])
            if i > 0:
                qt = q_ref[p, at, cols].T
                r = r + dot(lanes(*split(states[j][i])), rows(qt, qt))
            r_high, r_low = split(r)
            r_ref[p, j, at] = lanes(r_high.T, r_low.T)
        for j in range(PAIR):
            vt = v_ref[p, :, span(j)].T
            m_ref[p, j, PACKED:TWO] = dot(vt, q_ref[p, :, span(j)])
            m_ref[p, j, TWO:] = halves_sum(dot(vt, r_ref[p, j]))
        for copy in copies(writes, write_sems, p):
            copy.start()

    for p in range(pairs):
        wait(writes, write_sems, p)


def second_stage_kernel(
    q_ref, v_ref, r_ref, back_ref, gain_ref, scale_ref, y_ref, part_ref, rr_ref, gains_ref, a_ref
):
    pairs, _, tokens, _ = r_ref.shape
    units = chunk_units(tokens)
    steps = tokens // CHUNK
    mask = ordered(CHUNK) <= 0
    part_ref[...] = jnp.zeros_like(part_ref)
    for h in range(pairs * PAIR):
        gains_ref[h] = jnp.broadcast_to(gain_ref[h], (BLK, BLK)).T

    @pl.loop(0, pairs)
    def _(p):
        backs = [back_ref[p * PAIR + j] for j in range(PAIR)]
        s_both = [rows(*split(unpack(back[:PACKED]))) for back in backs]
        heads = [pl.ds(pl.multiple_of((p * PAIR + j) * BLK, BLK), BLK) for j in range(PAIR)]
        for j in range(PAIR):
            for i in range(steps):
                at = span(i, CHUNK)
                q = q_ref[at, heads[j]]
                r = halves_sum(r_ref[p, j, at].astype(f32)) + dot(lanes(q, q), s_both[j])
                rr_ref[j, at] = lanes(*split(r))
        for i, j, at, cols in units:
            qt = q_ref[at, heads[j]].T
            a = dot(rr_ref[j, at], rows(qt, qt))
            a_ref[j, i] = rows(*split(jnp.where(mask, a, 0.0)))
        sums = [[] for _ in range(PAIR)]
        for i, j, at, cols in units:
            if i + 1 < steps:
                sums[j].append(halves_sum(dot(v_ref[at, heads[j]].T, rr_ref[j, at])))
        states = [running(sums[j], backs[j][PACKED:]) for j in range(PAIR)]
        for i, j, at, cols in units:
            h = p * PAIR + j
            vt, qt = v_ref[at, heads[j]].T, q_ref[at, heads[j]].T
            num = dot(lanes(vt, vt), a_ref[j, i]) + dot(lanes(*split(states[j][i])), rows(qt, qt))
            y = num * scale_ref[h]
            part_ref[:, at] += jnp.sum((y * y).reshape(BLK // 8, 8, CHUNK), axis=0)
            y_ref[p, cols, at] = y * lanes(*[gains_ref[h]] * (CHUNK // BLK))


def owner_kernel(moments_ref, s_ref, c_ref, base_ref, total_ref):
    members = moments_ref.shape[0]
    packed = jnp.zeros((PACKED, BLK), f32)
    c = jnp.zeros((BLK, BLK), f32)
    d = jnp.zeros((BLK, BLK), f32)
    for m in range(members):
        s_ref[m], c_ref[m], base_ref[m] = packed, c, d
        c_own = moments_ref[m, PACKED:TWO]
        d = d + moments_ref[m, TWO:]
        if m > 0:
            d = d + dot_f32(c_own, unpack(packed))
        packed = packed + moments_ref[m, :PACKED]
        c = c + c_own
    c_ref[members] = c
    total_ref[:PACKED] = packed
    total_ref[PACKED:] = d


def owner_onward_kernel(c_ref, total_ref, before_ref, out_ref):
    s_before = before_ref[:PACKED]
    out_ref[:PACKED] = total_ref[:PACKED] + s_before
    crossed = dot_f32(c_ref[c_ref.shape[0] - 1], unpack(s_before))
    out_ref[PACKED:] = total_ref[PACKED:] + before_ref[PACKED:] + crossed


def owner_back_kernel(s_ref, c_ref, base_ref, before_ref, back_ref):
    packed, d_before = before_ref[:PACKED], before_ref[PACKED:]
    s_before = unpack(packed)
    for m in range(back_ref.shape[0]):
        back_ref[m, :PACKED] = s_ref[m] + packed
        d = base_ref[m] + d_before
        back_ref[m, PACKED:] = d if m == 0 else d + dot_f32(c_ref[m], s_before)


def norm_kernel(features, y_ref, mine_ref, other_ref, out_hbm, out_ref, sems):
    pairs, wide, tokens = y_ref.shape
    total = jnp.sum(mine_ref[...] + other_ref[...], axis=0, keepdims=True)
    inv = lax.rsqrt(total * (1.0 / features) + epsilon)
    moves = []
    for i in range(tokens // CHUNK):
        at = span(i, CHUNK)
        for p in range(pairs):
            out_ref[at, span(p, wide)] = (y_ref[p, :, at] * inv[:, at]).astype(bf16).T
        moves.append(pltpu.make_async_copy(out_ref.at[at], out_hbm.at[at], sems.at[i]))
        moves[-1].start()
    for copy in moves:
        copy.wait()


def params(limit=SMALL):
    return pltpu.CompilerParams(vmem_limit_bytes=limit)


def per_device(query_rows, key_rows, value_rows, head_scale, out_gain):
    tokens, width = query_rows.shape
    heads = head_scale.shape[0]
    seq = lax.axis_size("seq")
    members = heads
    groups = seq // members
    index_groups = [[g * members + m for m in range(members)] for g in range(groups)]
    onward = [(i, i + members) for i in range(seq - members)]

    def swap(a):
        return lax.all_to_all(a, "seq", 0, 0, axis_index_groups=index_groups)

    mats = lambda n: jax.ShapeDtypeStruct((n, BLK, BLK), f32)
    pairs = heads // PAIR
    shape = jax.ShapeDtypeStruct
    upright = shape((pairs, tokens, PAIR * BLK), bf16)
    turned_f32 = shape((pairs, PAIR * BLK, tokens), f32)
    twofold = shape((pairs, PAIR, tokens, 2 * BLK), bf16)
    scores = shape((PAIR, tokens // CHUNK, 2 * CHUNK, CHUNK), bf16)
    moment_mats = shape((pairs, PAIR, THREE, BLK), f32)
    anywhere = pl.BlockSpec(memory_space=pl.ANY)
    in_vmem = pl.BlockSpec(memory_space=pltpu.VMEM)
    in_smem = pl.BlockSpec(memory_space=pltpu.SMEM)

    def vmem(*arrays):
        return [pltpu.VMEM(a.shape, a.dtype) for a in arrays]

    def sems(*counts):
        return [pltpu.SemaphoreType.DMA((n, pairs)) for n in counts]

    r_local, moments = pl.pallas_call(
        first_stage_kernel,
        in_specs=[anywhere] * 3,
        out_specs=[anywhere] * 2,
        out_shape=[twofold, moment_mats],
        scratch_shapes=vmem(upright, upright, upright, twofold, moment_mats, scores) + sems(3, 2),
        compiler_params=params(LARGE),
        name="first_stage",
    )(query_rows, key_rows, value_rows)
    moments_in = swap(moments.reshape(heads, THREE, BLK))

    one = shape((TWO, BLK), f32)
    s_part, c_part, d_base, total = pl.pallas_call(
        owner_kernel,
        out_shape=[shape((members, PACKED, BLK), f32), mats(members + 1), mats(members), one],
        compiler_params=params(),
        name="owner",
    )(moments_in)
    before, passed = jnp.zeros_like(total), total
    for turn in range(groups - 1):
        if turn > 0:
            passed = pl.pallas_call(
                owner_onward_kernel, out_shape=one, compiler_params=params(), name="owner_onward"
            )(c_part, total, before)
        before = lax.ppermute(passed, "seq", onward)
    back = pl.pallas_call(
        owner_back_kernel,
        out_shape=shape((members, TWO, BLK), f32),
        compiler_params=params(),
        name="owner_back",
    )(s_part, c_part, d_base, before)
    back_in = swap(back)

    part_shape = shape((8, tokens), f32)
    y, part = pl.pallas_call(
        second_stage_kernel,
        in_specs=[in_vmem] * 5 + [in_smem],
        out_shape=[turned_f32, part_shape],
        scratch_shapes=vmem(shape(twofold.shape[1:], bf16), mats(heads), scores),
        compiler_params=params(LATE),
        name="second_stage",
    )(query_rows, value_rows, r_local, back_in, out_gain.reshape(heads, 1, BLK), head_scale)
    shards = lax.axis_size("head")
    other = jnp.zeros_like(part)
    for turn in range(1, shards):
        other = other + lax.ppermute(part, "head", [(i, (i + turn) % shards) for i in range(shards)])
    return pl.pallas_call(
        functools.partial(norm_kernel, width * shards),
        in_specs=[in_vmem] * 3,
        out_specs=anywhere,
        out_shape=shape((tokens, width), bf16),
        scratch_shapes=vmem(shape((tokens, width), bf16)) + [pltpu.SemaphoreType.DMA((tokens // CHUNK,))],
        compiler_params=params(LAST),
        name="norm",
    )(y, part, other)


def solution(mesh):
    return jax.shard_map(
        per_device,
        mesh=mesh,
        in_specs=(P("seq", "head"), P("seq", "head"), P("seq", "head"), P("head"), P("head")),
        out_specs=P("seq", "head"),
        check_vma=False,
    )
```

```python
import functools

import jax
import jax.numpy as jnp
from jax import lax
from jax.experimental import pallas as pl
from jax.experimental.pallas import tpu as pltpu
from jax.sharding import PartitionSpec as P

BLK = 128
CHUNK = 256
PAIR = 2
HALF = BLK // 2
PACKED = HALF + 8
TWO = PACKED + BLK
THREE = TWO + BLK
SMALL = 8 * 1024 * 1024
LARGE = 60 * 1024 * 1024
LATE = 42 * 1024 * 1024
LAST = 12 * 1024 * 1024

epsilon = 1e-06
f32, bf16 = jnp.float32, jnp.bfloat16

NN = (((1,), (0,)), ((), ()))
NT = (((1,), (1,)), ((), ()))
TN = (((0,), (0,)), ((), ()))


def dot(a, b, dims=NN):
    return lax.dot_general(a, b, dims, preferred_element_type=f32)


def split(a):
    high = a.astype(bf16)
    return high, (a - high.astype(f32)).astype(bf16)


def lanes(*parts):
    return jnp.concatenate(parts, axis=1)


def rows(*parts):
    return jnp.concatenate(parts, axis=0)


def dot_f32(a, b):
    a_high, a_low = split(a)
    b_high, b_low = split(b)
    return dot(lanes(a_high, a_low), rows(b_high, b_high)) + dot(a_high, b_low)


def ordered(size):
    shape = (size, size)
    return lax.broadcasted_iota(jnp.int32, shape, 0) - lax.broadcasted_iota(jnp.int32, shape, 1)


def span(j, size=BLK):
    return slice(j * size, (j + 1) * size)


def half_indices():
    shape = (HALF, BLK)
    return lax.broadcasted_iota(jnp.int32, shape, 0), lax.broadcasted_iota(jnp.int32, shape, 1)


def pack(s):
    row, lane = half_indices()
    corner = pltpu.roll(s[HALF:], HALF, 1)
    diagonal = jnp.sum(jnp.where(lane == row, corner, 0.0), axis=0, keepdims=True)
    return rows(jnp.where(lane >= row, s[:HALF], corner), jnp.broadcast_to(diagonal, (8, BLK)))


def unpack(packed):
    row, lane = half_indices()
    top, diagonal = packed[:HALF], packed[HALF : HALF + 1]
    flipped = rows(top, jnp.zeros_like(top)).T
    corner = jnp.where(lane < row, top, jnp.where(lane == row, diagonal, flipped[:HALF]))
    return rows(
        jnp.where(lane >= row, top, flipped[:HALF]),
        jnp.where(lane < HALF, flipped[HALF:], pltpu.roll(corner, HALF, 1)),
    )


def columns(p):
    return pl.ds(pl.multiple_of(p * PAIR * BLK, PAIR * BLK), PAIR * BLK)


def copies(moves, sems, p):
    return [
        pltpu.make_async_copy(source(p), target(p), sems.at[n, p])
        for n, (source, target) in enumerate(moves)
    ]


def start(moves, sems, first, last):
    for p in range(first, last):
        for copy in copies(moves, sems, p):
            copy.start()


def wait(moves, sems, p):
    for copy in copies(moves, sems, p):
        copy.wait()


def by_columns(hbm):
    return lambda p: hbm.at[:, columns(p)]


def by_pair(ref):
    return lambda p: ref.at[p]


def running(parts, first=None):
    totals = [first]
    for part in parts:
        totals.append(part if totals[-1] is None else totals[-1] + part)
    return totals


def halves_sum(a):
    return a[:, :BLK] + a[:, BLK:]


def chunk_units(tokens):
    return [(i, j, span(i, CHUNK), span(j)) for i in range(tokens // CHUNK) for j in range(PAIR)]


def first_stage_kernel(
    q_hbm, k_hbm, v_hbm, r_hbm, m_hbm, q_ref, k_ref, v_ref, r_ref, m_ref, a_ref, read_sems, v_sems, r_sems, m_sems
):
    pairs, tokens, _ = q_ref.shape
    steps = tokens // CHUNK
    units = chunk_units(tokens)
    mask = ordered(CHUNK) <= 0
    reads = [(by_columns(a), by_pair(b)) for a, b in ((q_hbm, q_ref), (k_hbm, k_ref))]
    v_reads = [(by_columns(v_hbm), by_pair(v_ref))]
    r_writes, m_writes = [(by_pair(r_ref), by_pair(r_hbm))], [(by_pair(m_ref), by_pair(m_hbm))]
    for p in range(pairs):
        start(reads, read_sems, p, p + 1)
        start(v_reads, v_sems, p, p + 1)

    @pl.loop(0, pairs)
    def _(p):
        wait(reads, read_sems, p)
        for i, j, at, cols in units:
            a = dot(k_ref[p, at, cols], q_ref[p, at, cols].T)
            a_ref[j, i] = rows(*split(jnp.where(mask, a, 0.0)))
        states = []
        for j in range(PAIR):
            blocks = [k_ref[p, span(i, CHUNK), span(j)] for i in range(steps)]
            states.append(running([dot(k.T, k) for k in blocks]))
            m_ref[p, j, :PACKED] = pack(states[j][steps])
        for i, j, at, cols in units:
            kt = k_ref[p, at, cols].T
            r = dot(lanes(kt, kt), a_ref[j, i])
            if i > 0:
                qt = q_ref[p, at, cols].T
                r = r + dot(lanes(*split(states[j][i])), rows(qt, qt))
            r_high, r_low = split(r)
            r_ref[p, j, at] = lanes(r_high.T, r_low.T)
        for copy in copies(r_writes, r_sems, p):
            copy.start()
        wait(v_reads, v_sems, p)
        for j in range(PAIR):
            vt = v_ref[p, :, span(j)].T
            m_ref[p, j, PACKED:TWO] = dot(vt, q_ref[p, :, span(j)])
            m_ref[p, j, TWO:] = halves_sum(dot(vt, r_ref[p, j]))
        for copy in copies(m_writes, m_sems, p):
            copy.start()

    for p in range(pairs):
        wait(r_writes, r_sems, p)
        wait(m_writes, m_sems, p)


def second_stage_kernel(
    q_ref, v_ref, r_hbm, back_ref, gain_ref, scale_ref, y_ref, part_ref, r_ref, rr_ref, gains_ref, a_ref, read_sems
):
    pairs, _, tokens, _ = r_ref.shape
    units = chunk_units(tokens)
    steps = tokens // CHUNK
    mask = ordered(CHUNK) <= 0
    reads = [(by_pair(r_hbm), by_pair(r_ref))]
    start(reads, read_sems, 0, pairs)
    part_ref[...] = jnp.zeros_like(part_ref)
    for h in range(pairs * PAIR):
        gains_ref[h] = jnp.broadcast_to(gain_ref[h], (BLK, BLK)).T

    @pl.loop(0, pairs)
    def _(p):
        backs = [back_ref[p * PAIR + j] for j in range(PAIR)]
        s_both = [rows(*split(unpack(back[:PACKED]))) for back in backs]
        heads = [pl.ds(pl.multiple_of((p * PAIR + j) * BLK, BLK), BLK) for j in range(PAIR)]
        wait(reads, read_sems, p)
        for j in range(PAIR):
            for i in range(steps):
                at = span(i, CHUNK)
                q = q_ref[at, heads[j]]
                r = halves_sum(r_ref[p, j, at].astype(f32)) + dot(lanes(q, q), s_both[j])
                rr_ref[j, at] = lanes(*split(r))
        for i, j, at, cols in units:
            qt = q_ref[at, heads[j]].T
            a = dot(rr_ref[j, at], rows(qt, qt))
            a_ref[j, i] = rows(*split(jnp.where(mask, a, 0.0)))
        sums = [[] for _ in range(PAIR)]
        for i, j, at, cols in units:
            if i + 1 < steps:
                sums[j].append(halves_sum(dot(v_ref[at, heads[j]].T, rr_ref[j, at])))
        states = [running(sums[j], backs[j][PACKED:]) for j in range(PAIR)]
        for i, j, at, cols in units:
            h = p * PAIR + j
            vt, qt = v_ref[at, heads[j]].T, q_ref[at, heads[j]].T
            num = dot(lanes(vt, vt), a_ref[j, i]) + dot(lanes(*split(states[j][i])), rows(qt, qt))
            y = num * scale_ref[h]
            part_ref[:, at] += jnp.sum((y * y).reshape(BLK // 8, 8, CHUNK), axis=0)
            y_ref[p, cols, at] = y * lanes(*[gains_ref[h]] * (CHUNK // BLK))


def owner_kernel(moments_ref, s_ref, c_ref, base_ref, total_ref):
    members = moments_ref.shape[0]
    packed = jnp.zeros((PACKED, BLK), f32)
    c = jnp.zeros((BLK, BLK), f32)
    d = jnp.zeros((BLK, BLK), f32)
    for m in range(members):
        s_ref[m], c_ref[m], base_ref[m] = packed, c, d
        c_own = moments_ref[m, PACKED:TWO]
        d = d + moments_ref[m, TWO:]
        if m > 0:
            d = d + dot_f32(c_own, unpack(packed))
        packed = packed + moments_ref[m, :PACKED]
        c = c + c_own
    c_ref[members] = c
    total_ref[:PACKED] = packed
    total_ref[PACKED:] = d


def owner_onward_kernel(c_ref, total_ref, before_ref, out_ref):
    s_before = before_ref[:PACKED]
    out_ref[:PACKED] = total_ref[:PACKED] + s_before
    crossed = dot_f32(c_ref[c_ref.shape[0] - 1], unpack(s_before))
    out_ref[PACKED:] = total_ref[PACKED:] + before_ref[PACKED:] + crossed


def owner_back_kernel(s_ref, c_ref, base_ref, before_ref, back_ref):
    packed, d_before = before_ref[:PACKED], before_ref[PACKED:]
    s_before = unpack(packed)
    for m in range(back_ref.shape[0]):
        back_ref[m, :PACKED] = s_ref[m] + packed
        d = base_ref[m] + d_before
        back_ref[m, PACKED:] = d if m == 0 else d + dot_f32(c_ref[m], s_before)


def norm_kernel(features, y_ref, mine_ref, other_ref, out_hbm, out_ref, sems):
    pairs, wide, tokens = y_ref.shape
    total = jnp.sum(mine_ref[...] + other_ref[...], axis=0, keepdims=True)
    inv = lax.rsqrt(total * (1.0 / features) + epsilon)
    moves = []
    for i in range(tokens // CHUNK):
        at = span(i, CHUNK)
        for p in range(pairs):
            out_ref[at, span(p, wide)] = (y_ref[p, :, at] * inv[:, at]).astype(bf16).T
        moves.append(pltpu.make_async_copy(out_ref.at[at], out_hbm.at[at], sems.at[i]))
        moves[-1].start()
    for copy in moves:
        copy.wait()


def params(limit=SMALL):
    return pltpu.CompilerParams(vmem_limit_bytes=limit)


def per_device(query_rows, key_rows, value_rows, head_scale, out_gain):
    tokens, width = query_rows.shape
    heads = head_scale.shape[0]
    seq = lax.axis_size("seq")
    members = heads
    groups = seq // members
    index_groups = [[g * members + m for m in range(members)] for g in range(groups)]
    onward = [(i, i + members) for i in range(seq - members)]

    def swap(a):
        return lax.all_to_all(a, "seq", 0, 0, axis_index_groups=index_groups)

    mats = lambda n: jax.ShapeDtypeStruct((n, BLK, BLK), f32)
    pairs = heads // PAIR
    shape = jax.ShapeDtypeStruct
    upright = shape((pairs, tokens, PAIR * BLK), bf16)
    turned_f32 = shape((pairs, PAIR * BLK, tokens), f32)
    twofold = shape((pairs, PAIR, tokens, 2 * BLK), bf16)
    scores = shape((PAIR, tokens // CHUNK, 2 * CHUNK, CHUNK), bf16)
    moment_mats = shape((pairs, PAIR, THREE, BLK), f32)
    anywhere = pl.BlockSpec(memory_space=pl.ANY)
    in_vmem = pl.BlockSpec(memory_space=pltpu.VMEM)
    in_smem = pl.BlockSpec(memory_space=pltpu.SMEM)

    def vmem(*arrays):
        return [pltpu.VMEM(a.shape, a.dtype) for a in arrays]

    def sems(*counts):
        return [pltpu.SemaphoreType.DMA((n, pairs)) for n in counts]

    r_local, moments = pl.pallas_call(
        first_stage_kernel,
        in_specs=[anywhere] * 3,
        out_specs=[anywhere] * 2,
        out_shape=[twofold, moment_mats],
        scratch_shapes=vmem(upright, upright, upright, twofold, moment_mats, scores) + sems(2, 1, 1, 1),
        compiler_params=params(LARGE),
        name="first_stage",
    )(query_rows, key_rows, value_rows)
    moments_in = swap(moments.reshape(heads, THREE, BLK))

    one = shape((TWO, BLK), f32)
    s_part, c_part, d_base, total = pl.pallas_call(
        owner_kernel,
        out_shape=[shape((members, PACKED, BLK), f32), mats(members + 1), mats(members), one],
        compiler_params=params(),
        name="owner",
    )(moments_in)
    before, passed = jnp.zeros_like(total), total
    for turn in range(groups - 1):
        if turn > 0:
            passed = pl.pallas_call(
                owner_onward_kernel, out_shape=one, compiler_params=params(), name="owner_onward"
            )(c_part, total, before)
        before = lax.ppermute(passed, "seq", onward)
    back = pl.pallas_call(
        owner_back_kernel,
        out_shape=shape((members, TWO, BLK), f32),
        compiler_params=params(),
        name="owner_back",
    )(s_part, c_part, d_base, before)
    back_in = swap(back)

    part_shape = shape((8, tokens), f32)
    y, part = pl.pallas_call(
        second_stage_kernel,
        in_specs=[in_vmem, in_vmem, anywhere, in_vmem, in_vmem, in_smem],
        out_shape=[turned_f32, part_shape],
        scratch_shapes=vmem(twofold, shape(twofold.shape[1:], bf16), mats(heads), scores) + sems(1),
        compiler_params=params(LATE),
        name="second_stage",
    )(query_rows, value_rows, r_local, back_in, out_gain.reshape(heads, 1, BLK), head_scale)
    shards = lax.axis_size("head")
    other = jnp.zeros_like(part)
    for turn in range(1, shards):
        other = other + lax.ppermute(part, "head", [(i, (i + turn) % shards) for i in range(shards)])
    return pl.pallas_call(
        functools.partial(norm_kernel, width * shards),
        in_specs=[in_vmem] * 3,
        out_specs=anywhere,
        out_shape=shape((tokens, width), bf16),
        scratch_shapes=vmem(shape((tokens, width), bf16)) + [pltpu.SemaphoreType.DMA((tokens // CHUNK,))],
        compiler_params=params(LAST),
        name="norm",
    )(y, part, other)


def solution(mesh):
    return jax.shard_map(
        per_device,
        mesh=mesh,
        in_specs=(P("seq", "head"), P("seq", "head"), P("seq", "head"), P("head"), P("head")),
        out_specs=P("seq", "head"),
        check_vma=False,
    )
```

```python
import functools

import jax
import jax.numpy as jnp
from jax import lax
from jax.experimental import pallas as pl
from jax.experimental.pallas import tpu as pltpu
from jax.sharding import PartitionSpec as P

BLK = 128
CHUNK = 256
PAIR = 2
HALF = BLK // 2
PACKED = HALF + 8
TWO = PACKED + BLK
THREE = TWO + BLK
SMALL = 8 * 1024 * 1024
LARGE = 60 * 1024 * 1024
FETCH = 46 * 1024 * 1024
LATE = 24 * 1024 * 1024
LAST = 12 * 1024 * 1024

epsilon = 1e-06
f32, bf16 = jnp.float32, jnp.bfloat16

NN = (((1,), (0,)), ((), ()))
NT = (((1,), (1,)), ((), ()))
TN = (((0,), (0,)), ((), ()))


def dot(a, b, dims=NN):
    return lax.dot_general(a, b, dims, preferred_element_type=f32)


def split(a):
    high = a.astype(bf16)
    return high, (a - high.astype(f32)).astype(bf16)


def lanes(*parts):
    return jnp.concatenate(parts, axis=1)


def rows(*parts):
    return jnp.concatenate(parts, axis=0)


def dot_f32(a, b):
    a_high, a_low = split(a)
    b_high, b_low = split(b)
    return dot(lanes(a_high, a_low), rows(b_high, b_high)) + dot(a_high, b_low)


def ordered(size):
    shape = (size, size)
    return lax.broadcasted_iota(jnp.int32, shape, 0) - lax.broadcasted_iota(jnp.int32, shape, 1)


def span(j, size=BLK):
    return slice(j * size, (j + 1) * size)


def half_indices():
    shape = (HALF, BLK)
    return lax.broadcasted_iota(jnp.int32, shape, 0), lax.broadcasted_iota(jnp.int32, shape, 1)


def pack(s):
    row, lane = half_indices()
    corner = pltpu.roll(s[HALF:], HALF, 1)
    diagonal = jnp.sum(jnp.where(lane == row, corner, 0.0), axis=0, keepdims=True)
    return rows(jnp.where(lane >= row, s[:HALF], corner), jnp.broadcast_to(diagonal, (8, BLK)))


def unpack(packed):
    row, lane = half_indices()
    top, diagonal = packed[:HALF], packed[HALF : HALF + 1]
    flipped = rows(top, jnp.zeros_like(top)).T
    corner = jnp.where(lane < row, top, jnp.where(lane == row, diagonal, flipped[:HALF]))
    return rows(
        jnp.where(lane >= row, top, flipped[:HALF]),
        jnp.where(lane < HALF, flipped[HALF:], pltpu.roll(corner, HALF, 1)),
    )


def columns(p):
    return pl.ds(pl.multiple_of(p * PAIR * BLK, PAIR * BLK), PAIR * BLK)


def copies(moves, sems, p):
    return [
        pltpu.make_async_copy(source(p), target(p), sems.at[n, p])
        for n, (source, target) in enumerate(moves)
    ]


def start(moves, sems, first, last):
    for p in range(first, last):
        for copy in copies(moves, sems, p):
            copy.start()


def wait(moves, sems, p):
    for copy in copies(moves, sems, p):
        copy.wait()


def by_columns(hbm):
    return lambda p: hbm.at[:, columns(p)]


def by_pair(ref):
    return lambda p: ref.at[p]


def running(parts, first=None):
    totals = [first]
    for part in parts:
        totals.append(part if totals[-1] is None else totals[-1] + part)
    return totals


def halves_sum(a):
    return a[:, :BLK] + a[:, BLK:]


def chunk_units(tokens):
    return [(i, j, span(i, CHUNK), span(j)) for i in range(tokens // CHUNK) for j in range(PAIR)]


def first_stage_kernel(
    q_hbm, k_hbm, v_hbm, r_hbm, m_hbm, q_ref, k_ref, v_ref, r_ref, m_ref, a_ref, read_sems, write_sems
):
    pairs, tokens, _ = q_ref.shape
    steps = tokens // CHUNK
    units = chunk_units(tokens)
    mask = ordered(CHUNK) <= 0
    reads = [(by_columns(a), by_pair(b)) for a, b in ((q_hbm, q_ref), (k_hbm, k_ref), (v_hbm, v_ref))]
    writes = [(by_pair(m_ref), by_pair(m_hbm)), (by_pair(r_ref), by_pair(r_hbm))]
    start(reads, read_sems, 0, pairs)

    @pl.loop(0, pairs)
    def _(p):
        wait(reads, read_sems, p)
        for i, j, at, cols in units:
            a = dot(k_ref[p, at, cols], q_ref[p, at, cols].T)
            a_ref[j, i] = rows(*split(jnp.where(mask, a, 0.0)))
        states = []
        for j in range(PAIR):
            blocks = [k_ref[p, span(i, CHUNK), span(j)] for i in range(steps)]
            states.append(running([dot(k.T, k) for k in blocks]))
            m_ref[p, j, :PACKED] = pack(states[j][steps])
        for i, j, at, cols in units:
            kt = k_ref[p, at, cols].T
            r = dot(lanes(kt, kt), a_ref[j, i])
            if i > 0:
                qt = q_ref[p, at, cols].T
                r = r + dot(lanes(*split(states[j][i])), rows(qt, qt))
            r_high, r_low = split(r)
            r_ref[p, j, at] = lanes(r_high.T, r_low.T)
        for j in range(PAIR):
            vt = v_ref[p, :, span(j)].T
            m_ref[p, j, PACKED:TWO] = dot(vt, q_ref[p, :, span(j)])
            m_ref[p, j, TWO:] = halves_sum(dot(vt, r_ref[p, j]))
        for copy in copies(writes, write_sems, p):
            copy.start()

    for p in range(pairs):
        wait(writes, write_sems, p)


def fetch_kernel(r_hbm, gain_ref, owned_hbm, r_ref, gains_ref, sems):
    pairs = r_ref.shape[0]
    reads = [(by_pair(r_hbm), by_pair(r_ref))]
    start(reads, sems, 0, pairs)
    for h in range(gains_ref.shape[0]):
        gains_ref[h] = jnp.broadcast_to(gain_ref[h], (BLK, BLK)).T
    for p in range(pairs):
        wait(reads, sems, p)


def second_stage_kernel(
    q_ref, v_ref, r_ref, back_ref, gains_ref, scale_ref, y_ref, part_ref, rr_ref, a_ref
):
    pairs, _, tokens, _ = r_ref.shape
    units = chunk_units(tokens)
    steps = tokens // CHUNK
    mask = ordered(CHUNK) <= 0
    part_ref[...] = jnp.zeros_like(part_ref)

    @pl.loop(0, pairs)
    def _(p):
        backs = [back_ref[p * PAIR + j] for j in range(PAIR)]
        s_both = [rows(*split(unpack(back[:PACKED]))) for back in backs]
        heads = [pl.ds(pl.multiple_of((p * PAIR + j) * BLK, BLK), BLK) for j in range(PAIR)]
        for j in range(PAIR):
            for i in range(steps):
                at = span(i, CHUNK)
                q = q_ref[at, heads[j]]
                r = halves_sum(r_ref[p, j, at].astype(f32)) + dot(lanes(q, q), s_both[j])
                rr_ref[j, at] = lanes(*split(r))
        for i, j, at, cols in units:
            qt = q_ref[at, heads[j]].T
            a = dot(rr_ref[j, at], rows(qt, qt))
            a_ref[j, i] = rows(*split(jnp.where(mask, a, 0.0)))
        sums = [[] for _ in range(PAIR)]
        for i, j, at, cols in units:
            if i + 1 < steps:
                sums[j].append(halves_sum(dot(v_ref[at, heads[j]].T, rr_ref[j, at])))
        states = [running(sums[j], backs[j][PACKED:]) for j in range(PAIR)]
        for i, j, at, cols in units:
            h = p * PAIR + j
            vt, qt = v_ref[at, heads[j]].T, q_ref[at, heads[j]].T
            num = dot(lanes(vt, vt), a_ref[j, i]) + dot(lanes(*split(states[j][i])), rows(qt, qt))
            y = num * scale_ref[h]
            part_ref[:, at] += jnp.sum((y * y).reshape(BLK // 8, 8, CHUNK), axis=0)
            y_ref[p, cols, at] = y * lanes(*[gains_ref[h]] * (CHUNK // BLK))


def owner_kernel(moments_ref, s_ref, c_ref, base_ref, total_ref):
    members = moments_ref.shape[0]
    packed = jnp.zeros((PACKED, BLK), f32)
    c = jnp.zeros((BLK, BLK), f32)
    d = jnp.zeros((BLK, BLK), f32)
    for m in range(members):
        s_ref[m], c_ref[m], base_ref[m] = packed, c, d
        c_own = moments_ref[m, PACKED:TWO]
        d = d + moments_ref[m, TWO:]
        if m > 0:
            d = d + dot_f32(c_own, unpack(packed))
        packed = packed + moments_ref[m, :PACKED]
        c = c + c_own
    c_ref[members] = c
    total_ref[:PACKED] = packed
    total_ref[PACKED:] = d


def owner_onward_kernel(c_ref, total_ref, before_ref, out_ref):
    s_before = before_ref[:PACKED]
    out_ref[:PACKED] = total_ref[:PACKED] + s_before
    crossed = dot_f32(c_ref[c_ref.shape[0] - 1], unpack(s_before))
    out_ref[PACKED:] = total_ref[PACKED:] + before_ref[PACKED:] + crossed


def owner_back_kernel(s_ref, c_ref, base_ref, before_ref, held_hbm, back_ref):
    packed, d_before = before_ref[:PACKED], before_ref[PACKED:]
    s_before = unpack(packed)
    for m in range(back_ref.shape[0]):
        back_ref[m, :PACKED] = s_ref[m] + packed
        d = base_ref[m] + d_before
        back_ref[m, PACKED:] = d if m == 0 else d + dot_f32(c_ref[m], s_before)


def norm_kernel(features, y_ref, mine_ref, other_ref, out_hbm, out_ref, sems):
    pairs, wide, tokens = y_ref.shape
    total = jnp.sum(mine_ref[...] + other_ref[...], axis=0, keepdims=True)
    inv = lax.rsqrt(total * (1.0 / features) + epsilon)
    moves = []
    for i in range(tokens // CHUNK):
        at = span(i, CHUNK)
        for p in range(pairs):
            out_ref[at, span(p, wide)] = (y_ref[p, :, at] * inv[:, at]).astype(bf16).T
        moves.append(pltpu.make_async_copy(out_ref.at[at], out_hbm.at[at], sems.at[i]))
        moves[-1].start()
    for copy in moves:
        copy.wait()


def params(limit=SMALL):
    return pltpu.CompilerParams(vmem_limit_bytes=limit)


def per_device(query_rows, key_rows, value_rows, head_scale, out_gain):
    tokens, width = query_rows.shape
    heads = head_scale.shape[0]
    seq = lax.axis_size("seq")
    members = heads
    groups = seq // members
    index_groups = [[g * members + m for m in range(members)] for g in range(groups)]
    onward = [(i, i + members) for i in range(seq - members)]

    def swap(a):
        return lax.all_to_all(a, "seq", 0, 0, axis_index_groups=index_groups)

    mats = lambda n: jax.ShapeDtypeStruct((n, BLK, BLK), f32)
    pairs = heads // PAIR
    shape = jax.ShapeDtypeStruct
    upright = shape((pairs, tokens, PAIR * BLK), bf16)
    turned_f32 = shape((pairs, PAIR * BLK, tokens), f32)
    twofold = shape((pairs, PAIR, tokens, 2 * BLK), bf16)
    scores = shape((PAIR, tokens // CHUNK, 2 * CHUNK, CHUNK), bf16)
    moment_mats = shape((pairs, PAIR, THREE, BLK), f32)
    anywhere = pl.BlockSpec(memory_space=pl.ANY)
    in_vmem = pl.BlockSpec(memory_space=pltpu.VMEM)
    in_smem = pl.BlockSpec(memory_space=pltpu.SMEM)

    def vmem(*arrays):
        return [pltpu.VMEM(a.shape, a.dtype) for a in arrays]

    def sems(*counts):
        return [pltpu.SemaphoreType.DMA((n, pairs)) for n in counts]

    r_local, moments = pl.pallas_call(
        first_stage_kernel,
        in_specs=[anywhere] * 3,
        out_specs=[anywhere] * 2,
        out_shape=[twofold, moment_mats],
        scratch_shapes=vmem(upright, upright, upright, twofold, moment_mats, scores) + sems(3, 2),
        compiler_params=params(LARGE),
        name="first_stage",
    )(query_rows, key_rows, value_rows)
    moments_in = swap(moments.reshape(heads, THREE, BLK))

    one = shape((TWO, BLK), f32)
    s_part, c_part, d_base, total = pl.pallas_call(
        owner_kernel,
        out_shape=[shape((members, PACKED, BLK), f32), mats(members + 1), mats(members), one],
        compiler_params=params(),
        name="owner",
    )(moments_in)
    r_held, gain_columns = pl.pallas_call(
        fetch_kernel,
        in_specs=[anywhere, in_vmem, anywhere],
        out_specs=[in_vmem] * 2,
        out_shape=[twofold, mats(heads)],
        scratch_shapes=sems(1),
        compiler_params=params(FETCH),
        name="fetch",
    )(r_local, out_gain.reshape(heads, 1, BLK), total)
    before, passed = jnp.zeros_like(total), total
    for turn in range(groups - 1):
        if turn > 0:
            passed = pl.pallas_call(
                owner_onward_kernel, out_shape=one, compiler_params=params(), name="owner_onward"
            )(c_part, total, before)
        before = lax.ppermute(passed, "seq", onward)
    back = pl.pallas_call(
        owner_back_kernel,
        in_specs=[in_vmem] * 4 + [anywhere],
        out_shape=shape((members, TWO, BLK), f32),
        compiler_params=params(),
        name="owner_back",
    )(s_part, c_part, d_base, before, r_held)
    back_in = swap(back)

    part_shape = shape((8, tokens), f32)
    y, part = pl.pallas_call(
        second_stage_kernel,
        in_specs=[in_vmem] * 5 + [in_smem],
        out_shape=[turned_f32, part_shape],
        scratch_shapes=vmem(shape(twofold.shape[1:], bf16), scores),
        compiler_params=params(LATE),
        name="second_stage",
    )(query_rows, value_rows, r_held, back_in, gain_columns, head_scale)
    shards = lax.axis_size("head")
    other = jnp.zeros_like(part)
    for turn in range(1, shards):
        other = other + lax.ppermute(part, "head", [(i, (i + turn) % shards) for i in range(shards)])
    return pl.pallas_call(
        functools.partial(norm_kernel, width * shards),
        in_specs=[in_vmem] * 3,
        out_specs=anywhere,
        out_shape=shape((tokens, width), bf16),
        scratch_shapes=vmem(shape((tokens, width), bf16)) + [pltpu.SemaphoreType.DMA((tokens // CHUNK,))],
        compiler_params=params(LAST),
        name="norm",
    )(y, part, other)


def solution(mesh):
    return jax.shard_map(
        per_device,
        mesh=mesh,
        in_specs=(P("seq", "head"), P("seq", "head"), P("seq", "head"), P("head"), P("head")),
        out_specs=P("seq", "head"),
        check_vma=False,
    )
```

```python
import functools

import jax
import jax.numpy as jnp
from jax import lax
from jax.experimental import pallas as pl
from jax.experimental.pallas import tpu as pltpu
from jax.sharding import PartitionSpec as P

BLK = 128
CHUNK = 256
PAIR = 2
HALF = BLK // 2
PACKED = HALF + 8
TWO = PACKED + BLK
THREE = TWO + BLK
SMALL = 8 * 1024 * 1024
LARGE = 60 * 1024 * 1024
FETCH = 46 * 1024 * 1024
LATE = 24 * 1024 * 1024
LAST = 12 * 1024 * 1024

epsilon = 1e-06
f32, bf16 = jnp.float32, jnp.bfloat16

NN = (((1,), (0,)), ((), ()))
NT = (((1,), (1,)), ((), ()))
TN = (((0,), (0,)), ((), ()))


def dot(a, b, dims=NN):
    return lax.dot_general(a, b, dims, preferred_element_type=f32)


def split(a):
    high = a.astype(bf16)
    return high, (a - high.astype(f32)).astype(bf16)


def lanes(*parts):
    return jnp.concatenate(parts, axis=1)


def rows(*parts):
    return jnp.concatenate(parts, axis=0)


def dot_f32(a, b):
    a_high, a_low = split(a)
    b_high, b_low = split(b)
    return dot(lanes(a_high, a_low), rows(b_high, b_high)) + dot(a_high, b_low)


def ordered(size):
    shape = (size, size)
    return lax.broadcasted_iota(jnp.int32, shape, 0) - lax.broadcasted_iota(jnp.int32, shape, 1)


def span(j, size=BLK):
    return slice(j * size, (j + 1) * size)


def half_indices():
    shape = (HALF, BLK)
    return lax.broadcasted_iota(jnp.int32, shape, 0), lax.broadcasted_iota(jnp.int32, shape, 1)


def pack(s):
    row, lane = half_indices()
    corner = pltpu.roll(s[HALF:], HALF, 1)
    diagonal = jnp.sum(jnp.where(lane == row, corner, 0.0), axis=0, keepdims=True)
    return rows(jnp.where(lane >= row, s[:HALF], corner), jnp.broadcast_to(diagonal, (8, BLK)))


def unpack(packed):
    row, lane = half_indices()
    top, diagonal = packed[:HALF], packed[HALF : HALF + 1]
    flipped = rows(top, jnp.zeros_like(top)).T
    corner = jnp.where(lane < row, top, jnp.where(lane == row, diagonal, flipped[:HALF]))
    return rows(
        jnp.where(lane >= row, top, flipped[:HALF]),
        jnp.where(lane < HALF, flipped[HALF:], pltpu.roll(corner, HALF, 1)),
    )


def columns(p):
    return pl.ds(pl.multiple_of(p * PAIR * BLK, PAIR * BLK), PAIR * BLK)


def copies(moves, sems, p):
    return [
        pltpu.make_async_copy(source(p), target(p), sems.at[n, p])
        for n, (source, target) in enumerate(moves)
    ]


def start(moves, sems, first, last):
    for p in range(first, last):
        for copy in copies(moves, sems, p):
            copy.start()


def wait(moves, sems, p):
    for copy in copies(moves, sems, p):
        copy.wait()


def by_columns(hbm):
    return lambda p: hbm.at[:, columns(p)]


def by_pair(ref):
    return lambda p: ref.at[p]


def running(parts, first=None):
    totals = [first]
    for part in parts:
        totals.append(part if totals[-1] is None else totals[-1] + part)
    return totals


def halves_sum(a):
    return a[:, :BLK] + a[:, BLK:]


def chunk_units(tokens):
    return [(i, j, span(i, CHUNK), span(j)) for i in range(tokens // CHUNK) for j in range(PAIR)]


def first_stage_kernel(
    q_hbm, k_hbm, v_hbm, r_hbm, m_hbm, q_ref, k_ref, v_ref, r_ref, m_ref, a_ref, read_sems, write_sems
):
    pairs, tokens, _ = q_ref.shape
    steps = tokens // CHUNK
    units = chunk_units(tokens)
    mask = ordered(CHUNK) <= 0
    reads = [(by_columns(a), by_pair(b)) for a, b in ((q_hbm, q_ref), (k_hbm, k_ref), (v_hbm, v_ref))]
    writes = [(by_pair(m_ref), by_pair(m_hbm)), (by_pair(r_ref), by_pair(r_hbm))]
    start(reads, read_sems, 0, pairs)

    @pl.loop(0, pairs)
    def _(p):
        wait(reads, read_sems, p)
        for i, j, at, cols in units:
            a = dot(k_ref[p, at, cols], q_ref[p, at, cols].T)
            a_ref[j, i] = rows(*split(jnp.where(mask, a, 0.0)))
        states = []
        for j in range(PAIR):
            blocks = [k_ref[p, span(i, CHUNK), span(j)] for i in range(steps)]
            states.append(running([dot(k.T, k) for k in blocks]))
            m_ref[p, j, :PACKED] = pack(states[j][steps])
        for i, j, at, cols in units:
            kt = k_ref[p, at, cols].T
            r = dot(lanes(kt, kt), a_ref[j, i])
            if i > 0:
                qt = q_ref[p, at, cols].T
                r = r + dot(lanes(*split(states[j][i])), rows(qt, qt))
            r_high, r_low = split(r)
            r_ref[p, j, at] = lanes(r_high.T, r_low.T)
        for j in range(PAIR):
            vt = v_ref[p, :, span(j)].T
            m_ref[p, j, PACKED:TWO] = dot(vt, q_ref[p, :, span(j)])
            m_ref[p, j, TWO:] = halves_sum(dot(vt, r_ref[p, j]))
        for copy in copies(writes, write_sems, p):
            copy.start()

    for p in range(pairs):
        wait(writes, write_sems, p)


def fetch_kernel(r_hbm, gain_ref, owned_hbm, r_ref, gains_ref, sems):
    pairs = r_ref.shape[0]
    reads = [(by_pair(r_hbm), by_pair(r_ref))]
    start(reads, sems, 0, pairs)
    for h in range(gains_ref.shape[0]):
        gains_ref[h] = jnp.broadcast_to(gain_ref[h], (BLK, BLK)).T
    for p in range(pairs):
        wait(reads, sems, p)


def second_stage_kernel(
    q_ref, v_ref, r_ref, back_ref, gains_ref, scale_ref, y_ref, part_ref, rr_ref, a_ref
):
    pairs, _, tokens, _ = r_ref.shape
    units = chunk_units(tokens)
    steps = tokens // CHUNK
    mask = ordered(CHUNK) <= 0
    part_ref[...] = jnp.zeros_like(part_ref)

    for p in range(pairs):
        turn = p % 2
        backs = [back_ref[p * PAIR + j] for j in range(PAIR)]
        s_both = [rows(*split(unpack(back[:PACKED]))) for back in backs]
        heads = [span(p * PAIR + j) for j in range(PAIR)]
        for j in range(PAIR):
            for i in range(steps):
                at = span(i, CHUNK)
                q = q_ref[at, heads[j]]
                r = halves_sum(r_ref[p, j, at].astype(f32)) + dot(lanes(q, q), s_both[j])
                rr_ref[turn, j, at] = lanes(*split(r))
        for i, j, at, cols in units:
            qt = q_ref[at, heads[j]].T
            a = dot(rr_ref[turn, j, at], rows(qt, qt))
            a_ref[turn, j, i] = rows(*split(jnp.where(mask, a, 0.0)))
        sums = [[] for _ in range(PAIR)]
        for i, j, at, cols in units:
            if i + 1 < steps:
                sums[j].append(halves_sum(dot(v_ref[at, heads[j]].T, rr_ref[turn, j, at])))
        states = [running(sums[j], backs[j][PACKED:]) for j in range(PAIR)]
        for i, j, at, cols in units:
            h = p * PAIR + j
            vt, qt = v_ref[at, heads[j]].T, q_ref[at, heads[j]].T
            num = dot(lanes(vt, vt), a_ref[turn, j, i]) + dot(lanes(*split(states[j][i])), rows(qt, qt))
            y = num * scale_ref[h]
            part_ref[:, at] += jnp.sum((y * y).reshape(BLK // 8, 8, CHUNK), axis=0)
            y_ref[p, cols, at] = y * lanes(*[gains_ref[h]] * (CHUNK // BLK))


def owner_kernel(moments_ref, s_ref, c_ref, base_ref, total_ref):
    members = moments_ref.shape[0]
    packed = jnp.zeros((PACKED, BLK), f32)
    c = jnp.zeros((BLK, BLK), f32)
    d = jnp.zeros((BLK, BLK), f32)
    for m in range(members):
        s_ref[m], c_ref[m], base_ref[m] = packed, c, d
        c_own = moments_ref[m, PACKED:TWO]
        d = d + moments_ref[m, TWO:]
        if m > 0:
            d = d + dot_f32(c_own, unpack(packed))
        packed = packed + moments_ref[m, :PACKED]
        c = c + c_own
    c_ref[members] = c
    total_ref[:PACKED] = packed
    total_ref[PACKED:] = d


def owner_onward_kernel(c_ref, total_ref, before_ref, out_ref):
    s_before = before_ref[:PACKED]
    out_ref[:PACKED] = total_ref[:PACKED] + s_before
    crossed = dot_f32(c_ref[c_ref.shape[0] - 1], unpack(s_before))
    out_ref[PACKED:] = total_ref[PACKED:] + before_ref[PACKED:] + crossed


def owner_back_kernel(s_ref, c_ref, base_ref, before_ref, held_hbm, back_ref):
    packed, d_before = before_ref[:PACKED], before_ref[PACKED:]
    s_before = unpack(packed)
    for m in range(back_ref.shape[0]):
        back_ref[m, :PACKED] = s_ref[m] + packed
        d = base_ref[m] + d_before
        back_ref[m, PACKED:] = d if m == 0 else d + dot_f32(c_ref[m], s_before)


def norm_kernel(features, y_ref, mine_ref, other_ref, out_hbm, out_ref, sems):
    pairs, wide, tokens = y_ref.shape
    total = jnp.sum(mine_ref[...] + other_ref[...], axis=0, keepdims=True)
    inv = lax.rsqrt(total * (1.0 / features) + epsilon)
    moves = []
    for i in range(tokens // CHUNK):
        at = span(i, CHUNK)
        for p in range(pairs):
            out_ref[at, span(p, wide)] = (y_ref[p, :, at] * inv[:, at]).astype(bf16).T
        moves.append(pltpu.make_async_copy(out_ref.at[at], out_hbm.at[at], sems.at[i]))
        moves[-1].start()
    for copy in moves:
        copy.wait()


def params(limit=SMALL):
    return pltpu.CompilerParams(vmem_limit_bytes=limit)


def per_device(query_rows, key_rows, value_rows, head_scale, out_gain):
    tokens, width = query_rows.shape
    heads = head_scale.shape[0]
    seq = lax.axis_size("seq")
    members = heads
    groups = seq // members
    index_groups = [[g * members + m for m in range(members)] for g in range(groups)]
    onward = [(i, i + members) for i in range(seq - members)]

    def swap(a):
        return lax.all_to_all(a, "seq", 0, 0, axis_index_groups=index_groups)

    mats = lambda n: jax.ShapeDtypeStruct((n, BLK, BLK), f32)
    pairs = heads // PAIR
    shape = jax.ShapeDtypeStruct
    upright = shape((pairs, tokens, PAIR * BLK), bf16)
    turned_f32 = shape((pairs, PAIR * BLK, tokens), f32)
    twofold = shape((pairs, PAIR, tokens, 2 * BLK), bf16)
    scores = shape((PAIR, tokens // CHUNK, 2 * CHUNK, CHUNK), bf16)
    moment_mats = shape((pairs, PAIR, THREE, BLK), f32)
    anywhere = pl.BlockSpec(memory_space=pl.ANY)
    in_vmem = pl.BlockSpec(memory_space=pltpu.VMEM)
    in_smem = pl.BlockSpec(memory_space=pltpu.SMEM)

    def vmem(*arrays):
        return [pltpu.VMEM(a.shape, a.dtype) for a in arrays]

    def sems(*counts):
        return [pltpu.SemaphoreType.DMA((n, pairs)) for n in counts]

    r_local, moments = pl.pallas_call(
        first_stage_kernel,
        in_specs=[anywhere] * 3,
        out_specs=[anywhere] * 2,
        out_shape=[twofold, moment_mats],
        scratch_shapes=vmem(upright, upright, upright, twofold, moment_mats, scores) + sems(3, 2),
        compiler_params=params(LARGE),
        name="first_stage",
    )(query_rows, key_rows, value_rows)
    moments_in = swap(moments.reshape(heads, THREE, BLK))

    one = shape((TWO, BLK), f32)
    s_part, c_part, d_base, total = pl.pallas_call(
        owner_kernel,
        out_shape=[shape((members, PACKED, BLK), f32), mats(members + 1), mats(members), one],
        compiler_params=params(),
        name="owner",
    )(moments_in)
    r_held, gain_columns = pl.pallas_call(
        fetch_kernel,
        in_specs=[anywhere, in_vmem, anywhere],
        out_specs=[in_vmem] * 2,
        out_shape=[twofold, mats(heads)],
        scratch_shapes=sems(1),
        compiler_params=params(FETCH),
        name="fetch",
    )(r_local, out_gain.reshape(heads, 1, BLK), total)
    before, passed = jnp.zeros_like(total), total
    for turn in range(groups - 1):
        if turn > 0:
            passed = pl.pallas_call(
                owner_onward_kernel, out_shape=one, compiler_params=params(), name="owner_onward"
            )(c_part, total, before)
        before = lax.ppermute(passed, "seq", onward)
    back = pl.pallas_call(
        owner_back_kernel,
        in_specs=[in_vmem] * 4 + [anywhere],
        out_shape=shape((members, TWO, BLK), f32),
        compiler_params=params(),
        name="owner_back",
    )(s_part, c_part, d_base, before, r_held)
    back_in = swap(back)

    part_shape = shape((8, tokens), f32)
    y, part = pl.pallas_call(
        second_stage_kernel,
        in_specs=[in_vmem] * 5 + [in_smem],
        out_shape=[turned_f32, part_shape],
        scratch_shapes=vmem(shape((2,) + twofold.shape[1:], bf16), shape((2,) + scores.shape, bf16)),
        compiler_params=params(LATE),
        name="second_stage",
    )(query_rows, value_rows, r_held, back_in, gain_columns, head_scale)
    shards = lax.axis_size("head")
    other = jnp.zeros_like(part)
    for turn in range(1, shards):
        other = other + lax.ppermute(part, "head", [(i, (i + turn) % shards) for i in range(shards)])
    return pl.pallas_call(
        functools.partial(norm_kernel, width * shards),
        in_specs=[in_vmem] * 3,
        out_specs=anywhere,
        out_shape=shape((tokens, width), bf16),
        scratch_shapes=vmem(shape((tokens, width), bf16)) + [pltpu.SemaphoreType.DMA((tokens // CHUNK,))],
        compiler_params=params(LAST),
        name="norm",
    )(y, part, other)


def solution(mesh):
    return jax.shard_map(
        per_device,
        mesh=mesh,
        in_specs=(P("seq", "head"), P("seq", "head"), P("seq", "head"), P("head"), P("head")),
        out_specs=P("seq", "head"),
        check_vma=False,
    )
```

```python
import functools

import jax
import jax.numpy as jnp
from jax import lax
from jax.experimental import pallas as pl
from jax.experimental.pallas import tpu as pltpu
from jax.sharding import PartitionSpec as P

BLK = 128
CHUNK = 256
PAIR = 2
HALF = BLK // 2
PACKED = HALF + 8
TWO = PACKED + BLK
THREE = TWO + BLK
SMALL = 8 * 1024 * 1024
LARGE = 60 * 1024 * 1024
FETCH = 46 * 1024 * 1024
LATE = 24 * 1024 * 1024
LAST = 12 * 1024 * 1024

epsilon = 1e-06
f32, bf16 = jnp.float32, jnp.bfloat16

NN = (((1,), (0,)), ((), ()))
NT = (((1,), (1,)), ((), ()))
TN = (((0,), (0,)), ((), ()))


def dot(a, b, dims=NN):
    return lax.dot_general(a, b, dims, preferred_element_type=f32)


def split(a):
    high = a.astype(bf16)
    return high, (a - high.astype(f32)).astype(bf16)


def lanes(*parts):
    return jnp.concatenate(parts, axis=1)


def rows(*parts):
    return jnp.concatenate(parts, axis=0)


def dot_f32(a, b):
    a_high, a_low = split(a)
    b_high, b_low = split(b)
    return dot(lanes(a_high, a_low), rows(b_high, b_high)) + dot(a_high, b_low)


def ordered(size):
    shape = (size, size)
    return lax.broadcasted_iota(jnp.int32, shape, 0) - lax.broadcasted_iota(jnp.int32, shape, 1)


def span(j, size=BLK):
    return slice(j * size, (j + 1) * size)


def half_indices():
    shape = (HALF, BLK)
    return lax.broadcasted_iota(jnp.int32, shape, 0), lax.broadcasted_iota(jnp.int32, shape, 1)


def pack(s):
    row, lane = half_indices()
    corner = pltpu.roll(s[HALF:], HALF, 1)
    diagonal = jnp.sum(jnp.where(lane == row, corner, 0.0), axis=0, keepdims=True)
    return rows(jnp.where(lane >= row, s[:HALF], corner), jnp.broadcast_to(diagonal, (8, BLK)))


def unpack(packed):
    row, lane = half_indices()
    top, diagonal = packed[:HALF], packed[HALF : HALF + 1]
    flipped = rows(top, jnp.zeros_like(top)).T
    corner = jnp.where(lane < row, top, jnp.where(lane == row, diagonal, flipped[:HALF]))
    return rows(
        jnp.where(lane >= row, top, flipped[:HALF]),
        jnp.where(lane < HALF, flipped[HALF:], pltpu.roll(corner, HALF, 1)),
    )


def columns(p):
    return pl.ds(pl.multiple_of(p * PAIR * BLK, PAIR * BLK), PAIR * BLK)


def copies(moves, sems, p):
    return [
        pltpu.make_async_copy(source(p), target(p), sems.at[n, p])
        for n, (source, target) in enumerate(moves)
    ]


def start(moves, sems, first, last):
    for p in range(first, last):
        for copy in copies(moves, sems, p):
            copy.start()


def wait(moves, sems, p):
    for copy in copies(moves, sems, p):
        copy.wait()


def by_columns(hbm):
    return lambda p: hbm.at[:, columns(p)]


def by_pair(ref):
    return lambda p: ref.at[p]


def running(parts, first=None):
    totals = [first]
    for part in parts:
        totals.append(part if totals[-1] is None else totals[-1] + part)
    return totals


def halves_sum(a):
    return a[:, :BLK] + a[:, BLK:]


def chunk_units(tokens):
    return [(i, j, span(i, CHUNK), span(j)) for i in range(tokens // CHUNK) for j in range(PAIR)]


def first_stage_kernel(
    q_hbm, k_hbm, v_hbm, r_hbm, m_hbm, q_ref, k_ref, v_ref, r_ref, m_ref, a_ref, read_sems, write_sems
):
    pairs, tokens, _ = q_ref.shape
    steps = tokens // CHUNK
    units = chunk_units(tokens)
    mask = ordered(CHUNK) <= 0
    reads = [(by_columns(a), by_pair(b)) for a, b in ((q_hbm, q_ref), (k_hbm, k_ref), (v_hbm, v_ref))]
    writes = [(by_pair(m_ref), by_pair(m_hbm)), (by_pair(r_ref), by_pair(r_hbm))]
    start(reads, read_sems, 0, pairs)

    for p in range(pairs):
        turn = p % 2
        wait(reads, read_sems, p)
        for i, j, at, cols in units:
            a = dot(k_ref[p, at, cols], q_ref[p, at, cols].T)
            a_ref[turn, j, i] = rows(*split(jnp.where(mask, a, 0.0)))
        states = []
        for j in range(PAIR):
            blocks = [k_ref[p, span(i, CHUNK), span(j)] for i in range(steps)]
            states.append(running([dot(k.T, k) for k in blocks]))
            m_ref[p, j, :PACKED] = pack(states[j][steps])
        for i, j, at, cols in units:
            kt = k_ref[p, at, cols].T
            r = dot(lanes(kt, kt), a_ref[turn, j, i])
            if i > 0:
                qt = q_ref[p, at, cols].T
                r = r + dot(lanes(*split(states[j][i])), rows(qt, qt))
            r_high, r_low = split(r)
            r_ref[p, j, at] = lanes(r_high.T, r_low.T)
        for j in range(PAIR):
            vt = v_ref[p, :, span(j)].T
            m_ref[p, j, PACKED:TWO] = dot(vt, q_ref[p, :, span(j)])
            m_ref[p, j, TWO:] = halves_sum(dot(vt, r_ref[p, j]))
        for copy in copies(writes, write_sems, p):
            copy.start()

    for p in range(pairs):
        wait(writes, write_sems, p)


def fetch_kernel(r_hbm, gain_ref, owned_hbm, r_ref, gains_ref, sems):
    pairs = r_ref.shape[0]
    reads = [(by_pair(r_hbm), by_pair(r_ref))]
    start(reads, sems, 0, pairs)
    for h in range(gains_ref.shape[0]):
        gains_ref[h] = jnp.broadcast_to(gain_ref[h], (BLK, BLK)).T
    for p in range(pairs):
        wait(reads, sems, p)


def second_stage_kernel(
    q_ref, v_ref, r_ref, back_ref, gains_ref, scale_ref, y_ref, part_ref, rr_ref, a_ref
):
    pairs, _, tokens, _ = r_ref.shape
    units = chunk_units(tokens)
    steps = tokens // CHUNK
    mask = ordered(CHUNK) <= 0
    part_ref[...] = jnp.zeros_like(part_ref)

    for p in range(pairs):
        turn = p % 2
        backs = [back_ref[p * PAIR + j] for j in range(PAIR)]
        s_both = [rows(*split(unpack(back[:PACKED]))) for back in backs]
        heads = [span(p * PAIR + j) for j in range(PAIR)]
        for j in range(PAIR):
            for i in range(steps):
                at = span(i, CHUNK)
                q = q_ref[at, heads[j]]
                r = halves_sum(r_ref[p, j, at].astype(f32)) + dot(lanes(q, q), s_both[j])
                rr_ref[turn, j, at] = lanes(*split(r))
        for i, j, at, cols in units:
            qt = q_ref[at, heads[j]].T
            a = dot(rr_ref[turn, j, at], rows(qt, qt))
            a_ref[turn, j, i] = rows(*split(jnp.where(mask, a, 0.0)))
        sums = [[] for _ in range(PAIR)]
        for i, j, at, cols in units:
            if i + 1 < steps:
                sums[j].append(halves_sum(dot(v_ref[at, heads[j]].T, rr_ref[turn, j, at])))
        states = [running(sums[j], backs[j][PACKED:]) for j in range(PAIR)]
        for i, j, at, cols in units:
            h = p * PAIR + j
            vt, qt = v_ref[at, heads[j]].T, q_ref[at, heads[j]].T
            num = dot(lanes(vt, vt), a_ref[turn, j, i]) + dot(lanes(*split(states[j][i])), rows(qt, qt))
            y = num * scale_ref[h]
            part_ref[:, at] += jnp.sum((y * y).reshape(BLK // 8, 8, CHUNK), axis=0)
            y_ref[p, cols, at] = y * lanes(*[gains_ref[h]] * (CHUNK // BLK))


def owner_kernel(moments_ref, s_ref, c_ref, base_ref, total_ref):
    members = moments_ref.shape[0]
    packed = jnp.zeros((PACKED, BLK), f32)
    c = jnp.zeros((BLK, BLK), f32)
    d = jnp.zeros((BLK, BLK), f32)
    for m in range(members):
        s_ref[m], c_ref[m], base_ref[m] = packed, c, d
        c_own = moments_ref[m, PACKED:TWO]
        d = d + moments_ref[m, TWO:]
        if m > 0:
            d = d + dot_f32(c_own, unpack(packed))
        packed = packed + moments_ref[m, :PACKED]
        c = c + c_own
    c_ref[members] = c
    total_ref[:PACKED] = packed
    total_ref[PACKED:] = d


def owner_onward_kernel(c_ref, total_ref, before_ref, out_ref):
    s_before = before_ref[:PACKED]
    out_ref[:PACKED] = total_ref[:PACKED] + s_before
    crossed = dot_f32(c_ref[c_ref.shape[0] - 1], unpack(s_before))
    out_ref[PACKED:] = total_ref[PACKED:] + before_ref[PACKED:] + crossed


def owner_back_kernel(s_ref, c_ref, base_ref, before_ref, held_hbm, back_ref):
    packed, d_before = before_ref[:PACKED], before_ref[PACKED:]
    s_before = unpack(packed)
    for m in range(back_ref.shape[0]):
        back_ref[m, :PACKED] = s_ref[m] + packed
        d = base_ref[m] + d_before
        back_ref[m, PACKED:] = d if m == 0 else d + dot_f32(c_ref[m], s_before)


def norm_kernel(features, y_ref, mine_ref, other_ref, out_hbm, out_ref, sems):
    pairs, wide, tokens = y_ref.shape
    total = jnp.sum(mine_ref[...] + other_ref[...], axis=0, keepdims=True)
    inv = lax.rsqrt(total * (1.0 / features) + epsilon)
    moves = []
    for i in range(tokens // CHUNK):
        at = span(i, CHUNK)
        for p in range(pairs):
            out_ref[at, span(p, wide)] = (y_ref[p, :, at] * inv[:, at]).astype(bf16).T
        moves.append(pltpu.make_async_copy(out_ref.at[at], out_hbm.at[at], sems.at[i]))
        moves[-1].start()
    for copy in moves:
        copy.wait()


def params(limit=SMALL):
    return pltpu.CompilerParams(vmem_limit_bytes=limit)


def per_device(query_rows, key_rows, value_rows, head_scale, out_gain):
    tokens, width = query_rows.shape
    heads = head_scale.shape[0]
    seq = lax.axis_size("seq")
    members = heads
    groups = seq // members
    index_groups = [[g * members + m for m in range(members)] for g in range(groups)]
    onward = [(i, i + members) for i in range(seq - members)]

    def swap(a):
        return lax.all_to_all(a, "seq", 0, 0, axis_index_groups=index_groups)

    mats = lambda n: jax.ShapeDtypeStruct((n, BLK, BLK), f32)
    pairs = heads // PAIR
    shape = jax.ShapeDtypeStruct
    upright = shape((pairs, tokens, PAIR * BLK), bf16)
    turned_f32 = shape((pairs, PAIR * BLK, tokens), f32)
    twofold = shape((pairs, PAIR, tokens, 2 * BLK), bf16)
    scores = shape((PAIR, tokens // CHUNK, 2 * CHUNK, CHUNK), bf16)
    moment_mats = shape((pairs, PAIR, THREE, BLK), f32)
    anywhere = pl.BlockSpec(memory_space=pl.ANY)
    in_vmem = pl.BlockSpec(memory_space=pltpu.VMEM)
    in_smem = pl.BlockSpec(memory_space=pltpu.SMEM)

    def vmem(*arrays):
        return [pltpu.VMEM(a.shape, a.dtype) for a in arrays]

    def sems(*counts):
        return [pltpu.SemaphoreType.DMA((n, pairs)) for n in counts]

    r_local, moments = pl.pallas_call(
        first_stage_kernel,
        in_specs=[anywhere] * 3,
        out_specs=[anywhere] * 2,
        out_shape=[twofold, moment_mats],
        scratch_shapes=vmem(upright, upright, upright, twofold, moment_mats, shape((2,) + scores.shape, bf16)) + sems(3, 2),
        compiler_params=params(LARGE),
        name="first_stage",
    )(query_rows, key_rows, value_rows)
    moments_in = swap(moments.reshape(heads, THREE, BLK))

    one = shape((TWO, BLK), f32)
    s_part, c_part, d_base, total = pl.pallas_call(
        owner_kernel,
        out_shape=[shape((members, PACKED, BLK), f32), mats(members + 1), mats(members), one],
        compiler_params=params(),
        name="owner",
    )(moments_in)
    r_held, gain_columns = pl.pallas_call(
        fetch_kernel,
        in_specs=[anywhere, in_vmem, anywhere],
        out_specs=[in_vmem] * 2,
        out_shape=[twofold, mats(heads)],
        scratch_shapes=sems(1),
        compiler_params=params(FETCH),
        name="fetch",
    )(r_local, out_gain.reshape(heads, 1, BLK), total)
    before, passed = jnp.zeros_like(total), total
    for turn in range(groups - 1):
        if turn > 0:
            passed = pl.pallas_call(
                owner_onward_kernel, out_shape=one, compiler_params=params(), name="owner_onward"
            )(c_part, total, before)
        before = lax.ppermute(passed, "seq", onward)
    back = pl.pallas_call(
        owner_back_kernel,
        in_specs=[in_vmem] * 4 + [anywhere],
        out_shape=shape((members, TWO, BLK), f32),
        compiler_params=params(),
        name="owner_back",
    )(s_part, c_part, d_base, before, r_held)
    back_in = swap(back)

    part_shape = shape((8, tokens), f32)
    y, part = pl.pallas_call(
        second_stage_kernel,
        in_specs=[in_vmem] * 5 + [in_smem],
        out_shape=[turned_f32, part_shape],
        scratch_shapes=vmem(shape((2,) + twofold.shape[1:], bf16), shape((2,) + scores.shape, bf16)),
        compiler_params=params(LATE),
        name="second_stage",
    )(query_rows, value_rows, r_held, back_in, gain_columns, head_scale)
    shards = lax.axis_size("head")
    other = jnp.zeros_like(part)
    for turn in range(1, shards):
        other = other + lax.ppermute(part, "head", [(i, (i + turn) % shards) for i in range(shards)])
    return pl.pallas_call(
        functools.partial(norm_kernel, width * shards),
        in_specs=[in_vmem] * 3,
        out_specs=anywhere,
        out_shape=shape((tokens, width), bf16),
        scratch_shapes=vmem(shape((tokens, width), bf16)) + [pltpu.SemaphoreType.DMA((tokens // CHUNK,))],
        compiler_params=params(LAST),
        name="norm",
    )(y, part, other)


def solution(mesh):
    return jax.shard_map(
        per_device,
        mesh=mesh,
        in_specs=(P("seq", "head"), P("seq", "head"), P("seq", "head"), P("head"), P("head")),
        out_specs=P("seq", "head"),
        check_vma=False,
    )
```
